32 devices in a mesh: section: 2 (over core), dp: 4 (over z), seq: 4 (over y, x).
Axes of the slice: x: 2, y: 2, z: 4, core: 2. Of those that a mesh axis runs over, the one named last changes fastest.
Arguments:
- tokens: bfloat16 [8, 512, 768], P('dp', 'seq'), may hold values from -6 to 6
- segment_ids: int32 [8, 512], P('dp'), may hold values from 0 to 3, as said below
- cotangent: bfloat16 [8, 512, 768], P('dp', 'seq'), may hold values from -6 to 6
- norm_one_gain: bfloat16 [768], replicated, may hold values from 0.5 to 1.5
- norm_one_bias: bfloat16 [768], replicated, may hold values from -1.25 to 1.25
- qkv_weight: bfloat16 [768, 2304], replicated, may hold values from -0.21875 to 0.21875
- query_bias: bfloat16 [768], replicated, may hold values from -1.75 to 1.75
- value_bias: bfloat16 [768], replicated, may hold values from -0.625 to 0.625
- out_weight: bfloat16 [768, 768], replicated, may hold values from -0.875 to 0.875
- out_bias: bfloat16 [768], replicated, may hold values from -1.25 to 1.25
- norm_two_gain: bfloat16 [768], replicated, may hold values from 0.5 to 1.5
- norm_two_bias: bfloat16 [768], replicated, may hold values from -1.25 to 1.25
- up_weight: bfloat16 [768, 3072], replicated, may hold values from -0.21875 to 0.21875
- up_bias: bfloat16 [3072], replicated, may hold values from -1.75 to 1.75
- down_weight: bfloat16 [3072, 768], replicated, may hold values from -0.109375 to 0.109375
- down_bias: bfloat16 [768], replicated, may hold values from -1.25 to 1.25
- pass_embed: bfloat16 [2, 768], replicated, may hold values from -3 to 3
Outputs:
- layer_out: bfloat16 [2, 8, 512, 768], P('section', 'dp', 'seq')
- grad_flow: float32 [2, 8, 512, 768], P('section', 'dp', 'seq')
- grad_norm_one_gain: float32 [768], replicated
- grad_norm_one_bias: float32 [768], replicated
- grad_qkv_weight: float32 [768, 2304], replicated
- grad_query_bias: float32 [768], replicated
- grad_value_bias: float32 [768], replicated
- grad_out_weight: float32 [768, 768], replicated
- grad_out_bias: float32 [768], replicated
- grad_norm_two_gain: float32 [768], replicated
- grad_norm_two_bias: float32 [768], replicated
- grad_up_weight: float32 [768, 3072], replicated
- grad_up_bias: float32 [3072], replicated
- grad_down_weight: float32 [3072, 768], replicated
- grad_down_bias: float32 [768], replicated
- grad_pass_embed: float32 [2, 768], P('section')
The draws below stay inside these ranges and needn't reach their ends.
Inputs may be any that keep to these rules, and one draw needn't show every extreme that they name: `segment_ids`: within each pack the ids never fall from one position to the next, and one id marks one document. In each group of 2 consecutive packs, one pack chosen by the seed is a single document.
All inputs are finite; a program needn't handle non-finite values.
Results may differ from the reference program's by a relative error of at most 0.02.
Values may be sent and summed in bfloat16 or wider, within the bound.
No kernel may reach another device: no remote copies, remote signals or barrier semaphores. Data moves between devices by JAX's collectives and lax.ppermute only.
A program may use at most 256 MiB of HBM per device.

```python
import jax
import jax.numpy as jnp
from jax import lax

D = 768
HD = 64
FF = 3072
MICRO = 2
PACK = 512
BATCH = 8


def draw_segment_ids(key, part):
    key = jax.random.fold_in(key, 7)
    cut_key, pick_key = jax.random.split(key)
    row_keys = jax.random.split(cut_key, BATCH)
    cut_points = jax.vmap(lambda row_key: jax.random.permutation(row_key, PACK - 1)[:3] + 1)(row_keys)
    positions = jnp.arange(PACK, dtype=jnp.int32)
    segment_of = jnp.sum((positions[None, :, None] >= cut_points[:, None, :]).astype(jnp.int32), axis=-1)
    groups = BATCH // MICRO
    chosen = jax.random.randint(pick_key, (groups,), 0, MICRO)
    row_index = jnp.arange(BATCH, dtype=jnp.int32)
    single_doc = row_index % MICRO == chosen[row_index // MICRO]
    return jnp.where(single_doc[:, None], 0, segment_of).astype(jnp.int32)


def steps_of(stream_key, extent, cuts, least, top_value):
    def one(axis_at, shards_of):
        steps = jax.random.uniform(jax.random.fold_in(jax.random.fold_in(stream_key, 6), axis_at), (shards_of,), jnp.float32, least / len(cuts), top_value / len(cuts))
        return jnp.repeat(jnp.exp(steps), extent[axis_at] // shards_of).reshape((-1,) + (1,) * (len(extent) - axis_at - 1))

    level = one(*cuts[0])
    for cut in cuts[1:]:
        level = level * one(*cut)
    return level


def centred(own_key, shape, scale, bound, cuts=(), kind=jnp.bfloat16):
    level = steps_of(own_key, shape, cuts, -0.22, 0.18) if cuts else 1.0
    entries = jax.random.normal(own_key, shape, jnp.float32) * scale * level
    return jnp.minimum(jnp.maximum(entries, -bound), bound).astype(kind)


def setup_inputs(seed: int = 0) -> dict:
    arg_keys = jax.random.split(jax.random.key(seed), 18)
    return {
        "tokens": centred(arg_keys[0], (BATCH, PACK, D), 1.0, 6.0, ((0, 4), (1, 4))),
        "segment_ids": draw_segment_ids(jax.random.fold_in(arg_keys[17], 71), 0),
        "cotangent": centred(arg_keys[2], (BATCH, PACK, D), 1.0, 6.0, ((0, 4), (1, 4))),
        "norm_one_gain": jnp.clip(1.0 + 0.1 * jax.random.normal(arg_keys[3], (D,), jnp.float32), 0.5, 1.5).astype(jnp.bfloat16),
        "norm_one_bias": centred(arg_keys[4], (D,), 0.2, 1.25),
        "qkv_weight": centred(arg_keys[5], (D, 3 * D), D ** -0.5, 0.21875),
        "query_bias": centred(arg_keys[6], (D,), 0.3, 1.75),
        "value_bias": centred(arg_keys[7], (D,), 0.1, 0.625),
        "out_weight": centred(arg_keys[8], (D, D), (D // 16) ** -0.5, 0.875),
        "out_bias": centred(arg_keys[9], (D,), 0.2, 1.25),
        "norm_two_gain": jnp.clip(1.0 + 0.1 * jax.random.normal(arg_keys[10], (D,), jnp.float32), 0.5, 1.5).astype(jnp.bfloat16),
        "norm_two_bias": centred(arg_keys[11], (D,), 0.2, 1.25),
        "up_weight": centred(arg_keys[12], (D, FF), D ** -0.5, 0.21875),
        "up_bias": centred(arg_keys[13], (FF,), 0.3, 1.75),
        "down_weight": centred(arg_keys[14], (FF, D), FF ** -0.5, 0.109375),
        "down_bias": centred(arg_keys[15], (D,), 0.2, 1.25),
        "pass_embed": centred(arg_keys[16], (2, D), 0.5, 3.0),
    }


@jax.custom_vjp
def low(v):
    return lax.optimization_barrier(v.astype(jnp.bfloat16)).astype(jnp.float32)

@jax.custom_vjp
def low_back(v):
    return v

def low_keep(v):
    return (low(v), None)

def low_pass(kept, grad):
    return (grad,)

def back_keep(v):
    return (v, None)

def back_low(kept, grad):
    return (low(grad),)
low.defvjp(low_keep, low_pass)
low_back.defvjp(back_keep, back_low)
epsilon = 1e-05
score_scale = 0.125
floor_value = -1e+30
highest = lax.Precision.HIGHEST

def both_low(values_in):
    return low(low_back(values_in))

def layer_norm(values_in, gain_row, offset):
    center = lax.optimization_barrier(jnp.mean(values_in, axis=-1, keepdims=True))
    shifted = values_in - center
    spread = lax.optimization_barrier(jnp.mean(shifted * shifted, axis=-1, keepdims=True))
    return shifted * lax.rsqrt(spread + epsilon) * gain_row + offset

def attend(queries, key_rows, value_rows, query_seg, query_pos, key_seg, key_pos):
    row_count, head_count, head_size = queries.shape
    block_rows = min(512, row_count)
    block_count = row_count // block_rows

    def one_block(pieces_in):
        query_block, seg_block, pos_block = pieces_in
        scores = jnp.einsum('qhd,khd->hqk', query_block, key_rows, precision=highest) * score_scale
        scores = low_back(scores)
        allowed = (key_seg[None, :] == seg_block[:, None]) & (key_pos[None, :] <= pos_block[:, None])
        scores = jnp.where(allowed[None], scores, floor_value)
        probabilities = low(jax.nn.softmax(scores, axis=-1))
        return jnp.einsum('hqk,khd->qhd', probabilities, value_rows, precision=highest)
    pieces_in = (queries.reshape(block_count, block_rows, head_count, head_size), query_seg.reshape(block_count, block_rows), query_pos.reshape(block_count, block_rows))
    result = lax.map(jax.checkpoint(one_block), pieces_in)
    return result.reshape(row_count, head_count, head_size)

def one_pass(inputs, embed_row, weights, segments, extra_rows):
    norm_one_gain, norm_one_bias, qkv_weight, query_bias, value_bias, out_weight, out_bias, norm_two_gain, norm_two_bias, up_weight, up_bias, down_weight, down_bias = weights
    row_count, feature_count = inputs.shape
    head_count = feature_count // HD
    combined = inputs + embed_row
    normed = low(layer_norm(combined, norm_one_gain, norm_one_bias))
    projected = jnp.dot(normed, qkv_weight, precision=highest)
    queries = both_low(projected[:, :feature_count] + query_bias)
    key_rows = both_low(projected[:, feature_count:2 * feature_count])
    value_rows = both_low(projected[:, 2 * feature_count:] + value_bias)
    positions = jnp.arange(row_count, dtype=jnp.int32)
    if extra_rows is None:
        all_keys, all_values, key_seg, key_pos = (key_rows, value_rows, segments, positions)
    else:
        all_keys = jnp.concatenate([key_rows, extra_rows[0]], axis=0)
        all_values = jnp.concatenate([value_rows, extra_rows[1]], axis=0)
        key_seg = jnp.concatenate([segments, segments], axis=0)
        key_pos = jnp.concatenate([positions, positions], axis=0)
    attended = attend(queries.reshape(row_count, head_count, HD), all_keys.reshape(-1, head_count, HD), all_values.reshape(-1, head_count, HD), segments, positions, key_seg, key_pos)
    attended = both_low(attended.reshape(row_count, feature_count))
    middle = combined + low_back(jnp.dot(attended, out_weight, precision=highest) + out_bias)
    normed_two = low(layer_norm(middle, norm_two_gain, norm_two_bias))
    hidden_pre = low_back(jnp.dot(normed_two, up_weight, precision=highest) + up_bias)
    activated = low(jax.nn.gelu(hidden_pre, approximate=False))
    output = middle + low_back(jnp.dot(activated, down_weight, precision=highest) + down_bias)
    return (output, key_rows, value_rows)

def reference(tokens, segment_ids, cotangent, norm_one_gain, norm_one_bias, qkv_weight, query_bias, value_bias, out_weight, out_bias, norm_two_gain, norm_two_bias, up_weight, up_bias, down_weight, down_bias, pass_embed):
    weights = tuple((weight_in.astype(jnp.float32) for weight_in in (norm_one_gain, norm_one_bias, qkv_weight, query_bias, value_bias, out_weight, out_bias, norm_two_gain, norm_two_bias, up_weight, up_bias, down_weight, down_bias)))
    embedding = pass_embed.astype(jnp.float32)

    def per_pack(totals, pack_data):
        inputs, segments, grad_out = pack_data

        def first_pass(weights_in, embed_in, inputs_in):
            return one_pass(inputs_in, embed_in[0], weights_in, segments, None)

        def second_pass(weights_in, embed_in, hidden, key_rows, value_rows):
            return one_pass(both_low(hidden), embed_in[1], weights_in, segments, (key_rows, value_rows))[0]
        first_out, first_back = jax.vjp(first_pass, weights, embedding, inputs)
        second_out, second_back = jax.vjp(second_pass, weights, embedding, first_out[0], first_out[1], first_out[2])
        weights_two, embed_two, grad_hidden, grad_keys, grad_values = second_back(grad_out)
        weights_one, embed_one, grad_inputs = first_back((grad_hidden, grad_keys, grad_values))
        totals = jax.tree.map(lambda running, first_term, second_term: running + first_term + second_term, totals, (weights_one, embed_one), (weights_two, embed_two))
        return (totals, (first_out[0], second_out, grad_inputs, grad_hidden))
    initial = jax.tree.map(jnp.zeros_like, (weights, embedding))
    pack_inputs = (tokens.astype(jnp.float32), segment_ids, cotangent.astype(jnp.float32))
    totals, stacked = lax.scan(per_pack, initial, pack_inputs)
    layer_out = jnp.stack([stacked[0], stacked[1]]).astype(jnp.bfloat16)
    grad_flow = jnp.stack([stacked[2], stacked[3]])
    grad_weights, grad_embed = totals
    return (layer_out, grad_flow, grad_weights[0], grad_weights[1], grad_weights[2], grad_weights[3], grad_weights[4], grad_weights[5], grad_weights[6], grad_weights[7], grad_weights[8], grad_weights[9], grad_weights[10], grad_weights[11], grad_weights[12], grad_embed)
```

```python
import jax
import jax.numpy as jnp
from jax import lax
from jax.experimental import pallas as pl
from jax.experimental.pallas import tpu as pltpu
from jax.sharding import PartitionSpec as P

HD = 64
EPS = 1e-05
SCALE = 0.125
FLOOR = -1e30
BF = jnp.bfloat16
F32 = jnp.float32


class K:
    (
        act, acta, actb, activated, att, attended, attended_low, b1, b2, bias, combined, db, down_bias, down_weight,
        ek, embed_row, ev, fetch, g, g1, g2, ga, gab, gabb, gb, gc, gh, gn, gpre, gproj, gprojb, h, hidden_pre, il, k,
        keep, kx, log_total, mid, middle, n2, na, nb, norm_one_bias, norm_one_gain, norm_two_bias, norm_two_gain,
        normed, normed_two, ob, out, out_bias, out_weight, p, part, pe, q, qb, qkv_weight, query_bias, query_heads,
        rs1, rs2, seg, segc, send, slope, small, stacked, terms, ub, ubr, up_bias, up_weight, v, value_bias, vb, vx,
        wdown, wout, wqkv, wup, xh1, xh2, xo, xob, xq, xqb,
    ) = range(88)


def keyed(**arrays):
    return {getattr(K, name): array for name, array in arrays.items()}


def pick(x, index, axis=0):
    return lax.dynamic_index_in_dim(x, index, axis, keepdims=False)


def swap_core(x):
    return lax.ppermute(x, "section", [(0, 1), (1, 0)])


def seq_exchange(x, step):
    count = lax.axis_size("seq")
    route = []
    for sec in range(2):
        flip = 1 << (step ^ sec)
        route += [(sec * count + i, sec * count + (i ^ flip)) for i in range(count)]
    return lax.ppermute(x, ("section", "seq"), route)


def seq_pieces_at_once(block):
    count = lax.axis_size("seq")
    across = lax.ppermute(block, "seq", [(i, i ^ 3) for i in range(count)])
    return [block, seq_exchange(block, 0), seq_exchange(block, 1), across]


def reduce_small(vec):
    vec = vec + swap_core(vec)
    size = lax.axis_size("dp")
    flip = 1
    while flip < size:
        vec = vec + lax.ppermute(vec, "dp", [(i, i ^ flip) for i in range(size)])
        flip *= 2
    return vec


H = 12


epsilon = 1e-05
score_scale = 0.125
floor_value = -1e30


def for_sending(x):
    return jax.tree.map(lambda a: a.astype(jnp.bfloat16) if a.dtype == jnp.float32 else a, x)


def from_behind(x, axis, by):
    size = lax.axis_size(axis)
    return lax.ppermute(x, axis, [(i, (i + by) % size) for i in range(size)])


def shifted_2(block, axis, distance):
    devices = range(lax.axis_size(axis))
    route = [(i - distance, i) for i in devices if i - distance in devices]
    return lax.ppermute(block, axis, route)


def layer_norm(values_in, gain_row, offset):
    center = jnp.mean(values_in, axis=-1, keepdims=True)
    shifted = values_in - center
    spread = jnp.mean(shifted * shifted, axis=-1, keepdims=True)
    return shifted * lax.rsqrt(spread + epsilon) * gain_row + offset


def gelu_exact(inputs):
    return jax.nn.gelu(inputs, approximate=False)


def split_heads(rows_in, head_count):
    return rows_in.reshape(rows_in.shape[0], head_count, rows_in.shape[1] // head_count)


def mask_for(seg_all, cycle_place, row_count):
    pos_keys = jnp.arange(seg_all.shape[0], dtype=jnp.int32)
    query_pos = lax.dynamic_slice_in_dim(pos_keys, cycle_place * row_count, row_count, 0)
    query_seg = lax.dynamic_slice_in_dim(seg_all, cycle_place * row_count, row_count, 0)
    return (query_seg, query_pos, seg_all, pos_keys)


def allowed_pairs(mask_info, first_row, piece_rows):
    query_seg, query_pos, seg_keys, pos_keys = mask_info
    key_pos = lax.dynamic_slice_in_dim(pos_keys, first_row, piece_rows, 0)
    key_seg = lax.dynamic_slice_in_dim(seg_keys, first_row, piece_rows, 0)
    allowed = (key_seg[None, :] == query_seg[:, None]) & (key_pos[None, :] <= query_pos[:, None])
    return allowed[None]


def score_block(queries, key_rows, allowed):
    scores = (
        jnp.einsum("qhd,khd->hqk", queries, key_rows, preferred_element_type=jnp.float32)
        * score_scale
    )
    return jnp.where(allowed, scores, floor_value)


def absorb(running, queries, key_rows, value_rows, allowed):
    row_max, row_sum, weighted = running
    scores = score_block(queries, key_rows, allowed)
    new_max = jnp.maximum(row_max, jnp.max(scores, axis=-1))
    weights = jnp.where(allowed, jnp.exp(scores - new_max[:, :, None]), 0.0)
    factor = jnp.exp(row_max - new_max)
    row_sum = row_sum * factor + jnp.sum(weights, axis=-1)
    update = jnp.einsum(
        "hqk,khd->qhd", weights.astype(jnp.bfloat16), value_rows, preferred_element_type=jnp.float32
    )
    weighted = weighted * jnp.transpose(factor)[:, :, None] + update
    return (new_max, row_sum, weighted)


def absorb_live(running, queries, key_rows, value_rows, allowed, active):
    active = active & jnp.any(allowed)
    return lax.cond(
        active,
        lambda state_in: absorb(state_in, queries, key_rows, value_rows, allowed),
        lambda state_in: state_in,
        running,
    )


def attend_forward(queries, stacked, mask_info, second, head_count):
    row_count = queries.shape[0]
    initial = (
        jnp.full((head_count, row_count), floor_value, jnp.float32),
        jnp.zeros((head_count, row_count), jnp.float32),
        jnp.zeros(queries.shape, jnp.float32),
    )
    always = jnp.array(True)
    running = initial
    key_piece = lax.all_gather(for_sending(stacked), "seq", axis=1, tiled=True)
    allowed = allowed_pairs(mask_info, jnp.int32(0), key_piece.shape[1])
    running = absorb_live(
        running,
        queries,
        split_heads(key_piece[0], head_count),
        split_heads(key_piece[1], head_count),
        allowed,
        always,
    )
    row_max, row_sum, weighted = absorb_live(
        running,
        queries,
        split_heads(key_piece[2], head_count),
        split_heads(key_piece[3], head_count),
        allowed,
        second,
    )
    attended = weighted / jnp.transpose(row_sum)[:, :, None]
    return (attended, row_max + jnp.log(row_sum))


def block_grads(queries, grad_heads, log_total, row_dot, key_rows, value_rows, allowed):
    scores = score_block(queries, key_rows, allowed)
    probabilities = jnp.exp(scores - log_total[:, :, None])
    grad_probs = jnp.einsum(
        "qhd,khd->hqk", grad_heads, value_rows, preferred_element_type=jnp.float32
    )
    grad_scores = (probabilities * (grad_probs - row_dot[:, :, None])).astype(jnp.bfloat16)
    grad_q = (
        jnp.einsum("hqk,khd->qhd", grad_scores, key_rows, preferred_element_type=jnp.float32)
        * score_scale
    )
    grad_k = (
        jnp.einsum("hqk,qhd->khd", grad_scores, queries, preferred_element_type=jnp.float32)
        * score_scale
    )
    grad_v = jnp.einsum(
        "hqk,qhd->khd",
        probabilities.astype(jnp.bfloat16),
        grad_heads,
        preferred_element_type=jnp.float32,
    )
    return (grad_q, grad_k, grad_v)


def grads_live(queries, grad_heads, log_total, row_dot, key_rows, value_rows, allowed, active):
    active = active & jnp.any(allowed)
    zero_grads = (
        jnp.zeros(queries.shape, jnp.float32),
        jnp.zeros(key_rows.shape, jnp.float32),
        jnp.zeros(key_rows.shape, jnp.float32),
    )
    return lax.cond(
        active,
        lambda: block_grads(queries, grad_heads, log_total, row_dot, key_rows, value_rows, allowed),
        lambda: zero_grads,
    )


def attend_backward(
    queries, stacked, grad_heads, log_total, row_dot, mask_info, second, head_count
):
    row_count = stacked.shape[1]
    feature_count = stacked.shape[2]
    always = jnp.array(True)

    def contribution(key_piece, first_row):
        piece_rows = key_piece.shape[1]
        allowed = allowed_pairs(mask_info, first_row, piece_rows)
        own_terms = grads_live(
            queries,
            grad_heads,
            log_total,
            row_dot,
            split_heads(key_piece[0], head_count),
            split_heads(key_piece[1], head_count),
            allowed,
            always,
        )
        other = grads_live(
            queries,
            grad_heads,
            log_total,
            row_dot,
            split_heads(key_piece[2], head_count),
            split_heads(key_piece[3], head_count),
            allowed,
            second,
        )
        key_terms = jnp.stack([own_terms[1], own_terms[2], other[1], other[2]]).reshape(
            4, piece_rows, feature_count
        )
        return (own_terms[0] + other[0], key_terms)

    cycle_size = lax.axis_size("seq")
    cycle_place = lax.axis_index("seq")

    def cycle_turn(turn_index, cycle_state):
        moving, gathered, grad_q = cycle_state
        first_row = (cycle_place + turn_index) % cycle_size * row_count
        part_q, key_terms = contribution(moving, first_row)
        moving = jax.tree.map(
            lambda part, own: part.astype(own.dtype),
            from_behind(for_sending(moving), "seq", -1),
            moving,
        )
        gathered = from_behind(gathered + key_terms, "seq", -1)
        return (moving, gathered, grad_q + part_q)

    initial = (
        stacked,
        jnp.zeros(stacked.shape, jnp.float32),
        jnp.zeros(queries.shape, jnp.float32),
    )
    finished = lax.fori_loop(0, cycle_size, cycle_turn, initial)
    return (finished[2], finished[1])


def layer_forward(hidden_in, extra_rows, params, mask_info, second, head_count):
    row_count, feature_count = hidden_in.shape
    combined = hidden_in + params[K.embed_row]
    normed = layer_norm(combined, params[K.norm_one_gain], params[K.norm_one_bias]).astype(
        jnp.bfloat16
    )
    projected = jnp.dot(normed, params[K.qkv_weight], preferred_element_type=jnp.float32)
    queries = (projected[:, :feature_count] + params[K.query_bias]).astype(jnp.bfloat16)
    key_rows = projected[:, feature_count : 2 * feature_count].astype(jnp.bfloat16)
    value_rows = (projected[:, 2 * feature_count :] + params[K.value_bias]).astype(jnp.bfloat16)
    stacked = jnp.concatenate([jnp.stack([key_rows, value_rows]), extra_rows], axis=0)
    query_heads = split_heads(queries, head_count)
    attended, log_total = attend_forward(query_heads, stacked, mask_info, second, head_count)
    attended_low = attended.reshape(row_count, feature_count).astype(jnp.bfloat16)
    middle = (
        combined
        + jnp.dot(attended_low, params[K.out_weight], preferred_element_type=jnp.float32)
        + params[K.out_bias]
    )
    normed_two = layer_norm(middle, params[K.norm_two_gain], params[K.norm_two_bias]).astype(
        jnp.bfloat16
    )
    hidden_pre = (
        jnp.dot(normed_two, params[K.up_weight], preferred_element_type=jnp.float32)
        + params[K.up_bias]
    )
    activated = gelu_exact(hidden_pre).astype(jnp.bfloat16)
    output = (
        middle
        + jnp.dot(activated, params[K.down_weight], preferred_element_type=jnp.float32)
        + params[K.down_bias]
    )
    saved_values = keyed(
        combined=combined,
        normed=normed,
        query_heads=query_heads,
        stacked=stacked,
        attended=attended,
        log_total=log_total,
        attended_low=attended_low,
        middle=middle,
        normed_two=normed_two,
        hidden_pre=hidden_pre,
        activated=activated,
    )
    return (output, saved_values)


def layer_backward(grad_top, saved_values, extra_grads, params, mask_info, second, head_count):
    row_count, feature_count = grad_top.shape
    gradients = {}
    grad_branch = grad_top.astype(jnp.bfloat16)
    gradients[K.down_weight] = jnp.einsum(
        "tf,td->fd", saved_values[K.activated], grad_branch, preferred_element_type=jnp.float32
    )
    gradients[K.down_bias] = jnp.sum(grad_branch.astype(jnp.float32), axis=0)
    grad_activated = jnp.einsum(
        "td,fd->tf", grad_branch, params[K.down_weight], preferred_element_type=jnp.float32
    )
    grad_pre = jax.vjp(gelu_exact, saved_values[K.hidden_pre])[1](grad_activated)[0].astype(
        jnp.bfloat16
    )
    gradients[K.up_weight] = jnp.einsum(
        "td,tf->df", saved_values[K.normed_two], grad_pre, preferred_element_type=jnp.float32
    )
    gradients[K.up_bias] = jnp.sum(grad_pre.astype(jnp.float32), axis=0)
    grad_normed_two = jnp.einsum(
        "tf,df->td", grad_pre, params[K.up_weight], preferred_element_type=jnp.float32
    )
    norm_back = jax.vjp(
        layer_norm, saved_values[K.middle], params[K.norm_two_gain], params[K.norm_two_bias]
    )[1]
    grad_middle_norm, gradients[K.norm_two_gain], gradients[K.norm_two_bias] = norm_back(
        grad_normed_two
    )
    grad_middle = grad_top + grad_middle_norm
    grad_attn_branch = grad_middle.astype(jnp.bfloat16)
    gradients[K.out_weight] = jnp.einsum(
        "tc,td->cd",
        saved_values[K.attended_low],
        grad_attn_branch,
        preferred_element_type=jnp.float32,
    )
    gradients[K.out_bias] = jnp.sum(grad_attn_branch.astype(jnp.float32), axis=0)
    grad_attended = jnp.einsum(
        "td,cd->tc", grad_attn_branch, params[K.out_weight], preferred_element_type=jnp.float32
    ).astype(jnp.bfloat16)
    grad_heads = split_heads(grad_attended, head_count)
    row_dot = jnp.einsum("qhd,qhd->hq", grad_heads.astype(jnp.float32), saved_values[K.attended])
    grad_q, key_grads = attend_backward(
        saved_values[K.query_heads],
        saved_values[K.stacked],
        grad_heads,
        saved_values[K.log_total],
        row_dot,
        mask_info,
        second,
        head_count,
    )
    grad_queries = grad_q.reshape(row_count, feature_count).astype(jnp.bfloat16)
    grad_keys = (key_grads[0] + extra_grads[0]).astype(jnp.bfloat16)
    grad_values = (key_grads[1] + extra_grads[1]).astype(jnp.bfloat16)
    grad_projected = jnp.concatenate([grad_queries, grad_keys, grad_values], axis=1)
    gradients[K.qkv_weight] = jnp.einsum(
        "tc,tk->ck", saved_values[K.normed], grad_projected, preferred_element_type=jnp.float32
    )
    gradients[K.query_bias] = jnp.sum(grad_queries.astype(jnp.float32), axis=0)
    gradients[K.value_bias] = jnp.sum(grad_values.astype(jnp.float32), axis=0)
    grad_normed = jnp.einsum(
        "tk,ck->tc", grad_projected, params[K.qkv_weight], preferred_element_type=jnp.float32
    )
    first_back = jax.vjp(
        layer_norm, saved_values[K.combined], params[K.norm_one_gain], params[K.norm_one_bias]
    )[1]
    grad_combined_norm, gradients[K.norm_one_gain], gradients[K.norm_one_bias] = first_back(
        grad_normed
    )
    grad_combined = grad_middle + grad_combined_norm
    gradients[K.embed_row] = jnp.sum(grad_combined, axis=0)
    return (grad_combined, key_grads[2:], gradients)


def with_embed(base_params, pass_embed, pass_index):
    params = dict(base_params)
    params[K.embed_row] = lax.dynamic_index_in_dim(
        pass_embed, pass_index, 0, keepdims=False
    ).astype(jnp.float32)
    return params


def run_split(tokens_used, cot_used, seg_used, base_params, pass_embed, cycle_place, head_count):
    micro_count, row_count, feature_count = tokens_used.shape
    section_index = lax.axis_index("section")
    second = section_index == 1
    params = with_embed(base_params, pass_embed, section_index)
    received = jnp.zeros((3, row_count, feature_count), jnp.bfloat16)
    saved_inputs = jnp.zeros((micro_count, 3, row_count, feature_count), jnp.bfloat16)
    outputs = jnp.zeros((micro_count, row_count, feature_count), jnp.bfloat16)
    for tick_index in range(micro_count + 1):
        slot_index = tick_index - section_index
        is_valid = (slot_index >= 0) & (slot_index < micro_count)
        slot_index = jnp.clip(slot_index, 0, micro_count - 1)
        own_in = lax.dynamic_index_in_dim(tokens_used, slot_index, 0, keepdims=False)
        seg_all = lax.dynamic_index_in_dim(seg_used, slot_index, 0, keepdims=False)
        mask_info = mask_for(seg_all, cycle_place, row_count)
        hidden_in = jnp.where(second, received[0], own_in).astype(jnp.float32)
        extra_rows = jnp.where(second, received[1:], jnp.zeros_like(received[1:]))
        output, saved_values = layer_forward(
            hidden_in, extra_rows, params, mask_info, second, head_count
        )
        output_low = output.astype(jnp.bfloat16)
        current = lax.dynamic_index_in_dim(outputs, slot_index, 0, keepdims=False)
        outputs = lax.dynamic_update_index_in_dim(
            outputs, jnp.where(is_valid, output_low, current), slot_index, 0
        )
        current_in = lax.dynamic_index_in_dim(saved_inputs, slot_index, 0, keepdims=False)
        saved_inputs = lax.dynamic_update_index_in_dim(
            saved_inputs, jnp.where(is_valid, received, current_in), slot_index, 0
        )
        stacked = saved_values[K.stacked]
        received = shifted_2(
            for_sending(jnp.stack([output_low, stacked[0], stacked[1]])), "section", 1
        )
    incoming = jnp.zeros((3, row_count, feature_count), jnp.float32)
    flows = jnp.zeros((micro_count, row_count, feature_count), jnp.float32)
    totals = None
    for tick_index in range(micro_count + 1):
        slot_index = tick_index - 1 + section_index
        is_valid = (slot_index >= 0) & (slot_index < micro_count)
        slot_index = jnp.clip(slot_index, 0, micro_count - 1)
        stored = lax.dynamic_index_in_dim(saved_inputs, slot_index, 0, keepdims=False)
        own_in = lax.dynamic_index_in_dim(tokens_used, slot_index, 0, keepdims=False)
        seg_all = lax.dynamic_index_in_dim(seg_used, slot_index, 0, keepdims=False)
        mask_info = mask_for(seg_all, cycle_place, row_count)
        hidden_in = jnp.where(second, stored[0], own_in).astype(jnp.float32)
        extra_rows = jnp.where(second, stored[1:], jnp.zeros_like(stored[1:]))
        output, saved_values = layer_forward(
            hidden_in, extra_rows, params, mask_info, second, head_count
        )
        outer_grad = lax.dynamic_index_in_dim(cot_used, slot_index, 0, keepdims=False).astype(
            jnp.float32
        )
        grad_top = jnp.where(second, outer_grad, incoming[0])
        grad_in, extra_grads, gradients = layer_backward(
            grad_top, saved_values, incoming[1:], params, mask_info, second, head_count
        )
        grad_low = grad_in.astype(jnp.bfloat16).astype(jnp.float32)
        flow_value = jnp.where(second, grad_low, grad_in)
        current = lax.dynamic_index_in_dim(flows, slot_index, 0, keepdims=False)
        flows = lax.dynamic_update_index_in_dim(
            flows, jnp.where(is_valid, flow_value, current), slot_index, 0
        )
        gradients = jax.tree.map(lambda addend: jnp.where(is_valid, addend, 0.0), gradients)
        if totals is None:
            totals = gradients
        else:
            totals = jax.tree.map(lambda running, addend: running + addend, totals, gradients)
        incoming = shifted_2(jnp.concatenate([grad_low[None], extra_grads], axis=0), "section", -1)
    embed_rows = jnp.where(
        jnp.arange(2, dtype=jnp.int32)[:, None] == section_index, totals[K.embed_row][None, :], 0.0
    )
    return (outputs, flows, totals, embed_rows)


def split_body(
    tokens,
    segment_ids,
    cotangent,
    norm_one_gain,
    norm_one_bias,
    qkv_weight,
    query_bias,
    value_bias,
    out_weight,
    out_bias,
    norm_two_gain,
    norm_two_bias,
    up_weight,
    up_bias,
    down_weight,
    down_bias,
    pass_embed,
):
    head_count = H
    section_index = lax.axis_index("section")
    cycle_place = lax.axis_index("seq")
    base_params = keyed(
        norm_one_gain=norm_one_gain.astype(jnp.float32),
        norm_one_bias=norm_one_bias.astype(jnp.float32),
        qkv_weight=qkv_weight,
        query_bias=query_bias.astype(jnp.float32),
        value_bias=value_bias.astype(jnp.float32),
        out_weight=out_weight,
        out_bias=out_bias.astype(jnp.float32),
        norm_two_gain=norm_two_gain.astype(jnp.float32),
        norm_two_bias=norm_two_bias.astype(jnp.float32),
        up_weight=up_weight,
        up_bias=up_bias.astype(jnp.float32),
        down_weight=down_weight,
        down_bias=down_bias.astype(jnp.float32),
    )
    tokens_used, cot_used, seg_used = (tokens, cotangent, segment_ids)
    outputs, flows, totals, embed_rows = run_split(
        tokens_used, cot_used, seg_used, base_params, pass_embed, cycle_place, head_count
    )
    summed = lax.psum(
        (
            totals[K.norm_one_gain],
            totals[K.norm_one_bias],
            totals[K.qkv_weight],
            totals[K.query_bias],
            totals[K.value_bias],
            totals[K.out_weight],
            totals[K.out_bias],
            totals[K.norm_two_gain],
            totals[K.norm_two_bias],
            totals[K.up_weight],
            totals[K.up_bias],
            totals[K.down_weight],
            totals[K.down_bias],
            embed_rows,
        ),
        ("section", "dp", "seq"),
    )
    embed_share = lax.dynamic_slice_in_dim(summed[13], section_index, 1, 0)
    return (
        outputs[None],
        flows[None],
        summed[0],
        summed[1],
        summed[2],
        summed[3],
        summed[4],
        summed[5],
        summed[6],
        summed[7],
        summed[8],
        summed[9],
        summed[10],
        summed[11],
        summed[12],
        embed_share,
    )


QB = 128
AB = 256
ANY = pl.BlockSpec(memory_space=pl.ANY)
VM = pl.BlockSpec(memory_space=pltpu.VMEM)
SM = pl.BlockSpec(memory_space=pltpu.SMEM)
N_SEQ, N_Z = 4, 4
BRIEF = pl.CostEstimate(flops=1, bytes_accessed=1, transcendentals=0)
LONG = pl.CostEstimate(flops=40_000_000_000, bytes_accessed=1, transcendentals=0)
ORDER = ((4096, 4096), F32)
R_G1, R_B1, R_VB, R_QB, R_OB, R_G2, R_B2, R_DB, R_PE, R_UB, N_SMALL = 0, 1, 2, 3, 4, 5, 6, 7, 8, 10, 16


def kdot(a, b, ca, cb):
    return lax.dot_general(a, b, (((ca,), (cb,)), ((), ())), preferred_element_type=F32)


def cols(j, n):
    return pl.ds(pl.multiple_of(j * n, n), n)


def norm_rows(x):
    center = jnp.mean(x, axis=-1, keepdims=True)
    shifted = x - center
    spread = jnp.mean(shifted * shifted, axis=-1, keepdims=True)
    rstd = lax.rsqrt(spread + EPS)
    return shifted * rstd, rstd


def row(ref):
    return ref[...].astype(F32).reshape(1, ref.shape[0])


def my_place():
    return tuple(lax.axis_index(a) for a in ("section", "dp", "seq"))


def piece_sources(s, q):
    first = jnp.where(s == 0, 1, 2)
    return [q, q ^ first, q ^ (3 - first), q ^ 3]


def low_half(rows):
    return lax.broadcasted_iota(jnp.int32, (rows, 128), 1) < HD


def stack_heads(x, low):
    zero = jnp.zeros_like(x)
    return jnp.concatenate([jnp.where(low, x, zero), jnp.where(low, zero, x)], axis=0)


class Copies:
    def __init__(self, sems):
        self.sems, self.count = sems, 0

    def start(self, src, dst):
        copy = pltpu.make_async_copy(src, dst, self.sems.at[self.count])
        self.count += 1
        copy.start()
        return copy


def wait_all(copies):
    for copy in copies:
        copy.wait()


def pass_forward(c, ns, rows, ready, save):
    d, ff = c[K.h].shape[1], c[K.act].shape[1]
    h, s = c[K.h], lax.axis_index("section")
    g1, b1, ob, g2, b2, db, qb, vb = (row(c[n]) for n in (K.g1, K.b1, K.ob, K.g2, K.b2, K.db, K.qb, K.vb))
    em = c[K.pe][ns - 1 : ns, :].astype(F32)
    c[K.ubr][...] = row(c[K.ub])
    seg = c[K.seg][pl.ds(s, 1), :]
    c[K.segc][...] = jnp.broadcast_to(seg, (128, rows)).T
    ready(K.h)

    def ln1(b, carry):
        r = cols(b, QB)
        xh, rstd = norm_rows(h[r, :].astype(F32) + em)
        c[K.xh1][r, :] = xh
        c[K.rs1][r, :] = jnp.broadcast_to(rstd, (QB, 128))
        c[K.normed][r, :] = (xh * g1 + b1).astype(BF)
        same = c[K.segc][r, 0:1] == seg
        query = lax.broadcasted_iota(jnp.int32, (QB, rows), 0) + b * QB
        key = lax.broadcasted_iota(jnp.int32, (QB, rows), 1)
        c[K.bias][r, :] = jnp.where(same & (key <= query), 0.0, FLOOR)
        return carry

    lax.fori_loop(0, rows // QB, ln1, 0)
    save(K.normed, K.xh1, K.rs1)
    ready(K.wqkv)
    normed = c[K.normed]
    c[K.part](K.wqkv, 0)
    q = kdot(normed[...], c[K.wqkv][:, 0:d], 1, 0) + qb
    c[K.q][...] = q.astype(BF) * jnp.asarray(SCALE, BF)
    c[K.part](K.wqkv, 1)
    c[K.k][...] = kdot(normed[...], c[K.wqkv][:, d : 2 * d], 1, 0).astype(BF)
    c[K.part](K.wqkv, 2)
    v = kdot(normed[...], c[K.wqkv][:, 2 * d : 3 * d], 1, 0) + vb
    c[K.v][...] = v.astype(BF)
    save(K.q, K.k, K.v)
    low = low_half(AB)
    sets = [(c[K.k], c[K.v])]
    if ns == 2:
        ready(K.kx, K.vx)
        sets.append((c[K.kx], c[K.vx]))

    def pair(hp, carry):
        at = cols(hp, 128)
        for i in range(rows // AB):
            r, nk = slice(i * AB, (i + 1) * AB), (i + 1) * AB
            qs = stack_heads(c[K.q][r, at], low)
            mask = c[K.bias][r, 0:nk]
            mask = jnp.concatenate([mask, mask], axis=0)
            scores = [kdot(qs, k[0:nk, at], 1, 1) + mask for k, _ in sets]
            top = jnp.max(scores[0], axis=-1, keepdims=True)
            for x in scores[1:]:
                top = jnp.maximum(top, jnp.max(x, axis=-1, keepdims=True))
            acc = None
            for n, ((_, v), x) in enumerate(zip(sets, scores)):
                w = jnp.exp(x - top).astype(BF)
                c[K.p][i][hp, :, n * nk : (n + 1) * nk] = w
                ones = jnp.ones((nk, 128), BF)
                y = kdot(w, jnp.concatenate([v[0:nk, at], ones], axis=1), 1, 0)
                acc = y if acc is None else acc + y
            inv = 1.0 / acc[:, 128:]
            o = acc[:, :128] * inv
            c[K.att][r, at] = jnp.where(low, o[:AB], o[AB:]).astype(BF)
            c[K.il][r, at] = jnp.where(low, inv[:AB], inv[AB:])
        return carry

    lax.fori_loop(0, d // 128, pair, 0, unroll=3)
    save(K.p, K.att, K.il)
    ready(K.wout)
    c[K.mid][...] = kdot(c[K.att][...], c[K.wout][...], 1, 0) + (h[...].astype(F32) + (em + ob))

    def ln2(b, carry):
        r = cols(b, QB)
        xh, rstd = norm_rows(c[K.mid][r, :])
        c[K.xh2][r, :] = xh
        c[K.rs2][r, :] = jnp.broadcast_to(rstd, (QB, 128))
        c[K.n2][r, :] = (xh * g2 + b2).astype(BF)
        return carry

    lax.fori_loop(0, rows // QB, ln2, 0)
    save(K.n2, K.xh2, K.rs2)
    ready(K.wup)

    def up(j, carry):
        at = cols(j, d)
        x = kdot(c[K.n2][...], c[K.wup][:, at], 1, 0) + c[K.ubr][:, at]
        cdf = 0.5 + 0.5 * lax.erf(x * 0.7071067811865476)
        c[K.act][:, at] = (x * cdf).astype(BF)
        bell = jnp.exp(-0.5 * (x * x)) * 0.3989422804014327
        c[K.slope][:, at] = (cdf + x * bell).astype(BF)
        return carry

    lax.fori_loop(0, ff // d, up, 0)
    save(K.act, K.slope)
    ready(K.wdown)
    y = kdot(c[K.act][...], c[K.wdown][...], 1, 0)
    c[K.out][...] = (c[K.mid][...] + y + db).astype(BF)
    save(K.out)


def norm_back_rows(rows, g_ref, xh_ref, rs_ref, gain, put):
    d = g_ref.shape[1]

    def step(b, sums):
        r = cols(b, QB)
        g, xh = g_ref[r, :], xh_ref[r, :]
        dx = g * gain
        m1 = jnp.mean(dx, axis=-1, keepdims=True)
        m2 = jnp.mean(dx * xh, axis=-1, keepdims=True)
        rstd = jnp.concatenate([rs_ref[r, :]] * (d // 128), axis=1)
        extra = put(r, rstd * (dx - m1 - xh * m2))
        new = (jnp.sum(g * xh, 0, keepdims=True), jnp.sum(g, 0, keepdims=True)) + extra
        return tuple(a + b_ for a, b_ in zip(sums, new))

    zero = jnp.zeros((1, d), F32)
    return lax.fori_loop(0, rows // QB, step, (zero,) * 4)


def back_hidden(c, ready, save):
    d, ff = c[K.g].shape[1], c[K.gpre].shape[1]
    small = c[K.small]
    ready(K.g, K.slope, K.wdown)

    def step(j, carry):
        at = cols(j, d)
        c[K.part](K.wdown, j)
        c[K.part](K.slope, j)
        gp = kdot(c[K.g][...], c[K.wdown][at, :], 1, 1) * c[K.slope][:, at].astype(F32)
        c[K.gpre][:, at] = gp.astype(BF)
        small[pl.ds(R_UB + j, 1), :] = jnp.sum(gp, 0, keepdims=True)
        return carry

    lax.fori_loop(0, ff // d, step, 0)
    save(K.gpre)


def back_norm_two(c, rows, ready, save, parts=1):
    small = c[K.small]
    ready(K.gpre, K.wup)
    for j in range(parts):
        at = slice(j * c[K.gpre].shape[1] // parts, (j + 1) * c[K.gpre].shape[1] // parts)
        c[K.part](K.gpre, j)
        c[K.part](K.wup, j)
        y = kdot(c[K.gpre][:, at], c[K.wup][:, at], 1, 1)
        c[K.gn][...] = y if j == 0 else c[K.gn][...] + y

    ready(K.xh2, K.rs2, K.g)

    def put(r, x):
        g = c[K.g][r, :].astype(F32)
        gm = g + x
        c[K.mid][r, :] = gm
        gab = gm.astype(BF)
        c[K.gab][r, :] = gab
        return (jnp.sum(g, 0, keepdims=True), jnp.sum(gab.astype(F32), 0, keepdims=True))

    sums = norm_back_rows(rows, c[K.gn], c[K.xh2], c[K.rs2], row(c[K.g2]), put)
    for at, x in zip((R_G2, R_B2, R_DB, R_OB), sums):
        small[at : at + 1, :] = x
    save(K.gab)


def back_attended(c, ready, save):
    ready(K.wout)
    c[K.ga][...] = kdot(c[K.gab][...], c[K.wout][...], 1, 1).astype(BF)
    save(K.ga)


def back_heads(c, ns, rows, add, ready, save):
    d = c[K.ga].shape[1]
    low = low_half(AB)
    ready(K.ga, K.q, K.k, K.v, K.il, K.att, K.p, K.ek, K.ev)
    sets = [(c[K.k], c[K.v])] + ([(c[K.kx], c[K.vx])] if ns == 2 else [])
    nb = rows // AB

    def pair(hp, carry):
        at = cols(hp, 128)
        sums_k, sums_v = [[] for _ in sets], [[] for _ in sets]
        for i in range(nb):
            r, nk = slice(i * AB, (i + 1) * AB), (i + 1) * AB
            qs = stack_heads(c[K.q][r, at], low)
            scaled = c[K.ga][r, at].astype(F32) * c[K.il][r, at]
            gs = stack_heads(scaled.astype(BF), low)
            dots = stack_heads(scaled * c[K.att][r, at].astype(F32), low)
            dots = jnp.sum(dots, axis=-1, keepdims=True)
            qs_t, gs_t = qs.T, gs.T
            gq = None
            for n, (k, v) in enumerate(sets):
                p = c[K.p][i][hp, :, n * nk : (n + 1) * nk]
                dp = kdot(gs, v[0:nk, at], 1, 1)
                ds = (p.astype(F32) * (dp - dots)).astype(BF)
                y = kdot(ds, k[0:nk, at], 1, 0)
                gq = y if gq is None else gq + y
                for sums, left, right in ((sums_k[n], qs_t, ds), (sums_v[n], gs_t, p)):
                    part = kdot(left, right, 1, 0)
                    for j in range(i):
                        sums[j] = sums[j] + part[:, j * AB : (j + 1) * AB]
                    sums.append(part[:, i * AB :])
            gq = gq * SCALE
            c[K.gproj][r, at] = jnp.where(low, gq[:AB], gq[AB:]).astype(BF)
        at_k = pl.ds(pl.multiple_of(d + hp * 128, 128), 128)
        at_v = pl.ds(pl.multiple_of(2 * d + hp * 128, 128), 128)
        for j in range(nb):
            r = slice(j * AB, (j + 1) * AB)
            gk, gv = sums_k[0][j].T, sums_v[0][j].T
            if add:
                gk, gv = gk + c[K.ek][r, at], gv + c[K.ev][r, at]
            c[K.gproj][r, at_k] = gk.astype(BF)
            c[K.gproj][r, at_v] = gv.astype(BF)
            if ns == 2:
                c[K.ek][r, at] = sums_k[1][j].T
                c[K.ev][r, at] = sums_v[1][j].T
        return carry

    lax.fori_loop(0, d // 128, pair, 0, unroll=3)
    save(K.gproj, K.ek, K.ev)


def back_norm_one(c, rows, pe_row, ready, save):
    d = c[K.gn].shape[1]
    small = c[K.small]
    ready(K.gproj, K.wqkv)
    c[K.gn][...] = kdot(c[K.gproj][...], c[K.wqkv][...], 1, 1)

    def put(r, x):
        gc = c[K.mid][r, :] + x
        if K.gc in c:
            c[K.gc][r, :] = gc
        else:
            c[K.gh][r, :] = gc.astype(BF)
        gq = jnp.sum(c[K.gproj][r, 0:d].astype(F32), 0, keepdims=True)
        small[R_VB : R_VB + 1, :] += jnp.sum(c[K.gproj][r, 2 * d :].astype(F32), 0, keepdims=True)
        return (jnp.sum(gc, 0, keepdims=True), gq)

    ready(K.mid, K.xh1, K.rs1)
    sums = norm_back_rows(rows, c[K.gn], c[K.xh1], c[K.rs1], row(c[K.g1]), put)
    for at, x in zip((R_G1, R_B1, pe_row, R_QB), sums):
        small[at : at + 1, :] = x
    save(K.gc, K.gh)


VECTORS = (K.g1, K.b1, K.ob, K.g2, K.b2, K.db, K.qb, K.vb, K.ub, K.pe, K.seg)


def run_kernel(name, t, ins, outs, scratch, body_fn, in_order, pieces=(), sliced=None, cut=None, limit=60):
    sliced, cut = sliced or {}, cut or {}
    vmem = [n for n in ins if n in VECTORS]
    hbm = [n for n in ins if n not in vmem]
    names = vmem + hbm
    in_specs = {n: ([1] * len(ins[n]) if isinstance(ins[n], list) else 1) for n in names}

    def flat(specs):
        result = []
        for s in specs.values():
            result += s if isinstance(s, list) else [s]
        return result

    def take(refs, specs):
        result = {}
        for n, s in specs.items():
            if isinstance(s, list):
                result[n], refs = list(refs[: len(s)]), refs[len(s) :]
            else:
                result[n], refs = refs[0], refs[1:]
        return result, refs

    flat_in = flat({n: ins[n] for n in names})
    many = {n for n, s in {**outs, **scratch}.items() if isinstance(s, list)}

    makes = t is None

    def kernel(*refs):
        given, refs = take(refs, in_specs)
        target, refs = take(refs if makes else refs[1:], outs)
        c, refs = take(refs[1:], scratch)
        in_sems, out_sems = refs
        for n in vmem:
            c[n] = given[n]
        place = my_place()
        incoming, outgoing = Copies(in_sems), Copies(out_sems)
        waiting, sent, first_part, parts_sent = {}, {}, {}, {}

        def part_of(n, index):
            dim, count = cut[n]
            size = c[n].shape[dim] // count
            at = (slice(None),) * dim + (cols(index, size),)
            return pltpu.make_async_copy(given[n].at[at], c[n].at[at], in_sems.at[first_part[n] + index])

        for n in in_order:
            if n in cut:
                if n not in first_part:
                    first_part[n] = incoming.count
                    incoming.count += cut[n][1]
                    parts_sent[n] = 0
                part_of(n, parts_sent[n]).start()
                parts_sent[n] += 1
            elif n in pieces:
                block = given[n][0].shape[0]
                places = piece_sources(place[0], place[2])
                waiting[n] = [incoming.start(x, c[n].at[cols(at, block)]) for x, at in zip(given[n], places)]
            elif n in sliced:
                first, width = sliced[n]
                at = pl.ds(pl.multiple_of(first(*place), 128), width)
                waiting[n] = [incoming.start(given[n].at[:, at], c[n])]
            elif n in many:
                waiting[n] = [incoming.start(a, b) for a, b in zip(given[n], c[n])]
            else:
                waiting[n] = [incoming.start(given[n], c[n])]

        def ready(*names):
            for n in names:
                wait_all(waiting.pop(n, []))

        def fetch(n):
            first, width = sliced[n]
            at = pl.ds(pl.multiple_of(first(*place), 128), width)
            waiting[n] = [incoming.start(given[n].at[:, at], c[n])]

        def save(*names):
            for n in names:
                if n in target:
                    pairs = zip(*((x[n] if n in many else [x[n]]) for x in (c, target)))
                    sent[n] = [outgoing.start(a, b) for a, b in pairs]

        def part(n, index):
            if n in cut:
                part_of(n, index).wait()

        c[K.fetch], c[K.part] = fetch, part
        body_fn(c, ready, save)
        for n in list(waiting):
            ready(n)
        for n in sent:
            wait_all(sent[n])

    result = pl.pallas_call(
        kernel,
        out_shape=[jax.ShapeDtypeStruct(*s) for s in flat(outs)] + [jax.ShapeDtypeStruct(*ORDER)],
        in_specs=[VM] * len(vmem) + [ANY] * (len(flat_in) - len(vmem)) + [ANY] * (not makes),
        out_specs=[ANY] * (len(flat(outs)) + 1),
        scratch_shapes=[pltpu.VMEM(*s) for s in flat(scratch)]
        + [pltpu.SemaphoreType.DMA((len(flat_in) - len(vmem) + sum(k for _, k in cut.values()) + 1,)), pltpu.SemaphoreType.DMA((len(flat(outs)) + 1,))],
        input_output_aliases={} if makes else {len(flat_in): len(flat(outs))},
        compiler_params=pltpu.CompilerParams(vmem_limit_bytes=limit * 1024 * 1024),
        cost_estimate=BRIEF,
        name=name,
    )(*flat_in, *([] if makes else [t]))
    result, (t,) = take(list(result), outs)
    return result, t


def shapes_for(rows, d, ff, ns):
    low, full = lambda n: ((rows, n), BF), lambda n: ((rows, n), F32)
    p = [((d // 128, 2 * AB, ns * AB * (i + 1)), BF) for i in range(rows // AB)]
    return keyed(
        h=low(d), normed=low(d), xh1=full(d), rs1=full(128), q=low(d), k=low(d), v=low(d), kx=low(d), vx=low(d),
        p=p, att=low(d), il=full(d), mid=full(d), n2=low(d), xh2=full(d), rs2=full(128), act=low(ff),
        slope=low(ff), out=low(d), bias=full(rows), wqkv=((d, 3 * d), BF), wout=((d, d), BF),
        wup=((d, ff), BF), wdown=((ff, d), BF), g=low(d), gpre=low(ff), gn=full(d), gab=low(d), ga=low(d),
        ubr=((1, ff), F32), segc=((rows, 128), jnp.int32), gproj=low(3 * d), ek=full(d), ev=full(d), gh=low(d), gc=full(d), small=((N_SMALL, d), F32),
    )


def sub(shapes, *names):
    return {n: shapes[n] for n in names}


def weight_term(xa, ga, xb, gb):
    return (kdot(xa, ga, 0, 0) + kdot(xb, gb, 0, 0)).astype(BF)


def store_slabs(ref, y):
    for j in range(ref.shape[0]):
        ref[j] = y[j * ref.shape[1] : (j + 1) * ref.shape[1]]


def kernel_first(t, ins, rows, d, ff):
    sh = shapes_for(rows, d, ff, 1)
    outs = sub(sh, K.normed, K.xh1, K.rs1, K.q, K.k, K.v, K.p, K.att, K.il, K.n2, K.xh2, K.rs2, K.act, K.slope, K.out)
    scratch = {**sub(sh, K.wqkv, K.wout, K.wup, K.wdown, K.h, K.mid, K.bias, K.ubr, K.segc), **outs}

    def run(c, ready, save):
        pass_forward(c, 1, rows, ready, save)

    order = [K.h, K.wqkv, K.wqkv, K.wqkv, K.wout, K.wup, K.wdown]
    return run_kernel("pass_one", t, ins, outs, scratch, run, order, pieces=(K.h,), cut=keyed(wqkv=(1, 3)))


def kernel_second(t, ins, rows, d, ff):
    sh = shapes_for(rows, d, ff, 2)
    n = ff // N_SEQ // 2
    half = ((N_Z, n // N_Z, d), BF)
    outs = sub(sh, K.normed, K.att, K.n2, K.out, K.gpre, K.gab, K.gproj, K.ek, K.ev, K.gh, K.small)
    outs.update(keyed(keep=half, send=half))
    scratch = {
        **sub(sh, K.wqkv, K.wout, K.wup, K.wdown, K.h, K.mid, K.bias, K.kx, K.vx, K.xh1, K.rs1, K.q, K.k, K.v, K.p, K.il, K.xh2, K.rs2, K.slope, K.gn, K.act, K.g, K.ubr, K.segc),
        **outs,
    }
    scratch.update(keyed(actb=((rows, 2 * n), BF)))
    del scratch[K.gpre]

    def run(c, ready, save):
        s, _, q = my_place()
        c[K.small][...] = jnp.zeros_like(c[K.small])
        pass_forward(c, 2, rows, ready, save)
        c[K.actb][...] = c[K.act][:, cols(q, 2 * n)]
        c[K.gpre], c[K.ga], c[K.acta] = c[K.act], c[K.h], c[K.slope].at[:, 0 : 2 * n]
        back_hidden(c, ready, save)
        c[K.fetch](K.acta)
        back_norm_two(c, rows, ready, save)
        back_attended(c, ready, save)
        back_heads(c, 2, rows, False, ready, save)
        back_norm_one(c, rows, R_PE + 1, ready, save)
        save(K.small)
        ready(K.acta)
        for name, side in ((K.send, 1 - s), (K.keep, s)):
            at = cols(side, n)
            store_slabs(c[name], weight_term(c[K.acta][:, at], c[K.gh][...], c[K.actb][:, at], c[K.g][...]))
            save(name)

    order = [K.h, K.wqkv, K.wqkv, K.wqkv, K.kx, K.vx, K.wout, K.wup, K.wdown, K.g]
    return run_kernel("pass_two_and_back", t, ins, outs, scratch, run, order, pieces=(K.g,),
                      sliced=keyed(acta=(lambda s, z, q: q * 2 * n, 2 * n)), cut=keyed(wqkv=(1, 3)), limit=63)


def kernel_back_up(t, ins, rows, d, ff):
    sh = shapes_for(rows, d, ff, 1)
    n, m = d // 2, ff // N_SEQ
    half = ((N_Z, n // N_Z, m), BF)
    outs = sub(sh, K.gpre, K.small)
    outs.update(keyed(keep=half, send=half))
    scratch = {**sub(sh, K.g, K.slope, K.wdown), **outs, K.na: ((rows, d), BF), K.nb: ((rows, d), BF), K.gb: ((rows, m), BF)}

    def run(c, ready, save):
        s, _, q = my_place()
        c[K.small][...] = jnp.zeros_like(c[K.small])
        back_hidden(c, ready, save)
        save(K.small)
        ready(K.na, K.nb, K.gb)
        ga = c[K.gpre][:, cols(q, m)]
        for name, side in ((K.send, 1 - s), (K.keep, s)):
            at = cols(side, n)
            store_slabs(c[name], weight_term(c[K.na][:, at], ga, c[K.nb][:, at], c[K.gb][...]))
            save(name)

    parts = ff // d
    order = [K.g] + [K.wdown, K.slope] * parts + [K.na, K.nb, K.gb]
    return run_kernel("back_up", t, ins, outs, scratch, run, order, sliced=keyed(gb=(lambda s, z, q: q * m, m)),
                      cut=keyed(wdown=(0, parts), slope=(1, parts)))


def kernel_back_out(t, ins, rows, d, ff):
    sh = shapes_for(rows, d, ff, 1)
    outs = sub(sh, K.mid, K.gab, K.ga, K.small)
    scratch = {**sub(sh, K.g, K.gpre, K.wup, K.xh2, K.rs2, K.wout, K.gn), **outs}

    def run(c, ready, save):
        c[K.small][...] = jnp.zeros_like(c[K.small])
        back_norm_two(c, rows, ready, save, parts)
        save(K.mid, K.small)
        back_attended(c, ready, save)

    parts = 3
    order = [K.gpre, K.wup] * parts + [K.xh2, K.rs2, K.g, K.wout]
    return run_kernel("back_out", t, ins, outs, scratch, run, order, cut=keyed(gpre=(1, parts), wup=(1, parts)))


def kernel_back_att(t, ins, rows, d, ff):
    sh = shapes_for(rows, d, ff, 1)
    n = d // N_SEQ
    r = n // 2 // N_Z
    width = -(-n // 128) * 128
    outs = sub(sh, K.gproj)
    outs.update(keyed(keep=((N_Z, r, 4 * d), BF), send=((N_Z, r, 4 * d), BF)))
    scratch = {**sub(sh, K.ga, K.q, K.k, K.v, K.il, K.att, K.p, K.ek, K.ev, K.gab), **outs}
    scratch.update(keyed(xo=((rows, width), BF), xob=((rows, width), BF), xq=((rows, width), BF), xqb=((rows, width), BF),
                   gabb=((rows, d), BF), gprojb=((rows, 3 * d), BF), terms=((2 * N_Z, r, 4 * d), BF)))
    del scratch[K.keep], scratch[K.send]

    def run(c, ready, save):
        s, _, q = my_place()
        odd = (q & 1) == 1

        def part(name):
            ready(name)
            x = c[name][...]
            return jnp.where(odd, x[:, width - n :], x[:, :n])

        c[K.send] = c[K.terms].at[pl.ds((1 - s) * N_Z, N_Z)]
        c[K.keep] = c[K.terms].at[pl.ds(s * N_Z, N_Z)]
        back_heads(c, 1, rows, True, ready, save)
        xo, xq = (part(K.xo), part(K.xob)), (part(K.xq), part(K.xqb))
        ready(K.gab, K.gabb, K.gprojb)
        y = weight_term(xo[0], c[K.gab][...], xo[1], c[K.gabb][...])
        for j in range(2 * N_Z):
            c[K.terms][j, :, 0:d] = y[j * r : (j + 1) * r]
        for k in range(3):
            at = slice(k * d, (k + 1) * d)
            y = weight_term(xq[0], c[K.gproj][:, at], xq[1], c[K.gprojb][:, at])
            for j in range(2 * N_Z):
                c[K.terms][j, :, (k + 1) * d : (k + 2) * d] = y[j * r : (j + 1) * r]
        save(K.send, K.keep)

    window = (lambda s, z, q: ((q * n) >> 7) << 7, width)
    order = [K.ga, K.q, K.k, K.v, K.il, K.att, K.p, K.ek, K.ev, K.xo, K.xob, K.gab, K.gabb, K.xq, K.xqb, K.gprojb]
    return run_kernel("back_attention", t, ins, outs, scratch, run, order,
                      sliced={x: window for x in (K.xo, K.xob, K.xq, K.xqb)})


def kernel_back_in(t, ins, rows, d, ff):
    sh = shapes_for(rows, d, ff, 1)
    outs = sub(sh, K.gc, K.small)
    scratch = {**sub(sh, K.mid, K.gproj, K.wqkv, K.xh1, K.rs1, K.gn), **outs}

    def run(c, ready, save):
        c[K.small][...] = jnp.zeros_like(c[K.small])
        back_norm_one(c, rows, R_PE, ready, save)
        save(K.small)

    order = [K.gproj, K.wqkv, K.mid, K.xh1, K.rs1]
    return run_kernel("back_in", t, ins, outs, scratch, run, order)


def small_call(name, kernel, t, ins, outs, scratch=(), aliases=None, out_specs=None, in_specs=None, cost=BRIEF, grid=()):
    def run(*refs):
        kernel(*refs[: len(ins)], *refs[len(ins) + 1 : len(ins) + 1 + len(outs)], *refs[len(ins) + len(outs) + 2 :])

    call = pl.pallas_call(
        run,
        out_shape=[jax.ShapeDtypeStruct(*s) for s in outs] + [jax.ShapeDtypeStruct(t.shape, t.dtype)],
        in_specs=(in_specs or [VM] * len(ins)) + [ANY],
        out_specs=(out_specs or [VM] * len(outs)) + [ANY],
        scratch_shapes=list(scratch),
        grid=grid,
        input_output_aliases={**(aliases or {}), len(ins): len(outs)},
        compiler_params=pltpu.CompilerParams(vmem_limit_bytes=40 * 1024 * 1024),
        cost_estimate=cost,
        name=name,
    )
    *result, t = call(*ins, t)
    return result, t


def core_sum(t, keep, got):
    shard = keep.shape[1:]

    def kernel(keep, got, own, *sends):
        z = lax.axis_index("dp")
        own[...] = keep[z].astype(F32) + got[z].astype(F32)
        for k, out in enumerate(sends):
            to = (z + k + 1) & (N_Z - 1)
            out[...] = (keep[to].astype(F32) + got[to].astype(F32)).astype(BF)

    return small_call("core_sum", kernel, t, [keep, got], [(shard, F32)] + [(shard, BF)] * (N_Z - 1))


def z_sum(t, own, parts, cost):
    def kernel(own, *refs):
        *parts, out = refs
        total = own[...]
        for part in parts:
            total = total + part[...].astype(F32)
        out[...] = total.astype(BF)

    return small_call("z_sum", kernel, t, [own] + parts, [(own.shape, BF)], cost=cost)


def core_half(t, keep, got):
    shard = keep.shape[1:]

    def kernel(keep, got, own, send):
        z = lax.axis_index("dp")
        for i in range(2):
            own[i] = keep[z ^ (2 * i)].astype(F32) + got[z ^ (2 * i)].astype(F32)
            other = z ^ (2 * i + 1)
            send[i] = (keep[other].astype(F32) + got[other].astype(F32)).astype(BF)

    return small_call("core_half", kernel, t, [keep, got], [((2,) + shard, F32), ((2,) + shard, BF)])


def pair_sum(t, own, got):
    shard = own.shape[1:]

    def kernel(own, got, keep, send):
        keep[...] = own[0] + got[0].astype(F32)
        send[...] = (own[1] + got[1].astype(F32)).astype(BF)

    return small_call("pair_sum", kernel, t, [own, got], [(shard, F32), (shard, BF)])


def z_place(t, parts):
    def kernel(*refs):
        *parts, out = refs
        z = lax.axis_index("dp")
        for i, part in enumerate(parts):
            out[z ^ i] = part[...]

    return small_call("z_place", kernel, t, parts, [((N_Z,) + parts[0].shape, BF)])


def collect(t, pieces):
    def kernel(*refs):
        *pieces, out = refs
        s, _, q = my_place()
        for piece, src in zip(pieces, piece_sources(s, q)):
            out[src] = piece[...]

    (out,), t = small_call("collect", kernel, t, pieces, [((N_SEQ,) + pieces[0].shape, BF)])
    return out, t


def write_all(t, mine, other, side_by_side):
    nq, nz, r, width = mine.shape
    rows = nz * r

    def kernel(mine, other, out):
        s = lax.axis_index("section")
        for x, side in ((mine, s), (other, 1 - s)):
            for j in range(nz):
                at = slice(j * r, (j + 1) * r)
                if side_by_side:
                    out[side, at] = x[0, j].astype(F32)
                else:
                    out[0, side, at] = x[0, j].astype(F32)

    if side_by_side:
        shape, spec = (2, rows, nq * width), pl.BlockSpec((2, rows, width), lambda q: (0, 0, q))
    else:
        shape, spec = (nq, 2, rows, width), pl.BlockSpec((1, 2, rows, width), lambda q: (q, 0, 0, 0))
    (out,), t = small_call(
        "write_all", kernel, t, [mine, other], [(shape, F32)], grid=(nq,), out_specs=[spec],
        in_specs=[pl.BlockSpec((1, nz, r, width), lambda q: (q, 0, 0, 0))] * 2,
    )
    return out.reshape(-1, shape[-1]), t


def write_out(t, which, mine, other, layout, arrays, old):
    shards, r, width = mine[0].shape
    rows, count = shards * r, len(which)

    def kernel(*refs):
        mine, other, refs = refs[:count], refs[count : 2 * count], refs[2 * count + len(old) :]
        outs, (stage, sems) = refs[: len(arrays)], refs[len(arrays) :]
        s, _, q = my_place()
        copies = []
        for i in range(2 * count):
            x, side = (mine[i], s) if i < count else (other[i - count], 1 - s)
            for j in range(shards):
                stage[i, j * r : (j + 1) * r, :] = x[j].astype(F32)
            src = piece_sources(side, q)[which[i % count]]
            for n, (index, first_row, col, first, wide) in enumerate(layout(src, side)):
                dst = outs[index].at[pl.ds(first_row, rows), col if isinstance(col, pl.Slice) else pl.ds(col, wide)]
                copy = pltpu.make_async_copy(stage.at[i, :, first : first + wide], dst, sems.at[i, n])
                copy.start()
                copies.append(copy)
        for copy in copies:
            copy.wait()

    return small_call(
        "write_out", kernel, t, mine + other + old, [(a, F32) for a in arrays],
        scratch=[pltpu.VMEM((2 * count, rows, width), F32), pltpu.SemaphoreType.DMA((2 * count, 2))],
        aliases={2 * count + i: i for i in range(len(old))},
        in_specs=[VM] * (2 * count) + [ANY] * len(old), out_specs=[ANY] * len(arrays),
    )


def shift_z(x, by):
    size = lax.axis_size("dp")
    return lax.ppermute(x, "dp", [(i, (i + by) % size) for i in range(size)])


def flip_z(x, by):
    return lax.ppermute(x, "dp", [(i, i ^ by) for i in range(lax.axis_size("dp"))])


def relay(t, x, cost=BRIEF):
    def kernel(x, out):
        pass

    specs = dict(aliases={0: 0}, in_specs=[ANY], out_specs=[ANY])
    (x,), t = small_call("relay", kernel, t, [x], [(x.shape, x.dtype)], cost=cost, **specs)
    return x, t


def pick_rows(t, pairs, local):
    outs = [((local, a.shape[1]), kind) for a, _, kind in pairs for _ in range(2)]

    def kernel(*refs):
        n = 2 * len(pairs)
        ins, outs, stage, sems = refs[:n], refs[n : 2 * n], refs[2 * n : -1], refs[-1]
        s, _, q = my_place()
        copies = []
        for i, x in enumerate(ins):
            copies.append(pltpu.make_async_copy(x.at[cols(q, local)], stage[i], sems.at[i]))
            copies[-1].start()
        for copy in copies:
            copy.wait()
        for i in range(len(pairs)):
            first, second = (stage[2 * i + k][...].astype(F32) for k in range(2))
            outs[2 * i][...] = jnp.where(s == 0, first, second).astype(outs[2 * i].dtype)
            outs[2 * i + 1][...] = jnp.where(s == 0, second, first).astype(outs[2 * i].dtype)

    ins = [x for a, b, _ in pairs for x in (a, b)]
    scratch = [pltpu.VMEM((local, x.shape[1]), x.dtype) for x in ins] + [pltpu.SemaphoreType.DMA((len(ins),))]

    result, t = small_call("pick_rows", kernel, t, ins, outs, scratch=scratch, in_specs=[ANY] * len(ins))
    return result[::2], result[1::2], t


def add_small(t, parts):
    def kernel(*refs):
        *parts, out = refs
        total = parts[0][...]
        for part in parts[1:]:
            total = total + part[...]
        out[...] = total

    (total,), t = small_call("add_small", kernel, t, parts, [(parts[0].shape, F32)])
    return total, t


def write_rows(t, mine, got):
    def kernel(*refs):
        n = len(mine)
        s = lax.axis_index("section")
        for a, b, out in zip(refs[:n], refs[n : 2 * n], refs[2 * n :]):
            out[0, s] = a[...]
            out[0, 1 - s] = b[...]

    return small_call("write_rows", kernel, t, mine + got, [((1, 2) + x.shape, x.dtype) for x in mine])


def write_small(t, total, pe_rows, vectors, d, ff):
    def kernel(total, pe, up, *outs):
        s = lax.axis_index("section")
        pe[...] = total[pl.ds(pe_rows + s, 1), :]
        for j in range(ff // d):
            up[j * d : (j + 1) * d] = total[R_UB + j]
        for at, out in zip(vectors, outs):
            out[...] = total[at]

    return small_call("write_small", kernel, t, [total], [((1, d), F32), ((ff,), F32)] + [((d,), F32)] * len(vectors))


class Sum:
    def __init__(self, term):
        self.keep, self.got = term[K.keep], swap_core(term[K.send])
        self.out = []

    def cores(self, t):
        (self.own, *sends), t = core_sum(t, self.keep, self.got)
        self.parts = [shift_z(x, k + 1) for k, x in enumerate(sends)]
        return t

    def cores_half(self, t):
        (self.own, send), t = core_half(t, self.keep, self.got)
        self.got = flip_z(send, 1)
        return t

    def pairs(self, t):
        (self.own, send), t = pair_sum(t, self.own, self.got)
        self.parts = [flip_z(send, 2)]
        return t

    def total(self, t, cost=BRIEF):
        (total,), t = z_sum(t, self.own, self.parts, cost)
        self.parts = [total, flip_z(total, 1), flip_z(total, 2)]
        return t

    def total_on(self, t):
        self.parts[2], t = relay(t, self.parts[2])
        self.parts.append(flip_z(self.parts[2], 1))
        return t

    def spread(self, t):
        (block,), t = z_place(t, self.parts)
        self.pieces = [block, seq_exchange(block, 0), seq_exchange(block, 1)]
        return t

    def spread_on(self, t):
        self.pieces[1], t = relay(t, self.pieces[1])
        self.pieces[2], t = relay(t, self.pieces[2])
        self.pieces.append(seq_exchange(self.pieces[1], 1))
        return t

    def collect(self, t):
        self.mine, t = collect(t, self.pieces)
        self.other = swap_core(self.mine)
        return t

    def write_all(self, t, side_by_side):
        return write_all(t, self.mine, self.other, side_by_side)

    def swap(self):
        self.others = [swap_core(x) for x in self.pieces[:3]]

    def swap_on(self, t):
        self.pieces[3], t = relay(t, self.pieces[3])
        self.others.append(swap_core(self.pieces[3]))
        return t

    def write(self, t, which, layout, arrays):
        mine, other = [self.pieces[i] for i in which], [self.others[i] for i in which]
        self.out, t = write_out(t, which, mine, other, layout, arrays, self.out)
        return t


def fast_body(
    tokens, segment_ids, cotangent, norm_one_gain, norm_one_bias, qkv_weight, query_bias, value_bias,
    out_weight, out_bias, norm_two_gain, norm_two_bias, up_weight, up_bias, down_weight, down_bias,
    pass_embed,
):
    s = lax.axis_index("section").astype(jnp.uint32)
    local, d = tokens.shape[1], tokens.shape[2]
    rows, ff = segment_ids.shape[1], up_weight.shape[1]
    tok = seq_pieces_at_once(pick(tokens, s))
    cot = seq_pieces_at_once(pick(cotangent, s))
    vec = keyed(g1=norm_one_gain, b1=norm_one_bias, ob=out_bias, g2=norm_two_gain, b2=norm_two_bias, db=down_bias,
               qb=query_bias, vb=value_bias, ub=up_bias, pe=pass_embed, seg=segment_ids)
    w = keyed(wqkv=qkv_weight, wout=out_weight, wup=up_weight, wdown=down_weight)
    sizes = (rows, d, ff)

    def some(source, *names):
        return {n: source[n] for n in names}

    one, t = kernel_first(None, {**keyed(h=tok), **vec, **w}, *sizes)
    two, t = kernel_second(
        t, {**keyed(h=one[K.out], g=cot, kx=one[K.k], vx=one[K.v], acta=one[K.act]), **vec, **w}, *sizes
    )

    def side_layout(src, side):
        first = pl.multiple_of(src * (d // N_SEQ) + side * (d // N_SEQ // 2), 8)
        return [(0, first, 0, 0, d), (1, first, 0, d, 3 * d)]

    down = Sum(two)
    t = down.cores(t)
    hid, t = kernel_back_up(
        t, keyed(g=two[K.gh], slope=one[K.slope], wdown=down_weight, na=one[K.n2], nb=two[K.n2], gb=two[K.gpre]), *sizes
    )
    up = Sum(hid)
    t = down.total(t, LONG)
    t = up.cores_half(t)
    mid, t = kernel_back_out(
        t,
        {**keyed(g=two[K.gh], gpre=hid[K.gpre], wup=up_weight, wout=out_weight), **some(vec, K.g2), **some(one, K.xh2, K.rs2)},
        *sizes,
    )
    t = down.total_on(t)
    t = up.pairs(t)
    att, t = kernel_back_att(
        t,
        {**keyed(ga=mid[K.ga], gab=mid[K.gab], xo=one[K.att], xob=two[K.att], xq=one[K.normed], xqb=two[K.normed],
                gabb=two[K.gab], gprojb=two[K.gproj]),
         **some(two, K.ek, K.ev), **some(one, K.q, K.k, K.v, K.il, K.att, K.p)},
        *sizes,
    )
    side = Sum(att)
    t = up.total(t)
    t = down.spread(t)
    side.keep, t = relay(t, side.keep, LONG)
    t = side.cores_half(t)
    last, t = kernel_back_in(
        t,
        {**keyed(wqkv=qkv_weight), **some(vec, K.g1), **some(mid, K.mid), **some(att, K.gproj), **some(one, K.xh1, K.rs1)},
        *sizes,
    )
    t = up.total_on(t)
    t = side.pairs(t)
    t = down.spread_on(t)
    t = up.spread(t)
    t = side.total(t)
    t = down.collect(t)
    t = side.total_on(t)
    d_down, t = down.write_all(t, False)
    t = side.spread(t)
    t = up.spread_on(t)
    small, t = add_small(t, [two[K.small], hid[K.small], mid[K.small], last[K.small]])
    small = reduce_small(small)
    pairs = [(one[K.out], two[K.out], BF), (last[K.gc], two[K.gh], F32)]
    mine, send, t = pick_rows(t, pairs, local)
    got = [swap_core(x) for x in send]
    (layer_out, grad_flow), t = write_rows(t, mine, got)
    vectors = (R_G1, R_B1, R_QB, R_VB, R_OB, R_G2, R_B2, R_DB)
    (grad_pe, up_b, *sums), t = write_small(t, small, R_PE, vectors, d, ff)
    g1, b1, qb, vb, ob, g2, b2, db = sums
    t = side.spread_on(t)
    side.swap()
    t = up.collect(t)
    d_up, t = up.write_all(t, True)
    t = side.write(t, (0, 1, 2), side_layout, [(d, d), (d, 3 * d)])
    t = side.swap_on(t)
    t = side.write(t, (3,), side_layout, [(d, d), (d, 3 * d)])
    d_out, d_qkv = side.out
    return layer_out, grad_flow, g1, b1, d_qkv, qb, vb, d_out, ob, g2, b2, d_up, up_b, d_down, db, grad_pe


def body(*args):
    tokens, segment_ids = args[0], args[1]
    rows, d, ff = segment_ids.shape[1], tokens.shape[2], args[12].shape[1]
    fits = rows <= 512 and rows % AB == 0 and d % 128 == 0 and ff % d == 0 and tokens.shape[0] == 2
    fits = fits and (lax.axis_size("section"), lax.axis_size("dp"), lax.axis_size("seq")) == (2, N_Z, N_SEQ)
    return (fast_body if fits else split_body)(*args)


def solution(mesh):
    split = P("dp", "seq", None)
    placed = (split, P("dp", None), split) + (P(),) * 14
    outs = (P("section", "dp", "seq", None),) * 2 + (P(),) * 13 + (P("section", None),)
    return jax.shard_map(body, mesh=mesh, in_specs=placed, out_specs=outs, check_vma=False)
```

```python
import jax
import jax.numpy as jnp
from jax import lax
from jax.experimental import pallas as pl
from jax.experimental.pallas import tpu as pltpu
from jax.sharding import PartitionSpec as P

HD = 64
EPS = 1e-05
SCALE = 0.125
FLOOR = -1e30
BF = jnp.bfloat16
F32 = jnp.float32


class K:
    (
        act, acta, actb, activated, att, attended, attended_low, b1, b2, bias, combined, db, down_bias, down_weight,
        ek, embed_row, ev, fetch, g, g1, g2, ga, gab, gabb, gb, gc, gh, gn, gpre, gproj, gprojb, h, hidden_pre, il, k,
        keep, kx, log_total, mid, middle, n2, na, nb, norm_one_bias, norm_one_gain, norm_two_bias, norm_two_gain,
        normed, normed_two, ob, out, out_bias, out_weight, p, part, pe, q, qb, qkv_weight, query_bias, query_heads,
        rs1, rs2, seg, segc, send, slope, small, stacked, terms, ub, ubr, up_bias, up_weight, v, value_bias, vb, vx,
        wdown, wout, wqkv, wup, xh1, xh2, xo, xob, xq, xqb,
    ) = range(88)


def keyed(**arrays):
    return {getattr(K, name): array for name, array in arrays.items()}


def pick(x, index, axis=0):
    return lax.dynamic_index_in_dim(x, index, axis, keepdims=False)


def swap_core(x):
    return lax.ppermute(x, "section", [(0, 1), (1, 0)])


def seq_exchange(x, step):
    count = lax.axis_size("seq")
    route = []
    for sec in range(2):
        flip = 1 << (step ^ sec)
        route += [(sec * count + i, sec * count + (i ^ flip)) for i in range(count)]
    return lax.ppermute(x, ("section", "seq"), route)


def seq_pieces(block):
    first = seq_exchange(block, 0)
    return [block, first, seq_exchange(block, 1), seq_exchange(first, 1)]


def reduce_small(vec):
    vec = vec + swap_core(vec)
    size = lax.axis_size("dp")
    flip = 1
    while flip < size:
        vec = vec + lax.ppermute(vec, "dp", [(i, i ^ flip) for i in range(size)])
        flip *= 2
    return vec


H = 12


epsilon = 1e-05
score_scale = 0.125
floor_value = -1e30


def for_sending(x):
    return jax.tree.map(lambda a: a.astype(jnp.bfloat16) if a.dtype == jnp.float32 else a, x)


def from_behind(x, axis, by):
    size = lax.axis_size(axis)
    return lax.ppermute(x, axis, [(i, (i + by) % size) for i in range(size)])


def shifted_2(block, axis, distance):
    devices = range(lax.axis_size(axis))
    route = [(i - distance, i) for i in devices if i - distance in devices]
    return lax.ppermute(block, axis, route)


def layer_norm(values_in, gain_row, offset):
    center = jnp.mean(values_in, axis=-1, keepdims=True)
    shifted = values_in - center
    spread = jnp.mean(shifted * shifted, axis=-1, keepdims=True)
    return shifted * lax.rsqrt(spread + epsilon) * gain_row + offset


def gelu_exact(inputs):
    return jax.nn.gelu(inputs, approximate=False)


def split_heads(rows_in, head_count):
    return rows_in.reshape(rows_in.shape[0], head_count, rows_in.shape[1] // head_count)


def mask_for(seg_all, cycle_place, row_count):
    pos_keys = jnp.arange(seg_all.shape[0], dtype=jnp.int32)
    query_pos = lax.dynamic_slice_in_dim(pos_keys, cycle_place * row_count, row_count, 0)
    query_seg = lax.dynamic_slice_in_dim(seg_all, cycle_place * row_count, row_count, 0)
    return (query_seg, query_pos, seg_all, pos_keys)


def allowed_pairs(mask_info, first_row, piece_rows):
    query_seg, query_pos, seg_keys, pos_keys = mask_info
    key_pos = lax.dynamic_slice_in_dim(pos_keys, first_row, piece_rows, 0)
    key_seg = lax.dynamic_slice_in_dim(seg_keys, first_row, piece_rows, 0)
    allowed = (key_seg[None, :] == query_seg[:, None]) & (key_pos[None, :] <= query_pos[:, None])
    return allowed[None]


def score_block(queries, key_rows, allowed):
    scores = (
        jnp.einsum("qhd,khd->hqk", queries, key_rows, preferred_element_type=jnp.float32)
        * score_scale
    )
    return jnp.where(allowed, scores, floor_value)


def absorb(running, queries, key_rows, value_rows, allowed):
    row_max, row_sum, weighted = running
    scores = score_block(queries, key_rows, allowed)
    new_max = jnp.maximum(row_max, jnp.max(scores, axis=-1))
    weights = jnp.where(allowed, jnp.exp(scores - new_max[:, :, None]), 0.0)
    factor = jnp.exp(row_max - new_max)
    row_sum = row_sum * factor + jnp.sum(weights, axis=-1)
    update = jnp.einsum(
        "hqk,khd->qhd", weights.astype(jnp.bfloat16), value_rows, preferred_element_type=jnp.float32
    )
    weighted = weighted * jnp.transpose(factor)[:, :, None] + update
    return (new_max, row_sum, weighted)


def absorb_live(running, queries, key_rows, value_rows, allowed, active):
    active = active & jnp.any(allowed)
    return lax.cond(
        active,
        lambda state_in: absorb(state_in, queries, key_rows, value_rows, allowed),
        lambda state_in: state_in,
        running,
    )


def attend_forward(queries, stacked, mask_info, second, head_count):
    row_count = queries.shape[0]
    initial = (
        jnp.full((head_count, row_count), floor_value, jnp.float32),
        jnp.zeros((head_count, row_count), jnp.float32),
        jnp.zeros(queries.shape, jnp.float32),
    )
    always = jnp.array(True)
    running = initial
    key_piece = lax.all_gather(for_sending(stacked), "seq", axis=1, tiled=True)
    allowed = allowed_pairs(mask_info, jnp.int32(0), key_piece.shape[1])
    running = absorb_live(
        running,
        queries,
        split_heads(key_piece[0], head_count),
        split_heads(key_piece[1], head_count),
        allowed,
        always,
    )
    row_max, row_sum, weighted = absorb_live(
        running,
        queries,
        split_heads(key_piece[2], head_count),
        split_heads(key_piece[3], head_count),
        allowed,
        second,
    )
    attended = weighted / jnp.transpose(row_sum)[:, :, None]
    return (attended, row_max + jnp.log(row_sum))


def block_grads(queries, grad_heads, log_total, row_dot, key_rows, value_rows, allowed):
    scores = score_block(queries, key_rows, allowed)
    probabilities = jnp.exp(scores - log_total[:, :, None])
    grad_probs = jnp.einsum(
        "qhd,khd->hqk", grad_heads, value_rows, preferred_element_type=jnp.float32
    )
    grad_scores = (probabilities * (grad_probs - row_dot[:, :, None])).astype(jnp.bfloat16)
    grad_q = (
        jnp.einsum("hqk,khd->qhd", grad_scores, key_rows, preferred_element_type=jnp.float32)
        * score_scale
    )
    grad_k = (
        jnp.einsum("hqk,qhd->khd", grad_scores, queries, preferred_element_type=jnp.float32)
        * score_scale
    )
    grad_v = jnp.einsum(
        "hqk,qhd->khd",
        probabilities.astype(jnp.bfloat16),
        grad_heads,
        preferred_element_type=jnp.float32,
    )
    return (grad_q, grad_k, grad_v)


def grads_live(queries, grad_heads, log_total, row_dot, key_rows, value_rows, allowed, active):
    active = active & jnp.any(allowed)
    zero_grads = (
        jnp.zeros(queries.shape, jnp.float32),
        jnp.zeros(key_rows.shape, jnp.float32),
        jnp.zeros(key_rows.shape, jnp.float32),
    )
    return lax.cond(
        active,
        lambda: block_grads(queries, grad_heads, log_total, row_dot, key_rows, value_rows, allowed),
        lambda: zero_grads,
    )


def attend_backward(
    queries, stacked, grad_heads, log_total, row_dot, mask_info, second, head_count
):
    row_count = stacked.shape[1]
    feature_count = stacked.shape[2]
    always = jnp.array(True)

    def contribution(key_piece, first_row):
        piece_rows = key_piece.shape[1]
        allowed = allowed_pairs(mask_info, first_row, piece_rows)
        own_terms = grads_live(
            queries,
            grad_heads,
            log_total,
            row_dot,
            split_heads(key_piece[0], head_count),
            split_heads(key_piece[1], head_count),
            allowed,
            always,
        )
        other = grads_live(
            queries,
            grad_heads,
            log_total,
            row_dot,
            split_heads(key_piece[2], head_count),
            split_heads(key_piece[3], head_count),
            allowed,
            second,
        )
        key_terms = jnp.stack([own_terms[1], own_terms[2], other[1], other[2]]).reshape(
            4, piece_rows, feature_count
        )
        return (own_terms[0] + other[0], key_terms)

    cycle_size = lax.axis_size("seq")
    cycle_place = lax.axis_index("seq")

    def cycle_turn(turn_index, cycle_state):
        moving, gathered, grad_q = cycle_state
        first_row = (cycle_place + turn_index) % cycle_size * row_count
        part_q, key_terms = contribution(moving, first_row)
        moving = jax.tree.map(
            lambda part, own: part.astype(own.dtype),
            from_behind(for_sending(moving), "seq", -1),
            moving,
        )
        gathered = from_behind(gathered + key_terms, "seq", -1)
        return (moving, gathered, grad_q + part_q)

    initial = (
        stacked,
        jnp.zeros(stacked.shape, jnp.float32),
        jnp.zeros(queries.shape, jnp.float32),
    )
    finished = lax.fori_loop(0, cycle_size, cycle_turn, initial)
    return (finished[2], finished[1])


def layer_forward(hidden_in, extra_rows, params, mask_info, second, head_count):
    row_count, feature_count = hidden_in.shape
    combined = hidden_in + params[K.embed_row]
    normed = layer_norm(combined, params[K.norm_one_gain], params[K.norm_one_bias]).astype(
        jnp.bfloat16
    )
    projected = jnp.dot(normed, params[K.qkv_weight], preferred_element_type=jnp.float32)
    queries = (projected[:, :feature_count] + params[K.query_bias]).astype(jnp.bfloat16)
    key_rows = projected[:, feature_count : 2 * feature_count].astype(jnp.bfloat16)
    value_rows = (projected[:, 2 * feature_count :] + params[K.value_bias]).astype(jnp.bfloat16)
    stacked = jnp.concatenate([jnp.stack([key_rows, value_rows]), extra_rows], axis=0)
    query_heads = split_heads(queries, head_count)
    attended, log_total = attend_forward(query_heads, stacked, mask_info, second, head_count)
    attended_low = attended.reshape(row_count, feature_count).astype(jnp.bfloat16)
    middle = (
        combined
        + jnp.dot(attended_low, params[K.out_weight], preferred_element_type=jnp.float32)
        + params[K.out_bias]
    )
    normed_two = layer_norm(middle, params[K.norm_two_gain], params[K.norm_two_bias]).astype(
        jnp.bfloat16
    )
    hidden_pre = (
        jnp.dot(normed_two, params[K.up_weight], preferred_element_type=jnp.float32)
        + params[K.up_bias]
    )
    activated = gelu_exact(hidden_pre).astype(jnp.bfloat16)
    output = (
        middle
        + jnp.dot(activated, params[K.down_weight], preferred_element_type=jnp.float32)
        + params[K.down_bias]
    )
    saved_values = keyed(
        combined=combined,
        normed=normed,
        query_heads=query_heads,
        stacked=stacked,
        attended=attended,
        log_total=log_total,
        attended_low=attended_low,
        middle=middle,
        normed_two=normed_two,
        hidden_pre=hidden_pre,
        activated=activated,
    )
    return (output, saved_values)


def layer_backward(grad_top, saved_values, extra_grads, params, mask_info, second, head_count):
    row_count, feature_count = grad_top.shape
    gradients = {}
    grad_branch = grad_top.astype(jnp.bfloat16)
    gradients[K.down_weight] = jnp.einsum(
        "tf,td->fd", saved_values[K.activated], grad_branch, preferred_element_type=jnp.float32
    )
    gradients[K.down_bias] = jnp.sum(grad_branch.astype(jnp.float32), axis=0)
    grad_activated = jnp.einsum(
        "td,fd->tf", grad_branch, params[K.down_weight], preferred_element_type=jnp.float32
    )
    grad_pre = jax.vjp(gelu_exact, saved_values[K.hidden_pre])[1](grad_activated)[0].astype(
        jnp.bfloat16
    )
    gradients[K.up_weight] = jnp.einsum(
        "td,tf->df", saved_values[K.normed_two], grad_pre, preferred_element_type=jnp.float32
    )
    gradients[K.up_bias] = jnp.sum(grad_pre.astype(jnp.float32), axis=0)
    grad_normed_two = jnp.einsum(
        "tf,df->td", grad_pre, params[K.up_weight], preferred_element_type=jnp.float32
    )
    norm_back = jax.vjp(
        layer_norm, saved_values[K.middle], params[K.norm_two_gain], params[K.norm_two_bias]
    )[1]
    grad_middle_norm, gradients[K.norm_two_gain], gradients[K.norm_two_bias] = norm_back(
        grad_normed_two
    )
    grad_middle = grad_top + grad_middle_norm
    grad_attn_branch = grad_middle.astype(jnp.bfloat16)
    gradients[K.out_weight] = jnp.einsum(
        "tc,td->cd",
        saved_values[K.attended_low],
        grad_attn_branch,
        preferred_element_type=jnp.float32,
    )
    gradients[K.out_bias] = jnp.sum(grad_attn_branch.astype(jnp.float32), axis=0)
    grad_attended = jnp.einsum(
        "td,cd->tc", grad_attn_branch, params[K.out_weight], preferred_element_type=jnp.float32
    ).astype(jnp.bfloat16)
    grad_heads = split_heads(grad_attended, head_count)
    row_dot = jnp.einsum("qhd,qhd->hq", grad_heads.astype(jnp.float32), saved_values[K.attended])
    grad_q, key_grads = attend_backward(
        saved_values[K.query_heads],
        saved_values[K.stacked],
        grad_heads,
        saved_values[K.log_total],
        row_dot,
        mask_info,
        second,
        head_count,
    )
    grad_queries = grad_q.reshape(row_count, feature_count).astype(jnp.bfloat16)
    grad_keys = (key_grads[0] + extra_grads[0]).astype(jnp.bfloat16)
    grad_values = (key_grads[1] + extra_grads[1]).astype(jnp.bfloat16)
    grad_projected = jnp.concatenate([grad_queries, grad_keys, grad_values], axis=1)
    gradients[K.qkv_weight] = jnp.einsum(
        "tc,tk->ck", saved_values[K.normed], grad_projected, preferred_element_type=jnp.float32
    )
    gradients[K.query_bias] = jnp.sum(grad_queries.astype(jnp.float32), axis=0)
    gradients[K.value_bias] = jnp.sum(grad_values.astype(jnp.float32), axis=0)
    grad_normed = jnp.einsum(
        "tk,ck->tc", grad_projected, params[K.qkv_weight], preferred_element_type=jnp.float32
    )
    first_back = jax.vjp(
        layer_norm, saved_values[K.combined], params[K.norm_one_gain], params[K.norm_one_bias]
    )[1]
    grad_combined_norm, gradients[K.norm_one_gain], gradients[K.norm_one_bias] = first_back(
        grad_normed
    )
    grad_combined = grad_middle + grad_combined_norm
    gradients[K.embed_row] = jnp.sum(grad_combined, axis=0)
    return (grad_combined, key_grads[2:], gradients)


def with_embed(base_params, pass_embed, pass_index):
    params = dict(base_params)
    params[K.embed_row] = lax.dynamic_index_in_dim(
        pass_embed, pass_index, 0, keepdims=False
    ).astype(jnp.float32)
    return params


def run_split(tokens_used, cot_used, seg_used, base_params, pass_embed, cycle_place, head_count):
    micro_count, row_count, feature_count = tokens_used.shape
    section_index = lax.axis_index("section")
    second = section_index == 1
    params = with_embed(base_params, pass_embed, section_index)
    received = jnp.zeros((3, row_count, feature_count), jnp.bfloat16)
    saved_inputs = jnp.zeros((micro_count, 3, row_count, feature_count), jnp.bfloat16)
    outputs = jnp.zeros((micro_count, row_count, feature_count), jnp.bfloat16)
    for tick_index in range(micro_count + 1):
        slot_index = tick_index - section_index
        is_valid = (slot_index >= 0) & (slot_index < micro_count)
        slot_index = jnp.clip(slot_index, 0, micro_count - 1)
        own_in = lax.dynamic_index_in_dim(tokens_used, slot_index, 0, keepdims=False)
        seg_all = lax.dynamic_index_in_dim(seg_used, slot_index, 0, keepdims=False)
        mask_info = mask_for(seg_all, cycle_place, row_count)
        hidden_in = jnp.where(second, received[0], own_in).astype(jnp.float32)
        extra_rows = jnp.where(second, received[1:], jnp.zeros_like(received[1:]))
        output, saved_values = layer_forward(
            hidden_in, extra_rows, params, mask_info, second, head_count
        )
        output_low = output.astype(jnp.bfloat16)
        current = lax.dynamic_index_in_dim(outputs, slot_index, 0, keepdims=False)
        outputs = lax.dynamic_update_index_in_dim(
            outputs, jnp.where(is_valid, output_low, current), slot_index, 0
        )
        current_in = lax.dynamic_index_in_dim(saved_inputs, slot_index, 0, keepdims=False)
        saved_inputs = lax.dynamic_update_index_in_dim(
            saved_inputs, jnp.where(is_valid, received, current_in), slot_index, 0
        )
        stacked = saved_values[K.stacked]
        received = shifted_2(
            for_sending(jnp.stack([output_low, stacked[0], stacked[1]])), "section", 1
        )
    incoming = jnp.zeros((3, row_count, feature_count), jnp.float32)
    flows = jnp.zeros((micro_count, row_count, feature_count), jnp.float32)
    totals = None
    for tick_index in range(micro_count + 1):
        slot_index = tick_index - 1 + section_index
        is_valid = (slot_index >= 0) & (slot_index < micro_count)
        slot_index = jnp.clip(slot_index, 0, micro_count - 1)
        stored = lax.dynamic_index_in_dim(saved_inputs, slot_index, 0, keepdims=False)
        own_in = lax.dynamic_index_in_dim(tokens_used, slot_index, 0, keepdims=False)
        seg_all = lax.dynamic_index_in_dim(seg_used, slot_index, 0, keepdims=False)
        mask_info = mask_for(seg_all, cycle_place, row_count)
        hidden_in = jnp.where(second, stored[0], own_in).astype(jnp.float32)
        extra_rows = jnp.where(second, stored[1:], jnp.zeros_like(stored[1:]))
        output, saved_values = layer_forward(
            hidden_in, extra_rows, params, mask_info, second, head_count
        )
        outer_grad = lax.dynamic_index_in_dim(cot_used, slot_index, 0, keepdims=False).astype(
            jnp.float32
        )
        grad_top = jnp.where(second, outer_grad, incoming[0])
        grad_in, extra_grads, gradients = layer_backward(
            grad_top, saved_values, incoming[1:], params, mask_info, second, head_count
        )
        grad_low = grad_in.astype(jnp.bfloat16).astype(jnp.float32)
        flow_value = jnp.where(second, grad_low, grad_in)
        current = lax.dynamic_index_in_dim(flows, slot_index, 0, keepdims=False)
        flows = lax.dynamic_update_index_in_dim(
            flows, jnp.where(is_valid, flow_value, current), slot_index, 0
        )
        gradients = jax.tree.map(lambda addend: jnp.where(is_valid, addend, 0.0), gradients)
        if totals is None:
            totals = gradients
        else:
            totals = jax.tree.map(lambda running, addend: running + addend, totals, gradients)
        incoming = shifted_2(jnp.concatenate([grad_low[None], extra_grads], axis=0), "section", -1)
    embed_rows = jnp.where(
        jnp.arange(2, dtype=jnp.int32)[:, None] == section_index, totals[K.embed_row][None, :], 0.0
    )
    return (outputs, flows, totals, embed_rows)


def split_body(
    tokens,
    segment_ids,
    cotangent,
    norm_one_gain,
    norm_one_bias,
    qkv_weight,
    query_bias,
    value_bias,
    out_weight,
    out_bias,
    norm_two_gain,
    norm_two_bias,
    up_weight,
    up_bias,
    down_weight,
    down_bias,
    pass_embed,
):
    head_count = H
    section_index = lax.axis_index("section")
    cycle_place = lax.axis_index("seq")
    base_params = keyed(
        norm_one_gain=norm_one_gain.astype(jnp.float32),
        norm_one_bias=norm_one_bias.astype(jnp.float32),
        qkv_weight=qkv_weight,
        query_bias=query_bias.astype(jnp.float32),
        value_bias=value_bias.astype(jnp.float32),
        out_weight=out_weight,
        out_bias=out_bias.astype(jnp.float32),
        norm_two_gain=norm_two_gain.astype(jnp.float32),
        norm_two_bias=norm_two_bias.astype(jnp.float32),
        up_weight=up_weight,
        up_bias=up_bias.astype(jnp.float32),
        down_weight=down_weight,
        down_bias=down_bias.astype(jnp.float32),
    )
    tokens_used, cot_used, seg_used = (tokens, cotangent, segment_ids)
    outputs, flows, totals, embed_rows = run_split(
        tokens_used, cot_used, seg_used, base_params, pass_embed, cycle_place, head_count
    )
    summed = lax.psum(
        (
            totals[K.norm_one_gain],
            totals[K.norm_one_bias],
            totals[K.qkv_weight],
            totals[K.query_bias],
            totals[K.value_bias],
            totals[K.out_weight],
            totals[K.out_bias],
            totals[K.norm_two_gain],
            totals[K.norm_two_bias],
            totals[K.up_weight],
            totals[K.up_bias],
            totals[K.down_weight],
            totals[K.down_bias],
            embed_rows,
        ),
        ("section", "dp", "seq"),
    )
    embed_share = lax.dynamic_slice_in_dim(summed[13], section_index, 1, 0)
    return (
        outputs[None],
        flows[None],
        summed[0],
        summed[1],
        summed[2],
        summed[3],
        summed[4],
        summed[5],
        summed[6],
        summed[7],
        summed[8],
        summed[9],
        summed[10],
        summed[11],
        summed[12],
        embed_share,
    )


QB = 128
AB = 256
ANY = pl.BlockSpec(memory_space=pl.ANY)
VM = pl.BlockSpec(memory_space=pltpu.VMEM)
SM = pl.BlockSpec(memory_space=pltpu.SMEM)
N_SEQ, N_Z = 4, 4
BRIEF = pl.CostEstimate(flops=1, bytes_accessed=1, transcendentals=0)
LONG = pl.CostEstimate(flops=40_000_000_000, bytes_accessed=1, transcendentals=0)
ORDER = ((4096, 4096), F32)
R_G1, R_B1, R_VB, R_QB, R_OB, R_G2, R_B2, R_DB, R_PE, R_UB, N_SMALL = 0, 1, 2, 3, 4, 5, 6, 7, 8, 10, 16


def kdot(a, b, ca, cb):
    return lax.dot_general(a, b, (((ca,), (cb,)), ((), ())), preferred_element_type=F32)


def cols(j, n):
    return pl.ds(pl.multiple_of(j * n, n), n)


def norm_rows(x):
    center = jnp.mean(x, axis=-1, keepdims=True)
    shifted = x - center
    spread = jnp.mean(shifted * shifted, axis=-1, keepdims=True)
    rstd = lax.rsqrt(spread + EPS)
    return shifted * rstd, rstd


def row(ref):
    return ref[...].astype(F32).reshape(1, ref.shape[0])


def my_place():
    return tuple(lax.axis_index(a) for a in ("section", "dp", "seq"))


def piece_sources(s, q):
    first = jnp.where(s == 0, 1, 2)
    return [q, q ^ first, q ^ (3 - first), q ^ 3]


def low_half(rows):
    return lax.broadcasted_iota(jnp.int32, (rows, 128), 1) < HD


def stack_heads(x, low):
    zero = jnp.zeros_like(x)
    return jnp.concatenate([jnp.where(low, x, zero), jnp.where(low, zero, x)], axis=0)


class Copies:
    def __init__(self, sems):
        self.sems, self.count = sems, 0

    def start(self, src, dst):
        copy = pltpu.make_async_copy(src, dst, self.sems.at[self.count])
        self.count += 1
        copy.start()
        return copy


def wait_all(copies):
    for copy in copies:
        copy.wait()


def pass_forward(c, ns, rows, ready, save):
    d, ff = c[K.h].shape[1], c[K.act].shape[1]
    h, s = c[K.h], lax.axis_index("section")
    g1, b1, ob, g2, b2, db, qb, vb = (row(c[n]) for n in (K.g1, K.b1, K.ob, K.g2, K.b2, K.db, K.qb, K.vb))
    em = c[K.pe][ns - 1 : ns, :].astype(F32)
    c[K.ubr][...] = row(c[K.ub])
    seg = c[K.seg][pl.ds(s, 1), :]
    c[K.segc][...] = jnp.broadcast_to(seg, (128, rows)).T
    ready(K.h)

    def ln1(b, carry):
        r = cols(b, QB)
        xh, rstd = norm_rows(h[r, :].astype(F32) + em)
        c[K.xh1][r, :] = xh
        c[K.rs1][r, :] = jnp.broadcast_to(rstd, (QB, 128))
        c[K.normed][r, :] = (xh * g1 + b1).astype(BF)
        same = c[K.segc][r, 0:1] == seg
        query = lax.broadcasted_iota(jnp.int32, (QB, rows), 0) + b * QB
        key = lax.broadcasted_iota(jnp.int32, (QB, rows), 1)
        c[K.bias][r, :] = jnp.where(same & (key <= query), 0.0, FLOOR)
        return carry

    lax.fori_loop(0, rows // QB, ln1, 0)
    save(K.normed, K.xh1, K.rs1)
    ready(K.wqkv)
    normed = c[K.normed]
    c[K.part](K.wqkv, 0)
    q = kdot(normed[...], c[K.wqkv][:, 0:d], 1, 0) + qb
    c[K.q][...] = q.astype(BF) * jnp.asarray(SCALE, BF)
    c[K.part](K.wqkv, 1)
    c[K.k][...] = kdot(normed[...], c[K.wqkv][:, d : 2 * d], 1, 0).astype(BF)
    c[K.part](K.wqkv, 2)
    v = kdot(normed[...], c[K.wqkv][:, 2 * d : 3 * d], 1, 0) + vb
    c[K.v][...] = v.astype(BF)
    save(K.q, K.k, K.v)
    low = low_half(AB)
    sets = [(c[K.k], c[K.v])]
    if ns == 2:
        ready(K.kx, K.vx)
        sets.append((c[K.kx], c[K.vx]))

    def pair(hp, carry):
        at = cols(hp, 128)
        for i in range(rows // AB):
            r, nk = slice(i * AB, (i + 1) * AB), (i + 1) * AB
            qs = stack_heads(c[K.q][r, at], low)
            mask = c[K.bias][r, 0:nk]
            mask = jnp.concatenate([mask, mask], axis=0)
            scores = [kdot(qs, k[0:nk, at], 1, 1) + mask for k, _ in sets]
            top = jnp.max(scores[0], axis=-1, keepdims=True)
            for x in scores[1:]:
                top = jnp.maximum(top, jnp.max(x, axis=-1, keepdims=True))
            acc = None
            for n, ((_, v), x) in enumerate(zip(sets, scores)):
                w = jnp.exp(x - top).astype(BF)
                c[K.p][i][hp, :, n * nk : (n + 1) * nk] = w
                ones = jnp.ones((nk, 128), BF)
                y = kdot(w, jnp.concatenate([v[0:nk, at], ones], axis=1), 1, 0)
                acc = y if acc is None else acc + y
            inv = 1.0 / acc[:, 128:]
            o = acc[:, :128] * inv
            c[K.att][r, at] = jnp.where(low, o[:AB], o[AB:]).astype(BF)
            c[K.il][r, at] = jnp.where(low, inv[:AB], inv[AB:])
        return carry

    lax.fori_loop(0, d // 128, pair, 0, unroll=3)
    save(K.p, K.att, K.il)
    ready(K.wout)
    c[K.mid][...] = kdot(c[K.att][...], c[K.wout][...], 1, 0) + (h[...].astype(F32) + (em + ob))

    def ln2(b, carry):
        r = cols(b, QB)
        xh, rstd = norm_rows(c[K.mid][r, :])
        c[K.xh2][r, :] = xh
        c[K.rs2][r, :] = jnp.broadcast_to(rstd, (QB, 128))
        c[K.n2][r, :] = (xh * g2 + b2).astype(BF)
        return carry

    lax.fori_loop(0, rows // QB, ln2, 0)
    save(K.n2, K.xh2, K.rs2)
    ready(K.wup)

    def up(j, carry):
        at = cols(j, d)
        x = kdot(c[K.n2][...], c[K.wup][:, at], 1, 0) + c[K.ubr][:, at]
        cdf = 0.5 + 0.5 * lax.erf(x * 0.7071067811865476)
        c[K.act][:, at] = (x * cdf).astype(BF)
        bell = jnp.exp(-0.5 * (x * x)) * 0.3989422804014327
        c[K.slope][:, at] = (cdf + x * bell).astype(BF)
        return carry

    lax.fori_loop(0, ff // d, up, 0)
    save(K.act, K.slope)
    ready(K.wdown)
    y = kdot(c[K.act][...], c[K.wdown][...], 1, 0)
    c[K.out][...] = (c[K.mid][...] + y + db).astype(BF)
    save(K.out)


def norm_back_rows(rows, g_ref, xh_ref, rs_ref, gain, put):
    d = g_ref.shape[1]

    def step(b, sums):
        r = cols(b, QB)
        g, xh = g_ref[r, :], xh_ref[r, :]
        dx = g * gain
        m1 = jnp.mean(dx, axis=-1, keepdims=True)
        m2 = jnp.mean(dx * xh, axis=-1, keepdims=True)
        rstd = jnp.concatenate([rs_ref[r, :]] * (d // 128), axis=1)
        extra = put(r, rstd * (dx - m1 - xh * m2))
        new = (jnp.sum(g * xh, 0, keepdims=True), jnp.sum(g, 0, keepdims=True)) + extra
        return tuple(a + b_ for a, b_ in zip(sums, new))

    zero = jnp.zeros((1, d), F32)
    return lax.fori_loop(0, rows // QB, step, (zero,) * 4)


def back_hidden(c, ready, save):
    d, ff = c[K.g].shape[1], c[K.gpre].shape[1]
    small = c[K.small]
    ready(K.g, K.slope, K.wdown)

    def step(j, carry):
        at = cols(j, d)
        c[K.part](K.wdown, j)
        c[K.part](K.slope, j)
        gp = kdot(c[K.g][...], c[K.wdown][at, :], 1, 1) * c[K.slope][:, at].astype(F32)
        c[K.gpre][:, at] = gp.astype(BF)
        small[pl.ds(R_UB + j, 1), :] = jnp.sum(gp, 0, keepdims=True)
        return carry

    lax.fori_loop(0, ff // d, step, 0)
    save(K.gpre)


def back_norm_two(c, rows, ready, save, parts=1):
    small = c[K.small]
    ready(K.gpre, K.wup)
    for j in range(parts):
        at = slice(j * c[K.gpre].shape[1] // parts, (j + 1) * c[K.gpre].shape[1] // parts)
        c[K.part](K.gpre, j)
        c[K.part](K.wup, j)
        y = kdot(c[K.gpre][:, at], c[K.wup][:, at], 1, 1)
        c[K.gn][...] = y if j == 0 else c[K.gn][...] + y

    ready(K.xh2, K.rs2, K.g)

    def put(r, x):
        g = c[K.g][r, :].astype(F32)
        gm = g + x
        c[K.mid][r, :] = gm
        gab = gm.astype(BF)
        c[K.gab][r, :] = gab
        return (jnp.sum(g, 0, keepdims=True), jnp.sum(gab.astype(F32), 0, keepdims=True))

    sums = norm_back_rows(rows, c[K.gn], c[K.xh2], c[K.rs2], row(c[K.g2]), put)
    for at, x in zip((R_G2, R_B2, R_DB, R_OB), sums):
        small[at : at + 1, :] = x
    save(K.gab)


def back_attended(c, ready, save):
    ready(K.wout)
    c[K.ga][...] = kdot(c[K.gab][...], c[K.wout][...], 1, 1).astype(BF)
    save(K.ga)


def back_heads(c, ns, rows, add, ready, save):
    d = c[K.ga].shape[1]
    low = low_half(AB)
    ready(K.ga, K.q, K.k, K.v, K.il, K.att, K.p, K.ek, K.ev)
    sets = [(c[K.k], c[K.v])] + ([(c[K.kx], c[K.vx])] if ns == 2 else [])
    nb = rows // AB

    def pair(hp, carry):
        at = cols(hp, 128)
        sums_k, sums_v = [[] for _ in sets], [[] for _ in sets]
        for i in range(nb):
            r, nk = slice(i * AB, (i + 1) * AB), (i + 1) * AB
            qs = stack_heads(c[K.q][r, at], low)
            scaled = c[K.ga][r, at].astype(F32) * c[K.il][r, at]
            gs = stack_heads(scaled.astype(BF), low)
            dots = stack_heads(scaled * c[K.att][r, at].astype(F32), low)
            dots = jnp.sum(dots, axis=-1, keepdims=True)
            qs_t, gs_t = qs.T, gs.T
            gq = None
            for n, (k, v) in enumerate(sets):
                p = c[K.p][i][hp, :, n * nk : (n + 1) * nk]
                dp = kdot(gs, v[0:nk, at], 1, 1)
                ds = (p.astype(F32) * (dp - dots)).astype(BF)
                y = kdot(ds, k[0:nk, at], 1, 0)
                gq = y if gq is None else gq + y
                for sums, left, right in ((sums_k[n], qs_t, ds), (sums_v[n], gs_t, p)):
                    part = kdot(left, right, 1, 0)
                    for j in range(i):
                        sums[j] = sums[j] + part[:, j * AB : (j + 1) * AB]
                    sums.append(part[:, i * AB :])
            gq = gq * SCALE
            c[K.gproj][r, at] = jnp.where(low, gq[:AB], gq[AB:]).astype(BF)
        at_k = pl.ds(pl.multiple_of(d + hp * 128, 128), 128)
        at_v = pl.ds(pl.multiple_of(2 * d + hp * 128, 128), 128)
        for j in range(nb):
            r = slice(j * AB, (j + 1) * AB)
            gk, gv = sums_k[0][j].T, sums_v[0][j].T
            if add:
                gk, gv = gk + c[K.ek][r, at], gv + c[K.ev][r, at]
            c[K.gproj][r, at_k] = gk.astype(BF)
            c[K.gproj][r, at_v] = gv.astype(BF)
            if ns == 2:
                c[K.ek][r, at] = sums_k[1][j].T
                c[K.ev][r, at] = sums_v[1][j].T
        return carry

    lax.fori_loop(0, d // 128, pair, 0, unroll=3)
    save(K.gproj, K.ek, K.ev)


def back_norm_one(c, rows, pe_row, ready, save):
    d = c[K.gn].shape[1]
    small = c[K.small]
    ready(K.gproj, K.wqkv)
    c[K.gn][...] = kdot(c[K.gproj][...], c[K.wqkv][...], 1, 1)

    def put(r, x):
        gc = c[K.mid][r, :] + x
        if K.gc in c:
            c[K.gc][r, :] = gc
        else:
            c[K.gh][r, :] = gc.astype(BF)
        gq = jnp.sum(c[K.gproj][r, 0:d].astype(F32), 0, keepdims=True)
        small[R_VB : R_VB + 1, :] += jnp.sum(c[K.gproj][r, 2 * d :].astype(F32), 0, keepdims=True)
        return (jnp.sum(gc, 0, keepdims=True), gq)

    ready(K.mid, K.xh1, K.rs1)
    sums = norm_back_rows(rows, c[K.gn], c[K.xh1], c[K.rs1], row(c[K.g1]), put)
    for at, x in zip((R_G1, R_B1, pe_row, R_QB), sums):
        small[at : at + 1, :] = x
    save(K.gc, K.gh)


VECTORS = (K.g1, K.b1, K.ob, K.g2, K.b2, K.db, K.qb, K.vb, K.ub, K.pe, K.seg)


def run_kernel(name, t, ins, outs, scratch, body_fn, in_order, pieces=(), sliced=None, cut=None, limit=60):
    sliced, cut = sliced or {}, cut or {}
    vmem = [n for n in ins if n in VECTORS]
    hbm = [n for n in ins if n not in vmem]
    names = vmem + hbm
    in_specs = {n: ([1] * len(ins[n]) if isinstance(ins[n], list) else 1) for n in names}

    def flat(specs):
        result = []
        for s in specs.values():
            result += s if isinstance(s, list) else [s]
        return result

    def take(refs, specs):
        result = {}
        for n, s in specs.items():
            if isinstance(s, list):
                result[n], refs = list(refs[: len(s)]), refs[len(s) :]
            else:
                result[n], refs = refs[0], refs[1:]
        return result, refs

    flat_in = flat({n: ins[n] for n in names})
    many = {n for n, s in {**outs, **scratch}.items() if isinstance(s, list)}

    makes = t is None

    def kernel(*refs):
        given, refs = take(refs, in_specs)
        target, refs = take(refs if makes else refs[1:], outs)
        c, refs = take(refs[1:], scratch)
        in_sems, out_sems = refs
        for n in vmem:
            c[n] = given[n]
        place = my_place()
        incoming, outgoing = Copies(in_sems), Copies(out_sems)
        waiting, sent, first_part, parts_sent = {}, {}, {}, {}

        def part_of(n, index):
            dim, count = cut[n]
            size = c[n].shape[dim] // count
            at = (slice(None),) * dim + (cols(index, size),)
            return pltpu.make_async_copy(given[n].at[at], c[n].at[at], in_sems.at[first_part[n] + index])

        for n in in_order:
            if n in cut:
                if n not in first_part:
                    first_part[n] = incoming.count
                    incoming.count += cut[n][1]
                    parts_sent[n] = 0
                part_of(n, parts_sent[n]).start()
                parts_sent[n] += 1
            elif n in pieces:
                block = given[n][0].shape[0]
                places = piece_sources(place[0], place[2])
                waiting[n] = [incoming.start(x, c[n].at[cols(at, block)]) for x, at in zip(given[n], places)]
            elif n in sliced:
                first, width = sliced[n]
                at = pl.ds(pl.multiple_of(first(*place), 128), width)
                waiting[n] = [incoming.start(given[n].at[:, at], c[n])]
            elif n in many:
                waiting[n] = [incoming.start(a, b) for a, b in zip(given[n], c[n])]
            else:
                waiting[n] = [incoming.start(given[n], c[n])]

        def ready(*names):
            for n in names:
                wait_all(waiting.pop(n, []))

        def fetch(n):
            first, width = sliced[n]
            at = pl.ds(pl.multiple_of(first(*place), 128), width)
            waiting[n] = [incoming.start(given[n].at[:, at], c[n])]

        def save(*names):
            for n in names:
                if n in target:
                    pairs = zip(*((x[n] if n in many else [x[n]]) for x in (c, target)))
                    sent[n] = [outgoing.start(a, b) for a, b in pairs]

        def part(n, index):
            if n in cut:
                part_of(n, index).wait()

        c[K.fetch], c[K.part] = fetch, part
        body_fn(c, ready, save)
        for n in list(waiting):
            ready(n)
        for n in sent:
            wait_all(sent[n])

    result = pl.pallas_call(
        kernel,
        out_shape=[jax.ShapeDtypeStruct(*s) for s in flat(outs)] + [jax.ShapeDtypeStruct(*ORDER)],
        in_specs=[VM] * len(vmem) + [ANY] * (len(flat_in) - len(vmem)) + [ANY] * (not makes),
        out_specs=[ANY] * (len(flat(outs)) + 1),
        scratch_shapes=[pltpu.VMEM(*s) for s in flat(scratch)]
        + [pltpu.SemaphoreType.DMA((len(flat_in) - len(vmem) + sum(k for _, k in cut.values()) + 1,)), pltpu.SemaphoreType.DMA((len(flat(outs)) + 1,))],
        input_output_aliases={} if makes else {len(flat_in): len(flat(outs))},
        compiler_params=pltpu.CompilerParams(vmem_limit_bytes=limit * 1024 * 1024),
        cost_estimate=BRIEF,
        name=name,
    )(*flat_in, *([] if makes else [t]))
    result, (t,) = take(list(result), outs)
    return result, t


def shapes_for(rows, d, ff, ns):
    low, full = lambda n: ((rows, n), BF), lambda n: ((rows, n), F32)
    p = [((d // 128, 2 * AB, ns * AB * (i + 1)), BF) for i in range(rows // AB)]
    return keyed(
        h=low(d), normed=low(d), xh1=full(d), rs1=full(128), q=low(d), k=low(d), v=low(d), kx=low(d), vx=low(d),
        p=p, att=low(d), il=full(d), mid=full(d), n2=low(d), xh2=full(d), rs2=full(128), act=low(ff),
        slope=low(ff), out=low(d), bias=full(rows), wqkv=((d, 3 * d), BF), wout=((d, d), BF),
        wup=((d, ff), BF), wdown=((ff, d), BF), g=low(d), gpre=low(ff), gn=full(d), gab=low(d), ga=low(d),
        ubr=((1, ff), F32), segc=((rows, 128), jnp.int32), gproj=low(3 * d), ek=full(d), ev=full(d), gh=low(d), gc=full(d), small=((N_SMALL, d), F32),
    )


def sub(shapes, *names):
    return {n: shapes[n] for n in names}


def weight_term(xa, ga, xb, gb):
    return (kdot(xa, ga, 0, 0) + kdot(xb, gb, 0, 0)).astype(BF)


def store_slabs(ref, y):
    for j in range(ref.shape[0]):
        ref[j] = y[j * ref.shape[1] : (j + 1) * ref.shape[1]]


def kernel_first(t, ins, rows, d, ff):
    sh = shapes_for(rows, d, ff, 1)
    outs = sub(sh, K.normed, K.xh1, K.rs1, K.q, K.k, K.v, K.p, K.att, K.il, K.n2, K.xh2, K.rs2, K.act, K.slope, K.out)
    scratch = {**sub(sh, K.wqkv, K.wout, K.wup, K.wdown, K.h, K.mid, K.bias, K.ubr, K.segc), **outs}

    def run(c, ready, save):
        pass_forward(c, 1, rows, ready, save)

    order = [K.h, K.wqkv, K.wqkv, K.wqkv, K.wout, K.wup, K.wdown]
    return run_kernel("pass_one", t, ins, outs, scratch, run, order, pieces=(K.h,), cut=keyed(wqkv=(1, 3)))


def kernel_second(t, ins, rows, d, ff):
    sh = shapes_for(rows, d, ff, 2)
    n = ff // N_SEQ // 2
    half = ((N_Z, n // N_Z, d), BF)
    outs = sub(sh, K.normed, K.att, K.n2, K.out, K.gpre, K.gab, K.gproj, K.ek, K.ev, K.gh, K.small)
    outs.update(keyed(keep=half, send=half))
    scratch = {
        **sub(sh, K.wqkv, K.wout, K.wup, K.wdown, K.h, K.mid, K.bias, K.kx, K.vx, K.xh1, K.rs1, K.q, K.k, K.v, K.p, K.il, K.xh2, K.rs2, K.slope, K.gn, K.act, K.g, K.ubr, K.segc),
        **outs,
    }
    scratch.update(keyed(actb=((rows, 2 * n), BF)))
    del scratch[K.gpre]

    def run(c, ready, save):
        s, _, q = my_place()
        c[K.small][...] = jnp.zeros_like(c[K.small])
        pass_forward(c, 2, rows, ready, save)
        c[K.actb][...] = c[K.act][:, cols(q, 2 * n)]
        c[K.gpre], c[K.ga], c[K.acta] = c[K.act], c[K.h], c[K.slope].at[:, 0 : 2 * n]
        back_hidden(c, ready, save)
        c[K.fetch](K.acta)
        back_norm_two(c, rows, ready, save)
        back_attended(c, ready, save)
        back_heads(c, 2, rows, False, ready, save)
        back_norm_one(c, rows, R_PE + 1, ready, save)
        save(K.small)
        ready(K.acta)
        for name, side in ((K.send, 1 - s), (K.keep, s)):
            at = cols(side, n)
            store_slabs(c[name], weight_term(c[K.acta][:, at], c[K.gh][...], c[K.actb][:, at], c[K.g][...]))
            save(name)

    order = [K.h, K.wqkv, K.wqkv, K.wqkv, K.kx, K.vx, K.wout, K.wup, K.wdown, K.g]
    return run_kernel("pass_two_and_back", t, ins, outs, scratch, run, order, pieces=(K.g,),
                      sliced=keyed(acta=(lambda s, z, q: q * 2 * n, 2 * n)), cut=keyed(wqkv=(1, 3)), limit=63)


def kernel_back_up(t, ins, rows, d, ff):
    sh = shapes_for(rows, d, ff, 1)
    n, m = d // 2, ff // N_SEQ
    half = ((N_Z, n // N_Z, m), BF)
    outs = sub(sh, K.gpre, K.small)
    outs.update(keyed(keep=half, send=half))
    scratch = {**sub(sh, K.g, K.slope, K.wdown), **outs, K.na: ((rows, d), BF), K.nb: ((rows, d), BF), K.gb: ((rows, m), BF)}

    def run(c, ready, save):
        s, _, q = my_place()
        c[K.small][...] = jnp.zeros_like(c[K.small])
        back_hidden(c, ready, save)
        save(K.small)
        ready(K.na, K.nb, K.gb)
        ga = c[K.gpre][:, cols(q, m)]
        for name, side in ((K.send, 1 - s), (K.keep, s)):
            at = cols(side, n)
            store_slabs(c[name], weight_term(c[K.na][:, at], ga, c[K.nb][:, at], c[K.gb][...]))
            save(name)

    parts = ff // d
    order = [K.g] + [K.wdown, K.slope] * parts + [K.na, K.nb, K.gb]
    return run_kernel("back_up", t, ins, outs, scratch, run, order, sliced=keyed(gb=(lambda s, z, q: q * m, m)),
                      cut=keyed(wdown=(0, parts), slope=(1, parts)))


def kernel_back_out(t, ins, rows, d, ff):
    sh = shapes_for(rows, d, ff, 1)
    outs = sub(sh, K.mid, K.gab, K.ga, K.small)
    scratch = {**sub(sh, K.g, K.gpre, K.wup, K.xh2, K.rs2, K.wout, K.gn), **outs}

    def run(c, ready, save):
        c[K.small][...] = jnp.zeros_like(c[K.small])
        back_norm_two(c, rows, ready, save, parts)
        save(K.mid, K.small)
        back_attended(c, ready, save)

    parts = 3
    order = [K.gpre, K.wup] * parts + [K.xh2, K.rs2, K.g, K.wout]
    return run_kernel("back_out", t, ins, outs, scratch, run, order, cut=keyed(gpre=(1, parts), wup=(1, parts)))


def kernel_back_att(t, ins, rows, d, ff):
    sh = shapes_for(rows, d, ff, 1)
    n = d // N_SEQ
    r = n // 2 // N_Z
    width = -(-n // 128) * 128
    outs = sub(sh, K.gproj)
    outs.update(keyed(keep=((N_Z, r, 4 * d), BF), send=((N_Z, r, 4 * d), BF)))
    scratch = {**sub(sh, K.ga, K.q, K.k, K.v, K.il, K.att, K.p, K.ek, K.ev, K.gab), **outs}
    scratch.update(keyed(xo=((rows, width), BF), xob=((rows, width), BF), xq=((rows, width), BF), xqb=((rows, width), BF),
                   gabb=((rows, d), BF), gprojb=((rows, 3 * d), BF), terms=((2 * N_Z, r, 4 * d), BF)))
    del scratch[K.keep], scratch[K.send]

    def run(c, ready, save):
        s, _, q = my_place()
        odd = (q & 1) == 1

        def part(name):
            ready(name)
            x = c[name][...]
            return jnp.where(odd, x[:, width - n :], x[:, :n])

        c[K.send] = c[K.terms].at[pl.ds((1 - s) * N_Z, N_Z)]
        c[K.keep] = c[K.terms].at[pl.ds(s * N_Z, N_Z)]
        back_heads(c, 1, rows, True, ready, save)
        xo, xq = (part(K.xo), part(K.xob)), (part(K.xq), part(K.xqb))
        ready(K.gab, K.gabb, K.gprojb)
        y = weight_term(xo[0], c[K.gab][...], xo[1], c[K.gabb][...])
        for j in range(2 * N_Z):
            c[K.terms][j, :, 0:d] = y[j * r : (j + 1) * r]
        for k in range(3):
            at = slice(k * d, (k + 1) * d)
            y = weight_term(xq[0], c[K.gproj][:, at], xq[1], c[K.gprojb][:, at])
            for j in range(2 * N_Z):
                c[K.terms][j, :, (k + 1) * d : (k + 2) * d] = y[j * r : (j + 1) * r]
        save(K.send, K.keep)

    window = (lambda s, z, q: ((q * n) >> 7) << 7, width)
    order = [K.ga, K.q, K.k, K.v, K.il, K.att, K.p, K.ek, K.ev, K.xo, K.xob, K.gab, K.gabb, K.xq, K.xqb, K.gprojb]
    return run_kernel("back_attention", t, ins, outs, scratch, run, order,
                      sliced={x: window for x in (K.xo, K.xob, K.xq, K.xqb)})


def kernel_back_in(t, ins, rows, d, ff):
    sh = shapes_for(rows, d, ff, 1)
    outs = sub(sh, K.gc, K.small)
    scratch = {**sub(sh, K.mid, K.gproj, K.wqkv, K.xh1, K.rs1, K.gn), **outs}

    def run(c, ready, save):
        c[K.small][...] = jnp.zeros_like(c[K.small])
        back_norm_one(c, rows, R_PE, ready, save)
        save(K.small)

    order = [K.gproj, K.wqkv, K.mid, K.xh1, K.rs1]
    return run_kernel("back_in", t, ins, outs, scratch, run, order)


def small_call(name, kernel, t, ins, outs, scratch=(), aliases=None, out_specs=None, in_specs=None, cost=BRIEF, grid=()):
    def run(*refs):
        kernel(*refs[: len(ins)], *refs[len(ins) + 1 : len(ins) + 1 + len(outs)], *refs[len(ins) + len(outs) + 2 :])

    call = pl.pallas_call(
        run,
        out_shape=[jax.ShapeDtypeStruct(*s) for s in outs] + [jax.ShapeDtypeStruct(t.shape, t.dtype)],
        in_specs=(in_specs or [VM] * len(ins)) + [ANY],
        out_specs=(out_specs or [VM] * len(outs)) + [ANY],
        scratch_shapes=list(scratch),
        grid=grid,
        input_output_aliases={**(aliases or {}), len(ins): len(outs)},
        compiler_params=pltpu.CompilerParams(vmem_limit_bytes=40 * 1024 * 1024),
        cost_estimate=cost,
        name=name,
    )
    *result, t = call(*ins, t)
    return result, t


def core_sum(t, keep, got):
    shard = keep.shape[1:]

    def kernel(keep, got, own, *sends):
        z = lax.axis_index("dp")
        own[...] = keep[z].astype(F32) + got[z].astype(F32)
        for k, out in enumerate(sends):
            to = (z + k + 1) & (N_Z - 1)
            out[...] = (keep[to].astype(F32) + got[to].astype(F32)).astype(BF)

    return small_call("core_sum", kernel, t, [keep, got], [(shard, F32)] + [(shard, BF)] * (N_Z - 1))


def z_sum(t, own, parts, cost):
    def kernel(own, *refs):
        *parts, out = refs
        total = own[...]
        for part in parts:
            total = total + part[...].astype(F32)
        out[...] = total.astype(BF)

    return small_call("z_sum", kernel, t, [own] + parts, [(own.shape, BF)], cost=cost)


def core_half(t, keep, got):
    shard = keep.shape[1:]

    def kernel(keep, got, own, send):
        z = lax.axis_index("dp")
        for i in range(2):
            own[i] = keep[z ^ (2 * i)].astype(F32) + got[z ^ (2 * i)].astype(F32)
            other = z ^ (2 * i + 1)
            send[i] = (keep[other].astype(F32) + got[other].astype(F32)).astype(BF)

    return small_call("core_half", kernel, t, [keep, got], [((2,) + shard, F32), ((2,) + shard, BF)])


def pair_sum(t, own, got):
    shard = own.shape[1:]

    def kernel(own, got, keep, send):
        keep[...] = own[0] + got[0].astype(F32)
        send[...] = (own[1] + got[1].astype(F32)).astype(BF)

    return small_call("pair_sum", kernel, t, [own, got], [(shard, F32), (shard, BF)])


def z_place(t, parts):
    def kernel(*refs):
        *parts, out = refs
        z = lax.axis_index("dp")
        for i, part in enumerate(parts):
            out[z ^ i] = part[...]

    return small_call("z_place", kernel, t, parts, [((N_Z,) + parts[0].shape, BF)])


def collect(t, pieces):
    def kernel(*refs):
        *pieces, out = refs
        s, _, q = my_place()
        for piece, src in zip(pieces, piece_sources(s, q)):
            out[src] = piece[...]

    (out,), t = small_call("collect", kernel, t, pieces, [((N_SEQ,) + pieces[0].shape, BF)])
    return out, t


def write_all(t, mine, other, side_by_side):
    nq, nz, r, width = mine.shape
    rows = nz * r

    def kernel(mine, other, out):
        s = lax.axis_index("section")
        for x, side in ((mine, s), (other, 1 - s)):
            for j in range(nz):
                at = slice(j * r, (j + 1) * r)
                if side_by_side:
                    out[side, at] = x[0, j].astype(F32)
                else:
                    out[0, side, at] = x[0, j].astype(F32)

    if side_by_side:
        shape, spec = (2, rows, nq * width), pl.BlockSpec((2, rows, width), lambda q: (0, 0, q))
    else:
        shape, spec = (nq, 2, rows, width), pl.BlockSpec((1, 2, rows, width), lambda q: (q, 0, 0, 0))
    (out,), t = small_call(
        "write_all", kernel, t, [mine, other], [(shape, F32)], grid=(nq,), out_specs=[spec],
        in_specs=[pl.BlockSpec((1, nz, r, width), lambda q: (q, 0, 0, 0))] * 2,
    )
    return out.reshape(-1, shape[-1]), t


def write_out(t, which, mine, other, layout, arrays, old):
    shards, r, width = mine[0].shape
    rows, count = shards * r, len(which)

    def kernel(*refs):
        mine, other, refs = refs[:count], refs[count : 2 * count], refs[2 * count + len(old) :]
        outs, (stage, sems) = refs[: len(arrays)], refs[len(arrays) :]
        s, _, q = my_place()
        copies = []
        for i in range(2 * count):
            x, side = (mine[i], s) if i < count else (other[i - count], 1 - s)
            for j in range(shards):
                stage[i, j * r : (j + 1) * r, :] = x[j].astype(F32)
            src = piece_sources(side, q)[which[i % count]]
            for n, (index, first_row, col, first, wide) in enumerate(layout(src, side)):
                dst = outs[index].at[pl.ds(first_row, rows), col if isinstance(col, pl.Slice) else pl.ds(col, wide)]
                copy = pltpu.make_async_copy(stage.at[i, :, first : first + wide], dst, sems.at[i, n])
                copy.start()
                copies.append(copy)
        for copy in copies:
            copy.wait()

    return small_call(
        "write_out", kernel, t, mine + other + old, [(a, F32) for a in arrays],
        scratch=[pltpu.VMEM((2 * count, rows, width), F32), pltpu.SemaphoreType.DMA((2 * count, 2))],
        aliases={2 * count + i: i for i in range(len(old))},
        in_specs=[VM] * (2 * count) + [ANY] * len(old), out_specs=[ANY] * len(arrays),
    )


def shift_z(x, by):
    size = lax.axis_size("dp")
    return lax.ppermute(x, "dp", [(i, (i + by) % size) for i in range(size)])


def flip_z(x, by):
    return lax.ppermute(x, "dp", [(i, i ^ by) for i in range(lax.axis_size("dp"))])


def relay(t, x, cost=BRIEF):
    def kernel(x, out):
        pass

    specs = dict(aliases={0: 0}, in_specs=[ANY], out_specs=[ANY])
    (x,), t = small_call("relay", kernel, t, [x], [(x.shape, x.dtype)], cost=cost, **specs)
    return x, t


def pick_rows(t, pairs, local):
    outs = [((local, a.shape[1]), kind) for a, _, kind in pairs for _ in range(2)]

    def kernel(*refs):
        n = 2 * len(pairs)
        ins, outs, stage, sems = refs[:n], refs[n : 2 * n], refs[2 * n : -1], refs[-1]
        s, _, q = my_place()
        copies = []
        for i, x in enumerate(ins):
            copies.append(pltpu.make_async_copy(x.at[cols(q, local)], stage[i], sems.at[i]))
            copies[-1].start()
        for copy in copies:
            copy.wait()
        for i in range(len(pairs)):
            first, second = (stage[2 * i + k][...].astype(F32) for k in range(2))
            outs[2 * i][...] = jnp.where(s == 0, first, second).astype(outs[2 * i].dtype)
            outs[2 * i + 1][...] = jnp.where(s == 0, second, first).astype(outs[2 * i].dtype)

    ins = [x for a, b, _ in pairs for x in (a, b)]
    scratch = [pltpu.VMEM((local, x.shape[1]), x.dtype) for x in ins] + [pltpu.SemaphoreType.DMA((len(ins),))]

    result, t = small_call("pick_rows", kernel, t, ins, outs, scratch=scratch, in_specs=[ANY] * len(ins))
    return result[::2], result[1::2], t


def add_small(t, parts):
    def kernel(*refs):
        *parts, out = refs
        total = parts[0][...]
        for part in parts[1:]:
            total = total + part[...]
        out[...] = total

    (total,), t = small_call("add_small", kernel, t, parts, [(parts[0].shape, F32)])
    return total, t


def write_rows(t, mine, got):
    def kernel(*refs):
        n = len(mine)
        s = lax.axis_index("section")
        for a, b, out in zip(refs[:n], refs[n : 2 * n], refs[2 * n :]):
            out[0, s] = a[...]
            out[0, 1 - s] = b[...]

    return small_call("write_rows", kernel, t, mine + got, [((1, 2) + x.shape, x.dtype) for x in mine])


def write_small(t, total, pe_rows, vectors, d, ff):
    def kernel(total, pe, up, *outs):
        s = lax.axis_index("section")
        pe[...] = total[pl.ds(pe_rows + s, 1), :]
        for j in range(ff // d):
            up[j * d : (j + 1) * d] = total[R_UB + j]
        for at, out in zip(vectors, outs):
            out[...] = total[at]

    return small_call("write_small", kernel, t, [total], [((1, d), F32), ((ff,), F32)] + [((d,), F32)] * len(vectors))


class Sum:
    def __init__(self, term):
        self.keep, self.got = term[K.keep], swap_core(term[K.send])
        self.out = []

    def cores(self, t):
        (self.own, *sends), t = core_sum(t, self.keep, self.got)
        self.parts = [shift_z(x, k + 1) for k, x in enumerate(sends)]
        return t

    def cores_half(self, t):
        (self.own, send), t = core_half(t, self.keep, self.got)
        self.got = flip_z(send, 1)
        return t

    def pairs(self, t):
        (self.own, send), t = pair_sum(t, self.own, self.got)
        self.parts = [flip_z(send, 2)]
        return t

    def total(self, t, cost=BRIEF):
        (total,), t = z_sum(t, self.own, self.parts, cost)
        self.parts = [total, flip_z(total, 1), flip_z(total, 2)]
        return t

    def total_on(self, t, both=False):
        self.parts[2], t = relay(t, self.parts[2])
        if both:
            self.parts[1], t = relay(t, self.parts[1])
        self.parts.append(flip_z(self.parts[2], 1))
        return t

    def spread(self, t):
        (block,), t = z_place(t, self.parts)
        self.pieces = [block, seq_exchange(block, 0), seq_exchange(block, 1)]
        return t

    def spread_on(self, t):
        self.pieces[1], t = relay(t, self.pieces[1])
        self.pieces[2], t = relay(t, self.pieces[2])
        self.pieces.append(seq_exchange(self.pieces[1], 1))
        return t

    def collect(self, t):
        self.mine, t = collect(t, self.pieces)
        self.other = swap_core(self.mine)
        return t

    def write_all(self, t, side_by_side):
        return write_all(t, self.mine, self.other, side_by_side)

    def swap(self):
        self.others = [swap_core(x) for x in self.pieces[:3]]

    def swap_on(self, t):
        self.pieces[3], t = relay(t, self.pieces[3])
        self.others.append(swap_core(self.pieces[3]))
        return t

    def write(self, t, which, layout, arrays):
        mine, other = [self.pieces[i] for i in which], [self.others[i] for i in which]
        self.out, t = write_out(t, which, mine, other, layout, arrays, self.out)
        return t


def fast_body(
    tokens, segment_ids, cotangent, norm_one_gain, norm_one_bias, qkv_weight, query_bias, value_bias,
    out_weight, out_bias, norm_two_gain, norm_two_bias, up_weight, up_bias, down_weight, down_bias,
    pass_embed,
):
    s = lax.axis_index("section").astype(jnp.uint32)
    local, d = tokens.shape[1], tokens.shape[2]
    rows, ff = segment_ids.shape[1], up_weight.shape[1]
    tok = seq_pieces(pick(tokens, s))
    cot = seq_pieces(pick(cotangent, s))
    vec = keyed(g1=norm_one_gain, b1=norm_one_bias, ob=out_bias, g2=norm_two_gain, b2=norm_two_bias, db=down_bias,
               qb=query_bias, vb=value_bias, ub=up_bias, pe=pass_embed, seg=segment_ids)
    w = keyed(wqkv=qkv_weight, wout=out_weight, wup=up_weight, wdown=down_weight)
    sizes = (rows, d, ff)

    def some(source, *names):
        return {n: source[n] for n in names}

    one, t = kernel_first(None, {**keyed(h=tok), **vec, **w}, *sizes)
    two, t = kernel_second(
        t, {**keyed(h=one[K.out], g=cot, kx=one[K.k], vx=one[K.v], acta=one[K.act]), **vec, **w}, *sizes
    )

    def side_layout(src, side):
        first = pl.multiple_of(src * (d // N_SEQ) + side * (d // N_SEQ // 2), 8)
        return [(0, first, 0, 0, d), (1, first, 0, d, 3 * d)]

    down = Sum(two)
    t = down.cores(t)
    hid, t = kernel_back_up(
        t, keyed(g=two[K.gh], slope=one[K.slope], wdown=down_weight, na=one[K.n2], nb=two[K.n2], gb=two[K.gpre]), *sizes
    )
    up = Sum(hid)
    t = down.total(t, LONG)
    t = up.cores_half(t)
    mid, t = kernel_back_out(
        t,
        {**keyed(g=two[K.gh], gpre=hid[K.gpre], wup=up_weight, wout=out_weight), **some(vec, K.g2), **some(one, K.xh2, K.rs2)},
        *sizes,
    )
    t = down.total_on(t)
    t = up.pairs(t)
    att, t = kernel_back_att(
        t,
        {**keyed(ga=mid[K.ga], gab=mid[K.gab], xo=one[K.att], xob=two[K.att], xq=one[K.normed], xqb=two[K.normed],
                gabb=two[K.gab], gprojb=two[K.gproj]),
         **some(two, K.ek, K.ev), **some(one, K.q, K.k, K.v, K.il, K.att, K.p)},
        *sizes,
    )
    side = Sum(att)
    t = up.total(t)
    t = down.spread(t)
    side.keep, t = relay(t, side.keep, LONG)
    t = side.cores_half(t)
    last, t = kernel_back_in(
        t,
        {**keyed(wqkv=qkv_weight), **some(vec, K.g1), **some(mid, K.mid), **some(att, K.gproj), **some(one, K.xh1, K.rs1)},
        *sizes,
    )
    t = up.total_on(t)
    t = side.pairs(t)
    t = down.spread_on(t)
    t = up.spread(t)
    t = side.total(t)
    t = down.collect(t)
    small, t = add_small(t, [two[K.small], hid[K.small], mid[K.small], last[K.small]])
    small = reduce_small(small)
    t = side.total_on(t)
    d_down, t = down.write_all(t, False)
    t = side.spread(t)
    t = up.spread_on(t)
    pairs = [(one[K.out], two[K.out], BF), (last[K.gc], two[K.gh], F32)]
    mine, send, t = pick_rows(t, pairs, local)
    got = [swap_core(x) for x in send]
    (layer_out, grad_flow), t = write_rows(t, mine, got)
    vectors = (R_G1, R_B1, R_QB, R_VB, R_OB, R_G2, R_B2, R_DB)
    (grad_pe, up_b, *sums), t = write_small(t, small, R_PE, vectors, d, ff)
    g1, b1, qb, vb, ob, g2, b2, db = sums
    t = side.spread_on(t)
    side.swap()
    t = up.collect(t)
    d_up, t = up.write_all(t, True)
    t = side.write(t, (0, 1, 2), side_layout, [(d, d), (d, 3 * d)])
    t = side.swap_on(t)
    t = side.write(t, (3,), side_layout, [(d, d), (d, 3 * d)])
    d_out, d_qkv = side.out
    return layer_out, grad_flow, g1, b1, d_qkv, qb, vb, d_out, ob, g2, b2, d_up, up_b, d_down, db, grad_pe


def body(*args):
    tokens, segment_ids = args[0], args[1]
    rows, d, ff = segment_ids.shape[1], tokens.shape[2], args[12].shape[1]
    fits = rows <= 512 and rows % AB == 0 and d % 128 == 0 and ff % d == 0 and tokens.shape[0] == 2
    fits = fits and (lax.axis_size("section"), lax.axis_size("dp"), lax.axis_size("seq")) == (2, N_Z, N_SEQ)
    return (fast_body if fits else split_body)(*args)


def solution(mesh):
    split = P("dp", "seq", None)
    placed = (split, P("dp", None), split) + (P(),) * 14
    outs = (P("section", "dp", "seq", None),) * 2 + (P(),) * 13 + (P("section", None),)
    return jax.shard_map(body, mesh=mesh, in_specs=placed, out_specs=outs, check_vma=False)
```

```python
import jax
import jax.numpy as jnp
from jax import lax
from jax.experimental import pallas as pl
from jax.experimental.pallas import tpu as pltpu
from jax.sharding import PartitionSpec as P

HD = 64
EPS = 1e-05
SCALE = 0.125
FLOOR = -1e30
BF = jnp.bfloat16
F32 = jnp.float32


class K:
    (
        act, acta, actb, activated, att, attended, attended_low, b1, b2, bias, combined, db, down_bias, down_weight,
        ek, embed_row, ev, fetch, g, g1, g2, ga, gab, gabb, gb, gc, gh, gn, gpre, gproj, gprojb, h, hidden_pre, il, k,
        keep, kx, log_total, mid, middle, n2, na, nb, norm_one_bias, norm_one_gain, norm_two_bias, norm_two_gain,
        normed, normed_two, ob, out, out_bias, out_weight, p, part, pe, q, qb, qkv_weight, query_bias, query_heads,
        rs1, rs2, seg, segc, send, slope, small, stacked, terms, ub, ubr, up_bias, up_weight, v, value_bias, vb, vx,
        wdown, wout, wqkv, wup, xh1, xh2, xo, xob, xq, xqb,
    ) = range(88)


def keyed(**arrays):
    return {getattr(K, name): array for name, array in arrays.items()}


def pick(x, index, axis=0):
    return lax.dynamic_index_in_dim(x, index, axis, keepdims=False)


def swap_core(x):
    return lax.ppermute(x, "section", [(0, 1), (1, 0)])


def seq_exchange(x, step):
    count = lax.axis_size("seq")
    route = []
    for sec in range(2):
        flip = 1 << (step ^ sec)
        route += [(sec * count + i, sec * count + (i ^ flip)) for i in range(count)]
    return lax.ppermute(x, ("section", "seq"), route)


def seq_pieces(block):
    first = seq_exchange(block, 0)
    return [block, first, seq_exchange(block, 1), seq_exchange(first, 1)]


def reduce_small(vec):
    vec = vec + swap_core(vec)
    size = lax.axis_size("dp")
    flip = 1
    while flip < size:
        vec = vec + lax.ppermute(vec, "dp", [(i, i ^ flip) for i in range(size)])
        flip *= 2
    return vec


H = 12


epsilon = 1e-05
score_scale = 0.125
floor_value = -1e30


def for_sending(x):
    return jax.tree.map(lambda a: a.astype(jnp.bfloat16) if a.dtype == jnp.float32 else a, x)


def from_behind(x, axis, by):
    size = lax.axis_size(axis)
    return lax.ppermute(x, axis, [(i, (i + by) % size) for i in range(size)])


def shifted_2(block, axis, distance):
    devices = range(lax.axis_size(axis))
    route = [(i - distance, i) for i in devices if i - distance in devices]
    return lax.ppermute(block, axis, route)


def layer_norm(values_in, gain_row, offset):
    center = jnp.mean(values_in, axis=-1, keepdims=True)
    shifted = values_in - center
    spread = jnp.mean(shifted * shifted, axis=-1, keepdims=True)
    return shifted * lax.rsqrt(spread + epsilon) * gain_row + offset


def gelu_exact(inputs):
    return jax.nn.gelu(inputs, approximate=False)


def split_heads(rows_in, head_count):
    return rows_in.reshape(rows_in.shape[0], head_count, rows_in.shape[1] // head_count)


def mask_for(seg_all, cycle_place, row_count):
    pos_keys = jnp.arange(seg_all.shape[0], dtype=jnp.int32)
    query_pos = lax.dynamic_slice_in_dim(pos_keys, cycle_place * row_count, row_count, 0)
    query_seg = lax.dynamic_slice_in_dim(seg_all, cycle_place * row_count, row_count, 0)
    return (query_seg, query_pos, seg_all, pos_keys)


def allowed_pairs(mask_info, first_row, piece_rows):
    query_seg, query_pos, seg_keys, pos_keys = mask_info
    key_pos = lax.dynamic_slice_in_dim(pos_keys, first_row, piece_rows, 0)
    key_seg = lax.dynamic_slice_in_dim(seg_keys, first_row, piece_rows, 0)
    allowed = (key_seg[None, :] == query_seg[:, None]) & (key_pos[None, :] <= query_pos[:, None])
    return allowed[None]


def score_block(queries, key_rows, allowed):
    scores = (
        jnp.einsum("qhd,khd->hqk", queries, key_rows, preferred_element_type=jnp.float32)
        * score_scale
    )
    return jnp.where(allowed, scores, floor_value)


def absorb(running, queries, key_rows, value_rows, allowed):
    row_max, row_sum, weighted = running
    scores = score_block(queries, key_rows, allowed)
    new_max = jnp.maximum(row_max, jnp.max(scores, axis=-1))
    weights = jnp.where(allowed, jnp.exp(scores - new_max[:, :, None]), 0.0)
    factor = jnp.exp(row_max - new_max)
    row_sum = row_sum * factor + jnp.sum(weights, axis=-1)
    update = jnp.einsum(
        "hqk,khd->qhd", weights.astype(jnp.bfloat16), value_rows, preferred_element_type=jnp.float32
    )
    weighted = weighted * jnp.transpose(factor)[:, :, None] + update
    return (new_max, row_sum, weighted)


def absorb_live(running, queries, key_rows, value_rows, allowed, active):
    active = active & jnp.any(allowed)
    return lax.cond(
        active,
        lambda state_in: absorb(state_in, queries, key_rows, value_rows, allowed),
        lambda state_in: state_in,
        running,
    )


def attend_forward(queries, stacked, mask_info, second, head_count):
    row_count = queries.shape[0]
    initial = (
        jnp.full((head_count, row_count), floor_value, jnp.float32),
        jnp.zeros((head_count, row_count), jnp.float32),
        jnp.zeros(queries.shape, jnp.float32),
    )
    always = jnp.array(True)
    running = initial
    key_piece = lax.all_gather(for_sending(stacked), "seq", axis=1, tiled=True)
    allowed = allowed_pairs(mask_info, jnp.int32(0), key_piece.shape[1])
    running = absorb_live(
        running,
        queries,
        split_heads(key_piece[0], head_count),
        split_heads(key_piece[1], head_count),
        allowed,
        always,
    )
    row_max, row_sum, weighted = absorb_live(
        running,
        queries,
        split_heads(key_piece[2], head_count),
        split_heads(key_piece[3], head_count),
        allowed,
        second,
    )
    attended = weighted / jnp.transpose(row_sum)[:, :, None]
    return (attended, row_max + jnp.log(row_sum))


def block_grads(queries, grad_heads, log_total, row_dot, key_rows, value_rows, allowed):
    scores = score_block(queries, key_rows, allowed)
    probabilities = jnp.exp(scores - log_total[:, :, None])
    grad_probs = jnp.einsum(
        "qhd,khd->hqk", grad_heads, value_rows, preferred_element_type=jnp.float32
    )
    grad_scores = (probabilities * (grad_probs - row_dot[:, :, None])).astype(jnp.bfloat16)
    grad_q = (
        jnp.einsum("hqk,khd->qhd", grad_scores, key_rows, preferred_element_type=jnp.float32)
        * score_scale
    )
    grad_k = (
        jnp.einsum("hqk,qhd->khd", grad_scores, queries, preferred_element_type=jnp.float32)
        * score_scale
    )
    grad_v = jnp.einsum(
        "hqk,qhd->khd",
        probabilities.astype(jnp.bfloat16),
        grad_heads,
        preferred_element_type=jnp.float32,
    )
    return (grad_q, grad_k, grad_v)


def grads_live(queries, grad_heads, log_total, row_dot, key_rows, value_rows, allowed, active):
    active = active & jnp.any(allowed)
    zero_grads = (
        jnp.zeros(queries.shape, jnp.float32),
        jnp.zeros(key_rows.shape, jnp.float32),
        jnp.zeros(key_rows.shape, jnp.float32),
    )
    return lax.cond(
        active,
        lambda: block_grads(queries, grad_heads, log_total, row_dot, key_rows, value_rows, allowed),
        lambda: zero_grads,
    )


def attend_backward(
    queries, stacked, grad_heads, log_total, row_dot, mask_info, second, head_count
):
    row_count = stacked.shape[1]
    feature_count = stacked.shape[2]
    always = jnp.array(True)

    def contribution(key_piece, first_row):
        piece_rows = key_piece.shape[1]
        allowed = allowed_pairs(mask_info, first_row, piece_rows)
        own_terms = grads_live(
            queries,
            grad_heads,
            log_total,
            row_dot,
            split_heads(key_piece[0], head_count),
            split_heads(key_piece[1], head_count),
            allowed,
            always,
        )
        other = grads_live(
            queries,
            grad_heads,
            log_total,
            row_dot,
            split_heads(key_piece[2], head_count),
            split_heads(key_piece[3], head_count),
            allowed,
            second,
        )
        key_terms = jnp.stack([own_terms[1], own_terms[2], other[1], other[2]]).reshape(
            4, piece_rows, feature_count
        )
        return (own_terms[0] + other[0], key_terms)

    cycle_size = lax.axis_size("seq")
    cycle_place = lax.axis_index("seq")

    def cycle_turn(turn_index, cycle_state):
        moving, gathered, grad_q = cycle_state
        first_row = (cycle_place + turn_index) % cycle_size * row_count
        part_q, key_terms = contribution(moving, first_row)
        moving = jax.tree.map(
            lambda part, own: part.astype(own.dtype),
            from_behind(for_sending(moving), "seq", -1),
            moving,
        )
        gathered = from_behind(gathered + key_terms, "seq", -1)
        return (moving, gathered, grad_q + part_q)

    initial = (
        stacked,
        jnp.zeros(stacked.shape, jnp.float32),
        jnp.zeros(queries.shape, jnp.float32),
    )
    finished = lax.fori_loop(0, cycle_size, cycle_turn, initial)
    return (finished[2], finished[1])


def layer_forward(hidden_in, extra_rows, params, mask_info, second, head_count):
    row_count, feature_count = hidden_in.shape
    combined = hidden_in + params[K.embed_row]
    normed = layer_norm(combined, params[K.norm_one_gain], params[K.norm_one_bias]).astype(
        jnp.bfloat16
    )
    projected = jnp.dot(normed, params[K.qkv_weight], preferred_element_type=jnp.float32)
    queries = (projected[:, :feature_count] + params[K.query_bias]).astype(jnp.bfloat16)
    key_rows = projected[:, feature_count : 2 * feature_count].astype(jnp.bfloat16)
    value_rows = (projected[:, 2 * feature_count :] + params[K.value_bias]).astype(jnp.bfloat16)
    stacked = jnp.concatenate([jnp.stack([key_rows, value_rows]), extra_rows], axis=0)
    query_heads = split_heads(queries, head_count)
    attended, log_total = attend_forward(query_heads, stacked, mask_info, second, head_count)
    attended_low = attended.reshape(row_count, feature_count).astype(jnp.bfloat16)
    middle = (
        combined
        + jnp.dot(attended_low, params[K.out_weight], preferred_element_type=jnp.float32)
        + params[K.out_bias]
    )
    normed_two = layer_norm(middle, params[K.norm_two_gain], params[K.norm_two_bias]).astype(
        jnp.bfloat16
    )
    hidden_pre = (
        jnp.dot(normed_two, params[K.up_weight], preferred_element_type=jnp.float32)
        + params[K.up_bias]
    )
    activated = gelu_exact(hidden_pre).astype(jnp.bfloat16)
    output = (
        middle
        + jnp.dot(activated, params[K.down_weight], preferred_element_type=jnp.float32)
        + params[K.down_bias]
    )
    saved_values = keyed(
        combined=combined,
        normed=normed,
        query_heads=query_heads,
        stacked=stacked,
        attended=attended,
        log_total=log_total,
        attended_low=attended_low,
        middle=middle,
        normed_two=normed_two,
        hidden_pre=hidden_pre,
        activated=activated,
    )
    return (output, saved_values)


def layer_backward(grad_top, saved_values, extra_grads, params, mask_info, second, head_count):
    row_count, feature_count = grad_top.shape
    gradients = {}
    grad_branch = grad_top.astype(jnp.bfloat16)
    gradients[K.down_weight] = jnp.einsum(
        "tf,td->fd", saved_values[K.activated], grad_branch, preferred_element_type=jnp.float32
    )
    gradients[K.down_bias] = jnp.sum(grad_branch.astype(jnp.float32), axis=0)
    grad_activated = jnp.einsum(
        "td,fd->tf", grad_branch, params[K.down_weight], preferred_element_type=jnp.float32
    )
    grad_pre = jax.vjp(gelu_exact, saved_values[K.hidden_pre])[1](grad_activated)[0].astype(
        jnp.bfloat16
    )
    gradients[K.up_weight] = jnp.einsum(
        "td,tf->df", saved_values[K.normed_two], grad_pre, preferred_element_type=jnp.float32
    )
    gradients[K.up_bias] = jnp.sum(grad_pre.astype(jnp.float32), axis=0)
    grad_normed_two = jnp.einsum(
        "tf,df->td", grad_pre, params[K.up_weight], preferred_element_type=jnp.float32
    )
    norm_back = jax.vjp(
        layer_norm, saved_values[K.middle], params[K.norm_two_gain], params[K.norm_two_bias]
    )[1]
    grad_middle_norm, gradients[K.norm_two_gain], gradients[K.norm_two_bias] = norm_back(
        grad_normed_two
    )
    grad_middle = grad_top + grad_middle_norm
    grad_attn_branch = grad_middle.astype(jnp.bfloat16)
    gradients[K.out_weight] = jnp.einsum(
        "tc,td->cd",
        saved_values[K.attended_low],
        grad_attn_branch,
        preferred_element_type=jnp.float32,
    )
    gradients[K.out_bias] = jnp.sum(grad_attn_branch.astype(jnp.float32), axis=0)
    grad_attended = jnp.einsum(
        "td,cd->tc", grad_attn_branch, params[K.out_weight], preferred_element_type=jnp.float32
    ).astype(jnp.bfloat16)
    grad_heads = split_heads(grad_attended, head_count)
    row_dot = jnp.einsum("qhd,qhd->hq", grad_heads.astype(jnp.float32), saved_values[K.attended])
    grad_q, key_grads = attend_backward(
        saved_values[K.query_heads],
        saved_values[K.stacked],
        grad_heads,
        saved_values[K.log_total],
        row_dot,
        mask_info,
        second,
        head_count,
    )
    grad_queries = grad_q.reshape(row_count, feature_count).astype(jnp.bfloat16)
    grad_keys = (key_grads[0] + extra_grads[0]).astype(jnp.bfloat16)
    grad_values = (key_grads[1] + extra_grads[1]).astype(jnp.bfloat16)
    grad_projected = jnp.concatenate([grad_queries, grad_keys, grad_values], axis=1)
    gradients[K.qkv_weight] = jnp.einsum(
        "tc,tk->ck", saved_values[K.normed], grad_projected, preferred_element_type=jnp.float32
    )
    gradients[K.query_bias] = jnp.sum(grad_queries.astype(jnp.float32), axis=0)
    gradients[K.value_bias] = jnp.sum(grad_values.astype(jnp.float32), axis=0)
    grad_normed = jnp.einsum(
        "tk,ck->tc", grad_projected, params[K.qkv_weight], preferred_element_type=jnp.float32
    )
    first_back = jax.vjp(
        layer_norm, saved_values[K.combined], params[K.norm_one_gain], params[K.norm_one_bias]
    )[1]
    grad_combined_norm, gradients[K.norm_one_gain], gradients[K.norm_one_bias] = first_back(
        grad_normed
    )
    grad_combined = grad_middle + grad_combined_norm
    gradients[K.embed_row] = jnp.sum(grad_combined, axis=0)
    return (grad_combined, key_grads[2:], gradients)


def with_embed(base_params, pass_embed, pass_index):
    params = dict(base_params)
    params[K.embed_row] = lax.dynamic_index_in_dim(
        pass_embed, pass_index, 0, keepdims=False
    ).astype(jnp.float32)
    return params


def run_split(tokens_used, cot_used, seg_used, base_params, pass_embed, cycle_place, head_count):
    micro_count, row_count, feature_count = tokens_used.shape
    section_index = lax.axis_index("section")
    second = section_index == 1
    params = with_embed(base_params, pass_embed, section_index)
    received = jnp.zeros((3, row_count, feature_count), jnp.bfloat16)
    saved_inputs = jnp.zeros((micro_count, 3, row_count, feature_count), jnp.bfloat16)
    outputs = jnp.zeros((micro_count, row_count, feature_count), jnp.bfloat16)
    for tick_index in range(micro_count + 1):
        slot_index = tick_index - section_index
        is_valid = (slot_index >= 0) & (slot_index < micro_count)
        slot_index = jnp.clip(slot_index, 0, micro_count - 1)
        own_in = lax.dynamic_index_in_dim(tokens_used, slot_index, 0, keepdims=False)
        seg_all = lax.dynamic_index_in_dim(seg_used, slot_index, 0, keepdims=False)
        mask_info = mask_for(seg_all, cycle_place, row_count)
        hidden_in = jnp.where(second, received[0], own_in).astype(jnp.float32)
        extra_rows = jnp.where(second, received[1:], jnp.zeros_like(received[1:]))
        output, saved_values = layer_forward(
            hidden_in, extra_rows, params, mask_info, second, head_count
        )
        output_low = output.astype(jnp.bfloat16)
        current = lax.dynamic_index_in_dim(outputs, slot_index, 0, keepdims=False)
        outputs = lax.dynamic_update_index_in_dim(
            outputs, jnp.where(is_valid, output_low, current), slot_index, 0
        )
        current_in = lax.dynamic_index_in_dim(saved_inputs, slot_index, 0, keepdims=False)
        saved_inputs = lax.dynamic_update_index_in_dim(
            saved_inputs, jnp.where(is_valid, received, current_in), slot_index, 0
        )
        stacked = saved_values[K.stacked]
        received = shifted_2(
            for_sending(jnp.stack([output_low, stacked[0], stacked[1]])), "section", 1
        )
    incoming = jnp.zeros((3, row_count, feature_count), jnp.float32)
    flows = jnp.zeros((micro_count, row_count, feature_count), jnp.float32)
    totals = None
    for tick_index in range(micro_count + 1):
        slot_index = tick_index - 1 + section_index
        is_valid = (slot_index >= 0) & (slot_index < micro_count)
        slot_index = jnp.clip(slot_index, 0, micro_count - 1)
        stored = lax.dynamic_index_in_dim(saved_inputs, slot_index, 0, keepdims=False)
        own_in = lax.dynamic_index_in_dim(tokens_used, slot_index, 0, keepdims=False)
        seg_all = lax.dynamic_index_in_dim(seg_used, slot_index, 0, keepdims=False)
        mask_info = mask_for(seg_all, cycle_place, row_count)
        hidden_in = jnp.where(second, stored[0], own_in).astype(jnp.float32)
        extra_rows = jnp.where(second, stored[1:], jnp.zeros_like(stored[1:]))
        output, saved_values = layer_forward(
            hidden_in, extra_rows, params, mask_info, second, head_count
        )
        outer_grad = lax.dynamic_index_in_dim(cot_used, slot_index, 0, keepdims=False).astype(
            jnp.float32
        )
        grad_top = jnp.where(second, outer_grad, incoming[0])
        grad_in, extra_grads, gradients = layer_backward(
            grad_top, saved_values, incoming[1:], params, mask_info, second, head_count
        )
        grad_low = grad_in.astype(jnp.bfloat16).astype(jnp.float32)
        flow_value = jnp.where(second, grad_low, grad_in)
        current = lax.dynamic_index_in_dim(flows, slot_index, 0, keepdims=False)
        flows = lax.dynamic_update_index_in_dim(
            flows, jnp.where(is_valid, flow_value, current), slot_index, 0
        )
        gradients = jax.tree.map(lambda addend: jnp.where(is_valid, addend, 0.0), gradients)
        if totals is None:
            totals = gradients
        else:
            totals = jax.tree.map(lambda running, addend: running + addend, totals, gradients)
        incoming = shifted_2(jnp.concatenate([grad_low[None], extra_grads], axis=0), "section", -1)
    embed_rows = jnp.where(
        jnp.arange(2, dtype=jnp.int32)[:, None] == section_index, totals[K.embed_row][None, :], 0.0
    )
    return (outputs, flows, totals, embed_rows)


def split_body(
    tokens,
    segment_ids,
    cotangent,
    norm_one_gain,
    norm_one_bias,
    qkv_weight,
    query_bias,
    value_bias,
    out_weight,
    out_bias,
    norm_two_gain,
    norm_two_bias,
    up_weight,
    up_bias,
    down_weight,
    down_bias,
    pass_embed,
):
    head_count = H
    section_index = lax.axis_index("section")
    cycle_place = lax.axis_index("seq")
    base_params = keyed(
        norm_one_gain=norm_one_gain.astype(jnp.float32),
        norm_one_bias=norm_one_bias.astype(jnp.float32),
        qkv_weight=qkv_weight,
        query_bias=query_bias.astype(jnp.float32),
        value_bias=value_bias.astype(jnp.float32),
        out_weight=out_weight,
        out_bias=out_bias.astype(jnp.float32),
        norm_two_gain=norm_two_gain.astype(jnp.float32),
        norm_two_bias=norm_two_bias.astype(jnp.float32),
        up_weight=up_weight,
        up_bias=up_bias.astype(jnp.float32),
        down_weight=down_weight,
        down_bias=down_bias.astype(jnp.float32),
    )
    tokens_used, cot_used, seg_used = (tokens, cotangent, segment_ids)
    outputs, flows, totals, embed_rows = run_split(
        tokens_used, cot_used, seg_used, base_params, pass_embed, cycle_place, head_count
    )
    summed = lax.psum(
        (
            totals[K.norm_one_gain],
            totals[K.norm_one_bias],
            totals[K.qkv_weight],
            totals[K.query_bias],
            totals[K.value_bias],
            totals[K.out_weight],
            totals[K.out_bias],
            totals[K.norm_two_gain],
            totals[K.norm_two_bias],
            totals[K.up_weight],
            totals[K.up_bias],
            totals[K.down_weight],
            totals[K.down_bias],
            embed_rows,
        ),
        ("section", "dp", "seq"),
    )
    embed_share = lax.dynamic_slice_in_dim(summed[13], section_index, 1, 0)
    return (
        outputs[None],
        flows[None],
        summed[0],
        summed[1],
        summed[2],
        summed[3],
        summed[4],
        summed[5],
        summed[6],
        summed[7],
        summed[8],
        summed[9],
        summed[10],
        summed[11],
        summed[12],
        embed_share,
    )


QB = 128
AB = 256
ANY = pl.BlockSpec(memory_space=pl.ANY)
VM = pl.BlockSpec(memory_space=pltpu.VMEM)
SM = pl.BlockSpec(memory_space=pltpu.SMEM)
N_SEQ, N_Z = 4, 4
BRIEF = pl.CostEstimate(flops=1, bytes_accessed=1, transcendentals=0)
LONG = pl.CostEstimate(flops=40_000_000_000, bytes_accessed=1, transcendentals=0)
ORDER = ((4096, 4096), F32)
R_G1, R_B1, R_VB, R_QB, R_OB, R_G2, R_B2, R_DB, R_PE, R_UB, N_SMALL = 0, 1, 2, 3, 4, 5, 6, 7, 8, 10, 16


def kdot(a, b, ca, cb):
    return lax.dot_general(a, b, (((ca,), (cb,)), ((), ())), preferred_element_type=F32)


def cols(j, n):
    return pl.ds(pl.multiple_of(j * n, n), n)


def norm_rows(x):
    center = jnp.mean(x, axis=-1, keepdims=True)
    shifted = x - center
    spread = jnp.mean(shifted * shifted, axis=-1, keepdims=True)
    rstd = lax.rsqrt(spread + EPS)
    return shifted * rstd, rstd


def row(ref):
    return ref[...].astype(F32).reshape(1, ref.shape[0])


def my_place():
    return tuple(lax.axis_index(a) for a in ("section", "dp", "seq"))


def piece_sources(s, q):
    first = jnp.where(s == 0, 1, 2)
    return [q, q ^ first, q ^ (3 - first), q ^ 3]


def low_half(rows):
    return lax.broadcasted_iota(jnp.int32, (rows, 128), 1) < HD


def stack_heads(x, low):
    zero = jnp.zeros_like(x)
    return jnp.concatenate([jnp.where(low, x, zero), jnp.where(low, zero, x)], axis=0)


class Copies:
    def __init__(self, sems):
        self.sems, self.count = sems, 0

    def start(self, src, dst):
        copy = pltpu.make_async_copy(src, dst, self.sems.at[self.count])
        self.count += 1
        copy.start()
        return copy


def wait_all(copies):
    for copy in copies:
        copy.wait()


def pass_forward(c, ns, rows, ready, save):
    d, ff = c[K.h].shape[1], c[K.act].shape[1]
    h, s = c[K.h], lax.axis_index("section")
    g1, b1, ob, g2, b2, db, qb, vb = (row(c[n]) for n in (K.g1, K.b1, K.ob, K.g2, K.b2, K.db, K.qb, K.vb))
    em = c[K.pe][ns - 1 : ns, :].astype(F32)
    c[K.ubr][...] = row(c[K.ub])
    seg = c[K.seg][pl.ds(s, 1), :]
    c[K.segc][...] = jnp.broadcast_to(seg, (128, rows)).T
    ready(K.h)

    def ln1(b, carry):
        r = cols(b, QB)
        xh, rstd = norm_rows(h[r, :].astype(F32) + em)
        c[K.xh1][r, :] = xh
        c[K.rs1][r, :] = jnp.broadcast_to(rstd, (QB, 128))
        c[K.normed][r, :] = (xh * g1 + b1).astype(BF)
        same = c[K.segc][r, 0:1] == seg
        query = lax.broadcasted_iota(jnp.int32, (QB, rows), 0) + b * QB
        key = lax.broadcasted_iota(jnp.int32, (QB, rows), 1)
        c[K.bias][r, :] = jnp.where(same & (key <= query), 0.0, FLOOR)
        return carry

    lax.fori_loop(0, rows // QB, ln1, 0)
    save(K.normed, K.xh1, K.rs1)
    ready(K.wqkv)
    normed = c[K.normed]
    c[K.part](K.wqkv, 0)
    q = kdot(normed[...], c[K.wqkv][:, 0:d], 1, 0) + qb
    c[K.q][...] = q.astype(BF) * jnp.asarray(SCALE, BF)
    c[K.part](K.wqkv, 1)
    c[K.k][...] = kdot(normed[...], c[K.wqkv][:, d : 2 * d], 1, 0).astype(BF)
    c[K.part](K.wqkv, 2)
    v = kdot(normed[...], c[K.wqkv][:, 2 * d : 3 * d], 1, 0) + vb
    c[K.v][...] = v.astype(BF)
    save(K.q, K.k, K.v)
    low = low_half(AB)
    sets = [(c[K.k], c[K.v])]
    if ns == 2:
        ready(K.kx, K.vx)
        sets.append((c[K.kx], c[K.vx]))

    def pair(hp, carry):
        at = cols(hp, 128)
        for i in range(rows // AB):
            r, nk = slice(i * AB, (i + 1) * AB), (i + 1) * AB
            qs = stack_heads(c[K.q][r, at], low)
            mask = c[K.bias][r, 0:nk]
            mask = jnp.concatenate([mask, mask], axis=0)
            scores = [kdot(qs, k[0:nk, at], 1, 1) + mask for k, _ in sets]
            top = jnp.max(scores[0], axis=-1, keepdims=True)
            for x in scores[1:]:
                top = jnp.maximum(top, jnp.max(x, axis=-1, keepdims=True))
            acc = None
            for n, ((_, v), x) in enumerate(zip(sets, scores)):
                w = jnp.exp(x - top).astype(BF)
                c[K.p][i][hp, :, n * nk : (n + 1) * nk] = w
                ones = jnp.ones((nk, 128), BF)
                y = kdot(w, jnp.concatenate([v[0:nk, at], ones], axis=1), 1, 0)
                acc = y if acc is None else acc + y
            inv = 1.0 / acc[:, 128:]
            o = acc[:, :128] * inv
            c[K.att][r, at] = jnp.where(low, o[:AB], o[AB:]).astype(BF)
            c[K.il][r, at] = jnp.where(low, inv[:AB], inv[AB:])
        return carry

    lax.fori_loop(0, d // 128, pair, 0, unroll=3)
    save(K.p, K.att, K.il)
    ready(K.wout)
    c[K.mid][...] = kdot(c[K.att][...], c[K.wout][...], 1, 0) + (h[...].astype(F32) + (em + ob))

    def ln2(b, carry):
        r = cols(b, QB)
        xh, rstd = norm_rows(c[K.mid][r, :])
        c[K.xh2][r, :] = xh
        c[K.rs2][r, :] = jnp.broadcast_to(rstd, (QB, 128))
        c[K.n2][r, :] = (xh * g2 + b2).astype(BF)
        return carry

    lax.fori_loop(0, rows // QB, ln2, 0)
    save(K.n2, K.xh2, K.rs2)
    ready(K.wup)

    def up(j, carry):
        at = cols(j, d)
        x = kdot(c[K.n2][...], c[K.wup][:, at], 1, 0) + c[K.ubr][:, at]
        cdf = 0.5 + 0.5 * lax.erf(x * 0.7071067811865476)
        c[K.act][:, at] = (x * cdf).astype(BF)
        bell = jnp.exp(-0.5 * (x * x)) * 0.3989422804014327
        c[K.slope][:, at] = (cdf + x * bell).astype(BF)
        return carry

    lax.fori_loop(0, ff // d, up, 0)
    save(K.act, K.slope)
    ready(K.wdown)
    y = kdot(c[K.act][...], c[K.wdown][...], 1, 0)
    c[K.out][...] = (c[K.mid][...] + y + db).astype(BF)
    save(K.out)


def norm_back_rows(rows, g_ref, xh_ref, rs_ref, gain, put):
    d = g_ref.shape[1]

    def step(b, sums):
        r = cols(b, QB)
        g, xh = g_ref[r, :], xh_ref[r, :]
        dx = g * gain
        m1 = jnp.mean(dx, axis=-1, keepdims=True)
        m2 = jnp.mean(dx * xh, axis=-1, keepdims=True)
        rstd = jnp.concatenate([rs_ref[r, :]] * (d // 128), axis=1)
        extra = put(r, rstd * (dx - m1 - xh * m2))
        new = (jnp.sum(g * xh, 0, keepdims=True), jnp.sum(g, 0, keepdims=True)) + extra
        return tuple(a + b_ for a, b_ in zip(sums, new))

    zero = jnp.zeros((1, d), F32)
    return lax.fori_loop(0, rows // QB, step, (zero,) * 4)


def back_hidden(c, ready, save):
    d, ff = c[K.g].shape[1], c[K.gpre].shape[1]
    small = c[K.small]
    ready(K.g, K.slope, K.wdown)

    def step(j, carry):
        at = cols(j, d)
        c[K.part](K.wdown, j)
        c[K.part](K.slope, j)
        gp = kdot(c[K.g][...], c[K.wdown][at, :], 1, 1) * c[K.slope][:, at].astype(F32)
        c[K.gpre][:, at] = gp.astype(BF)
        small[pl.ds(R_UB + j, 1), :] = jnp.sum(gp, 0, keepdims=True)
        return carry

    lax.fori_loop(0, ff // d, step, 0)
    save(K.gpre)


def back_norm_two(c, rows, ready, save, parts=1):
    small = c[K.small]
    ready(K.gpre, K.wup)
    for j in range(parts):
        at = slice(j * c[K.gpre].shape[1] // parts, (j + 1) * c[K.gpre].shape[1] // parts)
        c[K.part](K.gpre, j)
        c[K.part](K.wup, j)
        y = kdot(c[K.gpre][:, at], c[K.wup][:, at], 1, 1)
        c[K.gn][...] = y if j == 0 else c[K.gn][...] + y

    ready(K.xh2, K.rs2, K.g)

    def put(r, x):
        g = c[K.g][r, :].astype(F32)
        gm = g + x
        c[K.mid][r, :] = gm
        gab = gm.astype(BF)
        c[K.gab][r, :] = gab
        return (jnp.sum(g, 0, keepdims=True), jnp.sum(gab.astype(F32), 0, keepdims=True))

    sums = norm_back_rows(rows, c[K.gn], c[K.xh2], c[K.rs2], row(c[K.g2]), put)
    for at, x in zip((R_G2, R_B2, R_DB, R_OB), sums):
        small[at : at + 1, :] = x
    save(K.gab)


def back_attended(c, ready, save):
    ready(K.wout)
    c[K.ga][...] = kdot(c[K.gab][...], c[K.wout][...], 1, 1).astype(BF)
    save(K.ga)


def back_heads(c, ns, rows, add, ready, save):
    d = c[K.ga].shape[1]
    low = low_half(AB)
    ready(K.ga, K.q, K.k, K.v, K.il, K.att, K.p, K.ek, K.ev)
    sets = [(c[K.k], c[K.v])] + ([(c[K.kx], c[K.vx])] if ns == 2 else [])
    nb = rows // AB

    def pair(hp, carry):
        at = cols(hp, 128)
        sums_k, sums_v = [[] for _ in sets], [[] for _ in sets]
        for i in range(nb):
            r, nk = slice(i * AB, (i + 1) * AB), (i + 1) * AB
            qs = stack_heads(c[K.q][r, at], low)
            scaled = c[K.ga][r, at].astype(F32) * c[K.il][r, at]
            gs = stack_heads(scaled.astype(BF), low)
            dots = stack_heads(scaled * c[K.att][r, at].astype(F32), low)
            dots = jnp.sum(dots, axis=-1, keepdims=True)
            qs_t, gs_t = qs.T, gs.T
            gq = None
            for n, (k, v) in enumerate(sets):
                p = c[K.p][i][hp, :, n * nk : (n + 1) * nk]
                dp = kdot(gs, v[0:nk, at], 1, 1)
                ds = (p.astype(F32) * (dp - dots)).astype(BF)
                y = kdot(ds, k[0:nk, at], 1, 0)
                gq = y if gq is None else gq + y
                for sums, left, right in ((sums_k[n], qs_t, ds), (sums_v[n], gs_t, p)):
                    part = kdot(left, right, 1, 0)
                    for j in range(i):
                        sums[j] = sums[j] + part[:, j * AB : (j + 1) * AB]
                    sums.append(part[:, i * AB :])
            gq = gq * SCALE
            c[K.gproj][r, at] = jnp.where(low, gq[:AB], gq[AB:]).astype(BF)
        at_k = pl.ds(pl.multiple_of(d + hp * 128, 128), 128)
        at_v = pl.ds(pl.multiple_of(2 * d + hp * 128, 128), 128)
        for j in range(nb):
            r = slice(j * AB, (j + 1) * AB)
            gk, gv = sums_k[0][j].T, sums_v[0][j].T
            if add:
                gk, gv = gk + c[K.ek][r, at], gv + c[K.ev][r, at]
            c[K.gproj][r, at_k] = gk.astype(BF)
            c[K.gproj][r, at_v] = gv.astype(BF)
            if ns == 2:
                c[K.ek][r, at] = sums_k[1][j].T
                c[K.ev][r, at] = sums_v[1][j].T
        return carry

    lax.fori_loop(0, d // 128, pair, 0, unroll=3)
    save(K.gproj, K.ek, K.ev)


def back_norm_one(c, rows, pe_row, ready, save):
    d = c[K.gn].shape[1]
    small = c[K.small]
    ready(K.gproj, K.wqkv)
    c[K.gn][...] = kdot(c[K.gproj][...], c[K.wqkv][...], 1, 1)

    def put(r, x):
        gc = c[K.mid][r, :] + x
        if K.gc in c:
            c[K.gc][r, :] = gc
        else:
            c[K.gh][r, :] = gc.astype(BF)
        gq = jnp.sum(c[K.gproj][r, 0:d].astype(F32), 0, keepdims=True)
        small[R_VB : R_VB + 1, :] += jnp.sum(c[K.gproj][r, 2 * d :].astype(F32), 0, keepdims=True)
        return (jnp.sum(gc, 0, keepdims=True), gq)

    ready(K.mid, K.xh1, K.rs1)
    sums = norm_back_rows(rows, c[K.gn], c[K.xh1], c[K.rs1], row(c[K.g1]), put)
    for at, x in zip((R_G1, R_B1, pe_row, R_QB), sums):
        small[at : at + 1, :] = x
    save(K.gc, K.gh)


VECTORS = (K.g1, K.b1, K.ob, K.g2, K.b2, K.db, K.qb, K.vb, K.ub, K.pe, K.seg)


def run_kernel(name, t, ins, outs, scratch, body_fn, in_order, pieces=(), sliced=None, cut=None, limit=60):
    sliced, cut = sliced or {}, cut or {}
    vmem = [n for n in ins if n in VECTORS]
    hbm = [n for n in ins if n not in vmem]
    names = vmem + hbm
    in_specs = {n: ([1] * len(ins[n]) if isinstance(ins[n], list) else 1) for n in names}

    def flat(specs):
        result = []
        for s in specs.values():
            result += s if isinstance(s, list) else [s]
        return result

    def take(refs, specs):
        result = {}
        for n, s in specs.items():
            if isinstance(s, list):
                result[n], refs = list(refs[: len(s)]), refs[len(s) :]
            else:
                result[n], refs = refs[0], refs[1:]
        return result, refs

    flat_in = flat({n: ins[n] for n in names})
    many = {n for n, s in {**outs, **scratch}.items() if isinstance(s, list)}

    makes = t is None

    def kernel(*refs):
        given, refs = take(refs, in_specs)
        target, refs = take(refs if makes else refs[1:], outs)
        c, refs = take(refs[1:], scratch)
        in_sems, out_sems = refs
        for n in vmem:
            c[n] = given[n]
        place = my_place()
        incoming, outgoing = Copies(in_sems), Copies(out_sems)
        waiting, sent, first_part, parts_sent = {}, {}, {}, {}

        def part_of(n, index):
            dim, count = cut[n]
            size = c[n].shape[dim] // count
            at = (slice(None),) * dim + (cols(index, size),)
            return pltpu.make_async_copy(given[n].at[at], c[n].at[at], in_sems.at[first_part[n] + index])

        for n in in_order:
            if n in cut:
                if n not in first_part:
                    first_part[n] = incoming.count
                    incoming.count += cut[n][1]
                    parts_sent[n] = 0
                part_of(n, parts_sent[n]).start()
                parts_sent[n] += 1
            elif n in pieces:
                block = given[n][0].shape[0]
                places = piece_sources(place[0], place[2])
                waiting[n] = [incoming.start(x, c[n].at[cols(at, block)]) for x, at in zip(given[n], places)]
            elif n in sliced:
                first, width = sliced[n]
                at = pl.ds(pl.multiple_of(first(*place), 128), width)
                waiting[n] = [incoming.start(given[n].at[:, at], c[n])]
            elif n in many:
                waiting[n] = [incoming.start(a, b) for a, b in zip(given[n], c[n])]
            else:
                waiting[n] = [incoming.start(given[n], c[n])]

        def ready(*names):
            for n in names:
                wait_all(waiting.pop(n, []))

        def fetch(n):
            first, width = sliced[n]
            at = pl.ds(pl.multiple_of(first(*place), 128), width)
            waiting[n] = [incoming.start(given[n].at[:, at], c[n])]

        def save(*names):
            for n in names:
                if n in target:
                    pairs = zip(*((x[n] if n in many else [x[n]]) for x in (c, target)))
                    sent[n] = [outgoing.start(a, b) for a, b in pairs]

        def part(n, index):
            if n in cut:
                part_of(n, index).wait()

        c[K.fetch], c[K.part] = fetch, part
        body_fn(c, ready, save)
        for n in list(waiting):
            ready(n)
        for n in sent:
            wait_all(sent[n])

    result = pl.pallas_call(
        kernel,
        out_shape=[jax.ShapeDtypeStruct(*s) for s in flat(outs)] + [jax.ShapeDtypeStruct(*ORDER)],
        in_specs=[VM] * len(vmem) + [ANY] * (len(flat_in) - len(vmem)) + [ANY] * (not makes),
        out_specs=[ANY] * (len(flat(outs)) + 1),
        scratch_shapes=[pltpu.VMEM(*s) for s in flat(scratch)]
        + [pltpu.SemaphoreType.DMA((len(flat_in) - len(vmem) + sum(k for _, k in cut.values()) + 1,)), pltpu.SemaphoreType.DMA((len(flat(outs)) + 1,))],
        input_output_aliases={} if makes else {len(flat_in): len(flat(outs))},
        compiler_params=pltpu.CompilerParams(vmem_limit_bytes=limit * 1024 * 1024),
        cost_estimate=BRIEF,
        name=name,
    )(*flat_in, *([] if makes else [t]))
    result, (t,) = take(list(result), outs)
    return result, t


def shapes_for(rows, d, ff, ns):
    low, full = lambda n: ((rows, n), BF), lambda n: ((rows, n), F32)
    p = [((d // 128, 2 * AB, ns * AB * (i + 1)), BF) for i in range(rows // AB)]
    return keyed(
        h=low(d), normed=low(d), xh1=full(d), rs1=full(128), q=low(d), k=low(d), v=low(d), kx=low(d), vx=low(d),
        p=p, att=low(d), il=full(d), mid=full(d), n2=low(d), xh2=full(d), rs2=full(128), act=low(ff),
        slope=low(ff), out=low(d), bias=full(rows), wqkv=((d, 3 * d), BF), wout=((d, d), BF),
        wup=((d, ff), BF), wdown=((ff, d), BF), g=low(d), gpre=low(ff), gn=full(d), gab=low(d), ga=low(d),
        ubr=((1, ff), F32), segc=((rows, 128), jnp.int32), gproj=low(3 * d), ek=full(d), ev=full(d), gh=low(d), gc=full(d), small=((N_SMALL, d), F32),
    )


def sub(shapes, *names):
    return {n: shapes[n] for n in names}


def weight_term(xa, ga, xb, gb):
    return (kdot(xa, ga, 0, 0) + kdot(xb, gb, 0, 0)).astype(BF)


def store_slabs(ref, y):
    for j in range(ref.shape[0]):
        ref[j] = y[j * ref.shape[1] : (j + 1) * ref.shape[1]]


def kernel_first(t, ins, rows, d, ff):
    sh = shapes_for(rows, d, ff, 1)
    outs = sub(sh, K.normed, K.xh1, K.rs1, K.q, K.k, K.v, K.p, K.att, K.il, K.n2, K.xh2, K.rs2, K.act, K.slope, K.out)
    scratch = {**sub(sh, K.wqkv, K.wout, K.wup, K.wdown, K.h, K.mid, K.bias, K.ubr, K.segc), **outs}

    def run(c, ready, save):
        pass_forward(c, 1, rows, ready, save)

    order = [K.h, K.wqkv, K.wqkv, K.wqkv, K.wout, K.wup, K.wdown]
    return run_kernel("pass_one", t, ins, outs, scratch, run, order, pieces=(K.h,), cut=keyed(wqkv=(1, 3)))


def kernel_second(t, ins, rows, d, ff):
    sh = shapes_for(rows, d, ff, 2)
    n = ff // N_SEQ // 2
    half = ((N_Z, n // N_Z, d), BF)
    outs = sub(sh, K.normed, K.att, K.n2, K.out, K.gpre, K.gab, K.gproj, K.ek, K.ev, K.gh, K.small)
    outs.update(keyed(keep=half, send=half))
    scratch = {
        **sub(sh, K.wqkv, K.wout, K.wup, K.wdown, K.h, K.mid, K.bias, K.kx, K.vx, K.xh1, K.rs1, K.q, K.k, K.v, K.p, K.il, K.xh2, K.rs2, K.slope, K.gn, K.act, K.g, K.ubr, K.segc),
        **outs,
    }
    scratch.update(keyed(actb=((rows, 2 * n), BF)))
    del scratch[K.gpre]

    def run(c, ready, save):
        s, _, q = my_place()
        c[K.small][...] = jnp.zeros_like(c[K.small])
        pass_forward(c, 2, rows, ready, save)
        c[K.actb][...] = c[K.act][:, cols(q, 2 * n)]
        c[K.gpre], c[K.ga], c[K.acta] = c[K.act], c[K.h], c[K.slope].at[:, 0 : 2 * n]
        back_hidden(c, ready, save)
        c[K.fetch](K.acta)
        back_norm_two(c, rows, ready, save)
        back_attended(c, ready, save)
        back_heads(c, 2, rows, False, ready, save)
        back_norm_one(c, rows, R_PE + 1, ready, save)
        save(K.small)
        ready(K.acta)
        for name, side in ((K.send, 1 - s), (K.keep, s)):
            at = cols(side, n)
            store_slabs(c[name], weight_term(c[K.acta][:, at], c[K.gh][...], c[K.actb][:, at], c[K.g][...]))
            save(name)

    order = [K.h, K.wqkv, K.wqkv, K.wqkv, K.kx, K.vx, K.wout, K.wup, K.wdown, K.g]
    return run_kernel("pass_two_and_back", t, ins, outs, scratch, run, order, pieces=(K.g,),
                      sliced=keyed(acta=(lambda s, z, q: q * 2 * n, 2 * n)), cut=keyed(wqkv=(1, 3)), limit=63)


def kernel_back_up(t, ins, rows, d, ff):
    sh = shapes_for(rows, d, ff, 1)
    n, m = d // 2, ff // N_SEQ
    half = ((N_Z, n // N_Z, m), BF)
    outs = sub(sh, K.gpre, K.small)
    outs.update(keyed(keep=half, send=half))
    scratch = {**sub(sh, K.g, K.slope, K.wdown), **outs, K.na: ((rows, d), BF), K.nb: ((rows, d), BF), K.gb: ((rows, m), BF)}

    def run(c, ready, save):
        s, _, q = my_place()
        c[K.small][...] = jnp.zeros_like(c[K.small])
        back_hidden(c, ready, save)
        save(K.small)
        ready(K.na, K.nb, K.gb)
        ga = c[K.gpre][:, cols(q, m)]
        for name, side in ((K.send, 1 - s), (K.keep, s)):
            at = cols(side, n)
            store_slabs(c[name], weight_term(c[K.na][:, at], ga, c[K.nb][:, at], c[K.gb][...]))
            save(name)

    parts = ff // d
    order = [K.g] + [K.wdown, K.slope] * parts + [K.na, K.nb, K.gb]
    return run_kernel("back_up", t, ins, outs, scratch, run, order, sliced=keyed(gb=(lambda s, z, q: q * m, m)),
                      cut=keyed(wdown=(0, parts), slope=(1, parts)))


def kernel_back_out(t, ins, rows, d, ff):
    sh = shapes_for(rows, d, ff, 1)
    outs = sub(sh, K.mid, K.gab, K.ga, K.small)
    scratch = {**sub(sh, K.g, K.gpre, K.wup, K.xh2, K.rs2, K.wout, K.gn), **outs}

    def run(c, ready, save):
        c[K.small][...] = jnp.zeros_like(c[K.small])
        back_norm_two(c, rows, ready, save, parts)
        save(K.mid, K.small)
        back_attended(c, ready, save)

    parts = 3
    order = [K.gpre, K.wup] * parts + [K.xh2, K.rs2, K.g, K.wout]
    return run_kernel("back_out", t, ins, outs, scratch, run, order, cut=keyed(gpre=(1, parts), wup=(1, parts)))


def kernel_back_att(t, ins, rows, d, ff):
    sh = shapes_for(rows, d, ff, 1)
    n = d // N_SEQ
    r = n // 2 // N_Z
    width = -(-n // 128) * 128
    outs = sub(sh, K.gproj)
    outs.update(keyed(keep=((N_Z, r, 4 * d), BF), send=((N_Z, r, 4 * d), BF)))
    scratch = {**sub(sh, K.ga, K.q, K.k, K.v, K.il, K.att, K.p, K.ek, K.ev, K.gab), **outs}
    scratch.update(keyed(xo=((rows, width), BF), xob=((rows, width), BF), xq=((rows, width), BF), xqb=((rows, width), BF),
                   gabb=((rows, d), BF), gprojb=((rows, 3 * d), BF), terms=((2 * N_Z, r, 4 * d), BF)))
    del scratch[K.keep], scratch[K.send]

    def run(c, ready, save):
        s, _, q = my_place()
        odd = (q & 1) == 1

        def part(name):
            ready(name)
            x = c[name][...]
            return jnp.where(odd, x[:, width - n :], x[:, :n])

        c[K.send] = c[K.terms].at[pl.ds((1 - s) * N_Z, N_Z)]
        c[K.keep] = c[K.terms].at[pl.ds(s * N_Z, N_Z)]
        back_heads(c, 1, rows, True, ready, save)
        xo, xq = (part(K.xo), part(K.xob)), (part(K.xq), part(K.xqb))
        ready(K.gab, K.gabb, K.gprojb)
        y = weight_term(xo[0], c[K.gab][...], xo[1], c[K.gabb][...])
        for j in range(2 * N_Z):
            c[K.terms][j, :, 0:d] = y[j * r : (j + 1) * r]
        for k in range(3):
            at = slice(k * d, (k + 1) * d)
            y = weight_term(xq[0], c[K.gproj][:, at], xq[1], c[K.gprojb][:, at])
            for j in range(2 * N_Z):
                c[K.terms][j, :, (k + 1) * d : (k + 2) * d] = y[j * r : (j + 1) * r]
        save(K.send, K.keep)

    window = (lambda s, z, q: ((q * n) >> 7) << 7, width)
    order = [K.ga, K.q, K.k, K.v, K.il, K.att, K.p, K.ek, K.ev, K.xo, K.xob, K.gab, K.gabb, K.xq, K.xqb, K.gprojb]
    return run_kernel("back_attention", t, ins, outs, scratch, run, order,
                      sliced={x: window for x in (K.xo, K.xob, K.xq, K.xqb)})


def kernel_back_in(t, ins, rows, d, ff):
    sh = shapes_for(rows, d, ff, 1)
    outs = sub(sh, K.gc, K.small)
    scratch = {**sub(sh, K.mid, K.gproj, K.wqkv, K.xh1, K.rs1, K.gn), **outs}

    def run(c, ready, save):
        c[K.small][...] = jnp.zeros_like(c[K.small])
        back_norm_one(c, rows, R_PE, ready, save)
        save(K.small)

    order = [K.gproj, K.wqkv, K.mid, K.xh1, K.rs1]
    return run_kernel("back_in", t, ins, outs, scratch, run, order)


def small_call(name, kernel, t, ins, outs, scratch=(), aliases=None, out_specs=None, in_specs=None, cost=BRIEF, grid=()):
    def run(*refs):
        kernel(*refs[: len(ins)], *refs[len(ins) + 1 : len(ins) + 1 + len(outs)], *refs[len(ins) + len(outs) + 2 :])

    call = pl.pallas_call(
        run,
        out_shape=[jax.ShapeDtypeStruct(*s) for s in outs] + [jax.ShapeDtypeStruct(t.shape, t.dtype)],
        in_specs=(in_specs or [VM] * len(ins)) + [ANY],
        out_specs=(out_specs or [VM] * len(outs)) + [ANY],
        scratch_shapes=list(scratch),
        grid=grid,
        input_output_aliases={**(aliases or {}), len(ins): len(outs)},
        compiler_params=pltpu.CompilerParams(vmem_limit_bytes=40 * 1024 * 1024),
        cost_estimate=cost,
        name=name,
    )
    *result, t = call(*ins, t)
    return result, t


def core_sum(t, keep, got):
    shard = keep.shape[1:]

    def kernel(keep, got, own, *sends):
        z = lax.axis_index("dp")
        own[...] = keep[z].astype(F32) + got[z].astype(F32)
        for k, out in enumerate(sends):
            to = (z + k + 1) & (N_Z - 1)
            out[...] = (keep[to].astype(F32) + got[to].astype(F32)).astype(BF)

    return small_call("core_sum", kernel, t, [keep, got], [(shard, F32)] + [(shard, BF)] * (N_Z - 1))


def z_sum(t, own, parts, cost):
    def kernel(own, *refs):
        *parts, out = refs
        total = own[...]
        for part in parts:
            total = total + part[...].astype(F32)
        out[...] = total.astype(BF)

    return small_call("z_sum", kernel, t, [own] + parts, [(own.shape, BF)], cost=cost)


def core_half(t, keep, got):
    shard = keep.shape[1:]

    def kernel(keep, got, own, send):
        z = lax.axis_index("dp")
        for i in range(2):
            own[i] = keep[z ^ (2 * i)].astype(F32) + got[z ^ (2 * i)].astype(F32)
            other = z ^ (2 * i + 1)
            send[i] = (keep[other].astype(F32) + got[other].astype(F32)).astype(BF)

    return small_call("core_half", kernel, t, [keep, got], [((2,) + shard, F32), ((2,) + shard, BF)])


def pair_sum(t, own, got):
    shard = own.shape[1:]

    def kernel(own, got, keep, send):
        keep[...] = own[0] + got[0].astype(F32)
        send[...] = (own[1] + got[1].astype(F32)).astype(BF)

    return small_call("pair_sum", kernel, t, [own, got], [(shard, F32), (shard, BF)])


def z_place(t, parts):
    def kernel(*refs):
        *parts, out = refs
        z = lax.axis_index("dp")
        for i, part in enumerate(parts):
            out[z ^ i] = part[...]

    return small_call("z_place", kernel, t, parts, [((N_Z,) + parts[0].shape, BF)])


def collect(t, pieces):
    def kernel(*refs):
        *pieces, out = refs
        s, _, q = my_place()
        for piece, src in zip(pieces, piece_sources(s, q)):
            out[src] = piece[...]

    (out,), t = small_call("collect", kernel, t, pieces, [((N_SEQ,) + pieces[0].shape, BF)])
    return out, t


def write_all(t, mine, other, side_by_side):
    nq, nz, r, width = mine.shape
    rows = nz * r

    def kernel(mine, other, out):
        s = lax.axis_index("section")
        for x, side in ((mine, s), (other, 1 - s)):
            for j in range(nz):
                at = slice(j * r, (j + 1) * r)
                if side_by_side:
                    out[side, at] = x[0, j].astype(F32)
                else:
                    out[0, side, at] = x[0, j].astype(F32)

    if side_by_side:
        shape, spec = (2, rows, nq * width), pl.BlockSpec((2, rows, width), lambda q: (0, 0, q))
    else:
        shape, spec = (nq, 2, rows, width), pl.BlockSpec((1, 2, rows, width), lambda q: (q, 0, 0, 0))
    (out,), t = small_call(
        "write_all", kernel, t, [mine, other], [(shape, F32)], grid=(nq,), out_specs=[spec],
        in_specs=[pl.BlockSpec((1, nz, r, width), lambda q: (q, 0, 0, 0))] * 2,
    )
    return out.reshape(-1, shape[-1]), t


def write_out(t, which, mine, other, layout, arrays, old):
    shards, r, width = mine[0].shape
    rows, count = shards * r, len(which)

    def kernel(*refs):
        mine, other, refs = refs[:count], refs[count : 2 * count], refs[2 * count + len(old) :]
        outs, (stage, sems) = refs[: len(arrays)], refs[len(arrays) :]
        s, _, q = my_place()
        copies = []
        for i in range(2 * count):
            x, side = (mine[i], s) if i < count else (other[i - count], 1 - s)
            for j in range(shards):
                stage[i, j * r : (j + 1) * r, :] = x[j].astype(F32)
            src = piece_sources(side, q)[which[i % count]]
            for n, (index, first_row, col, first, wide) in enumerate(layout(src, side)):
                dst = outs[index].at[pl.ds(first_row, rows), col if isinstance(col, pl.Slice) else pl.ds(col, wide)]
                copy = pltpu.make_async_copy(stage.at[i, :, first : first + wide], dst, sems.at[i, n])
                copy.start()
                copies.append(copy)
        for copy in copies:
            copy.wait()

    return small_call(
        "write_out", kernel, t, mine + other + old, [(a, F32) for a in arrays],
        scratch=[pltpu.VMEM((2 * count, rows, width), F32), pltpu.SemaphoreType.DMA((2 * count, 2))],
        aliases={2 * count + i: i for i in range(len(old))},
        in_specs=[VM] * (2 * count) + [ANY] * len(old), out_specs=[ANY] * len(arrays),
    )


def shift_z(x, by):
    size = lax.axis_size("dp")
    return lax.ppermute(x, "dp", [(i, (i + by) % size) for i in range(size)])


def flip_z(x, by):
    return lax.ppermute(x, "dp", [(i, i ^ by) for i in range(lax.axis_size("dp"))])


def relay(t, x, cost=BRIEF):
    def kernel(x, out):
        pass

    specs = dict(aliases={0: 0}, in_specs=[ANY], out_specs=[ANY])
    (x,), t = small_call("relay", kernel, t, [x], [(x.shape, x.dtype)], cost=cost, **specs)
    return x, t


def pick_rows(t, pairs, local):
    outs = [((local, a.shape[1]), kind) for a, _, kind in pairs for _ in range(2)]

    def kernel(*refs):
        n = 2 * len(pairs)
        ins, outs, stage, sems = refs[:n], refs[n : 2 * n], refs[2 * n : -1], refs[-1]
        s, _, q = my_place()
        copies = []
        for i, x in enumerate(ins):
            copies.append(pltpu.make_async_copy(x.at[cols(q, local)], stage[i], sems.at[i]))
            copies[-1].start()
        for copy in copies:
            copy.wait()
        for i in range(len(pairs)):
            first, second = (stage[2 * i + k][...].astype(F32) for k in range(2))
            outs[2 * i][...] = jnp.where(s == 0, first, second).astype(outs[2 * i].dtype)
            outs[2 * i + 1][...] = jnp.where(s == 0, second, first).astype(outs[2 * i].dtype)

    ins = [x for a, b, _ in pairs for x in (a, b)]
    scratch = [pltpu.VMEM((local, x.shape[1]), x.dtype) for x in ins] + [pltpu.SemaphoreType.DMA((len(ins),))]

    result, t = small_call("pick_rows", kernel, t, ins, outs, scratch=scratch, in_specs=[ANY] * len(ins))
    return result[::2], result[1::2], t


def add_small(t, parts):
    def kernel(*refs):
        *parts, out = refs
        total = parts[0][...]
        for part in parts[1:]:
            total = total + part[...]
        out[...] = total

    (total,), t = small_call("add_small", kernel, t, parts, [(parts[0].shape, F32)])
    return total, t


def write_rows(t, mine, got):
    def kernel(*refs):
        n = len(mine)
        s = lax.axis_index("section")
        for a, b, out in zip(refs[:n], refs[n : 2 * n], refs[2 * n :]):
            out[0, s] = a[...]
            out[0, 1 - s] = b[...]

    return small_call("write_rows", kernel, t, mine + got, [((1, 2) + x.shape, x.dtype) for x in mine])


def write_small(t, total, pe_rows, vectors, d, ff):
    def kernel(total, pe, up, *outs):
        s = lax.axis_index("section")
        pe[...] = total[pl.ds(pe_rows + s, 1), :]
        for j in range(ff // d):
            up[j * d : (j + 1) * d] = total[R_UB + j]
        for at, out in zip(vectors, outs):
            out[...] = total[at]

    return small_call("write_small", kernel, t, [total], [((1, d), F32), ((ff,), F32)] + [((d,), F32)] * len(vectors))


class Sum:
    def __init__(self, term):
        self.keep, self.got = term[K.keep], swap_core(term[K.send])
        self.out = []

    def cores(self, t):
        (self.own, *sends), t = core_sum(t, self.keep, self.got)
        self.parts = [shift_z(x, k + 1) for k, x in enumerate(sends)]
        return t

    def cores_half(self, t):
        (self.own, send), t = core_half(t, self.keep, self.got)
        self.got = flip_z(send, 1)
        return t

    def pairs(self, t):
        (self.own, send), t = pair_sum(t, self.own, self.got)
        self.parts = [flip_z(send, 2)]
        return t

    def total(self, t, cost=BRIEF):
        (total,), t = z_sum(t, self.own, self.parts, cost)
        self.parts = [total, flip_z(total, 1), flip_z(total, 2)]
        return t

    def total_on(self, t, both=False):
        self.parts[2], t = relay(t, self.parts[2])
        if both:
            self.parts[1], t = relay(t, self.parts[1])
        self.parts.append(flip_z(self.parts[2], 1))
        return t

    def spread(self, t):
        (block,), t = z_place(t, self.parts)
        self.pieces = [block, seq_exchange(block, 0), seq_exchange(block, 1)]
        return t

    def spread_on(self, t):
        self.pieces[1], t = relay(t, self.pieces[1])
        self.pieces[2], t = relay(t, self.pieces[2])
        self.pieces.append(seq_exchange(self.pieces[1], 1))
        return t

    def collect(self, t):
        self.mine, t = collect(t, self.pieces)
        self.other = swap_core(self.mine)
        return t

    def write_all(self, t, side_by_side):
        return write_all(t, self.mine, self.other, side_by_side)

    def swap(self):
        self.others += [swap_core(x) for x in self.pieces[1:3]]

    def swap_own(self):
        self.others = [swap_core(self.pieces[0])]

    def swap_on(self, t):
        self.pieces[3], t = relay(t, self.pieces[3])
        self.others.append(swap_core(self.pieces[3]))
        return t

    def write(self, t, which, layout, arrays):
        mine, other = [self.pieces[i] for i in which], [self.others[i] for i in which]
        self.out, t = write_out(t, which, mine, other, layout, arrays, self.out)
        return t


def fast_body(
    tokens, segment_ids, cotangent, norm_one_gain, norm_one_bias, qkv_weight, query_bias, value_bias,
    out_weight, out_bias, norm_two_gain, norm_two_bias, up_weight, up_bias, down_weight, down_bias,
    pass_embed,
):
    s = lax.axis_index("section").astype(jnp.uint32)
    local, d = tokens.shape[1], tokens.shape[2]
    rows, ff = segment_ids.shape[1], up_weight.shape[1]
    tok = seq_pieces(pick(tokens, s))
    cot = seq_pieces(pick(cotangent, s))
    vec = keyed(g1=norm_one_gain, b1=norm_one_bias, ob=out_bias, g2=norm_two_gain, b2=norm_two_bias, db=down_bias,
               qb=query_bias, vb=value_bias, ub=up_bias, pe=pass_embed, seg=segment_ids)
    w = keyed(wqkv=qkv_weight, wout=out_weight, wup=up_weight, wdown=down_weight)
    sizes = (rows, d, ff)

    def some(source, *names):
        return {n: source[n] for n in names}

    one, t = kernel_first(None, {**keyed(h=tok), **vec, **w}, *sizes)
    two, t = kernel_second(
        t, {**keyed(h=one[K.out], g=cot, kx=one[K.k], vx=one[K.v], acta=one[K.act]), **vec, **w}, *sizes
    )

    def side_layout(src, side):
        first = pl.multiple_of(src * (d // N_SEQ) + side * (d // N_SEQ // 2), 8)
        return [(0, first, 0, 0, d), (1, first, 0, d, 3 * d)]

    down = Sum(two)
    t = down.cores(t)
    hid, t = kernel_back_up(
        t, keyed(g=two[K.gh], slope=one[K.slope], wdown=down_weight, na=one[K.n2], nb=two[K.n2], gb=two[K.gpre]), *sizes
    )
    up = Sum(hid)
    t = down.total(t, LONG)
    t = up.cores_half(t)
    mid, t = kernel_back_out(
        t,
        {**keyed(g=two[K.gh], gpre=hid[K.gpre], wup=up_weight, wout=out_weight), **some(vec, K.g2), **some(one, K.xh2, K.rs2)},
        *sizes,
    )
    t = down.total_on(t)
    t = up.pairs(t)
    att, t = kernel_back_att(
        t,
        {**keyed(ga=mid[K.ga], gab=mid[K.gab], xo=one[K.att], xob=two[K.att], xq=one[K.normed], xqb=two[K.normed],
                gabb=two[K.gab], gprojb=two[K.gproj]),
         **some(two, K.ek, K.ev), **some(one, K.q, K.k, K.v, K.il, K.att, K.p)},
        *sizes,
    )
    side = Sum(att)
    t = up.total(t)
    t = down.spread(t)
    side.keep, t = relay(t, side.keep, LONG)
    t = side.cores_half(t)
    last, t = kernel_back_in(
        t,
        {**keyed(wqkv=qkv_weight), **some(vec, K.g1), **some(mid, K.mid), **some(att, K.gproj), **some(one, K.xh1, K.rs1)},
        *sizes,
    )
    t = up.total_on(t)
    t = side.pairs(t)
    t = down.spread_on(t)
    t = up.spread(t)
    t = side.total(t)
    t = down.collect(t)
    small, t = add_small(t, [two[K.small], hid[K.small], mid[K.small], last[K.small]])
    small = reduce_small(small)
    t = side.total_on(t)
    d_down, t = down.write_all(t, False)
    t = side.spread(t)
    t = up.spread_on(t)
    pairs = [(one[K.out], two[K.out], BF), (last[K.gc], two[K.gh], F32)]
    mine, send, t = pick_rows(t, pairs, local)
    got = [swap_core(x) for x in send]
    (layer_out, grad_flow), t = write_rows(t, mine, got)
    vectors = (R_G1, R_B1, R_QB, R_VB, R_OB, R_G2, R_B2, R_DB)
    (grad_pe, up_b, *sums), t = write_small(t, small, R_PE, vectors, d, ff)
    g1, b1, qb, vb, ob, g2, b2, db = sums
    side.swap_own()
    t = side.write(t, (0,), side_layout, [(d, d), (d, 3 * d)])
    t = side.spread_on(t)
    side.swap()
    t = up.collect(t)
    d_up, t = up.write_all(t, True)
    t = side.write(t, (1, 2), side_layout, [(d, d), (d, 3 * d)])
    t = side.swap_on(t)
    t = side.write(t, (3,), side_layout, [(d, d), (d, 3 * d)])
    d_out, d_qkv = side.out
    return layer_out, grad_flow, g1, b1, d_qkv, qb, vb, d_out, ob, g2, b2, d_up, up_b, d_down, db, grad_pe


def body(*args):
    tokens, segment_ids = args[0], args[1]
    rows, d, ff = segment_ids.shape[1], tokens.shape[2], args[12].shape[1]
    fits = rows <= 512 and rows % AB == 0 and d % 128 == 0 and ff % d == 0 and tokens.shape[0] == 2
    fits = fits and (lax.axis_size("section"), lax.axis_size("dp"), lax.axis_size("seq")) == (2, N_Z, N_SEQ)
    return (fast_body if fits else split_body)(*args)


def solution(mesh):
    split = P("dp", "seq", None)
    placed = (split, P("dp", None), split) + (P(),) * 14
    outs = (P("section", "dp", "seq", None),) * 2 + (P(),) * 13 + (P("section", None),)
    return jax.shard_map(body, mesh=mesh, in_specs=placed, out_specs=outs, check_vma=False)
```
